32 devices in a mesh: req: 8 (over z, y), mp: 4 (over x, core).
Axes of the slice: x: 2, y: 2, z: 4, core: 2. Of those that a mesh axis runs over, the one named last changes fastest.
Arguments:
- cand_feats: bfloat16 [4096, 1024], P('req', 'mp'), may hold values from -6 to 6
- cand_perm: int32 [8, 512], P('req'), may hold values from 0 to 511, each once within a row
- w_in: bfloat16 [1024, 4, 1024], P(None, None, 'mp'), may hold values from -0.1875 to 0.1875
- w_out: bfloat16 [1024, 1024], P('mp'), may hold values from -0.1875 to 0.1875
- cache_k: bfloat16 [256, 32, 1024], P('req', None, 'mp'), may hold values from -6 to 6
- cache_v: bfloat16 [256, 32, 1024], P('req', None, 'mp'), may hold values from -1.5 to 1.5
- hist_len: int32 [8], P('req'), may hold values from 1 to 4096, as said below
- hist_home: int32 [8], replicated, may hold values from 0 to 7
- hist_slot: int32 [8, 128], replicated, may hold values from 0 to 31
- hist_mask: int32 [8, 4, 128], P('req'), may hold values 0 or 1
Outputs:
- scored: bfloat16 [4096, 1024], P('req', 'mp')
The draws below stay inside these ranges and needn't reach their ends.
Inputs may be any that keep to these rules, and one draw needn't show every extreme that they name: `cand_perm`: each row is a permutation of 0 to 511. `hist_len`: some request has a history of 4096 events.
All inputs are finite; a program needn't handle non-finite values. No bound on the sum of `hist_mask` on one device may be relied on, other than what follows from the above.
Results may differ from the reference program's by a relative error of at most 0.0067.
Values may be sent and summed in bfloat16 or wider, within the bound.
A program may use at most 64 MiB of HBM per device.

```python
import jax
import jax.numpy as jnp
from jax import lax

D = 1024
HEADS = 8
DH = 128
CANDS = 512
BLK = 32
MAXBLK = 128
BLK_DEV = 32
GROUP = 128
REQS = 8
CSLOT = 64
CGRP = 4
N_REQ = 8


def draw_hist_len(key, part):
    key = jax.random.fold_in(key, 11)
    first_key, second_key = jax.random.split(key)
    lengths = jax.random.randint(first_key, (REQS,), 1, MAXBLK * BLK + 1)
    chosen = jax.random.randint(second_key, (), 0, REQS)
    return jnp.where(jnp.arange(REQS) == chosen, MAXBLK * BLK, lengths).astype(jnp.int32)


def place_ends(entries, key, low, top_value):
    extent = entries.shape
    spot = [jax.random.randint(jax.random.fold_in(key, axis), (), 0, extent[axis]) for axis in range(len(extent))]
    entries = entries.at[tuple(spot)].set(low)
    longest = extent.index(max(extent))
    spot[longest] = (spot[longest] + 1) % extent[longest]
    return entries.at[tuple(spot)].set(top_value)


def shard_levels(stream_key, shape, pieces, low, largest):
    gain, own = 1.0, jax.random.fold_in(stream_key, 6)
    for axis_at, blocks in pieces:
        heights = jnp.exp(jax.random.uniform(jax.random.fold_in(own, axis_at), (blocks,), jnp.float32, low / len(pieces), largest / len(pieces)))
        gain = gain * jnp.repeat(heights, shape[axis_at] // blocks).reshape([-1 if axis == axis_at else 1 for axis in range(len(shape))])
    return gain


def noise(stream_key, dims, scale, most, cuts=(), kind=jnp.bfloat16):
    drawn = jax.random.normal(stream_key, dims, jnp.float32) * scale
    if len(cuts) > 0:
        drawn = shard_levels(stream_key, dims, cuts, -0.22, 0.18) * drawn
    return jnp.clip(drawn, min=-most, max=most).astype(kind)


def setup_inputs(seed: int = 0) -> dict:
    keys = jax.random.split(jax.random.key(seed), 11)
    return {
        "cand_feats": noise(keys[0], (N_REQ * N_REQ * CSLOT, D), 1.0, 6.0, ((0, 8), (1, 4))),
        "cand_perm": jax.vmap(lambda own: jax.random.permutation(own, CANDS))(jax.random.split(keys[1], REQS)).reshape((REQS, CANDS)).astype(jnp.int32),
        "w_in": noise(keys[2], (D, 4, HEADS * DH), D ** -0.5, 0.1875, ((2, 4),)),
        "w_out": noise(keys[3], (HEADS * DH, D), (HEADS * DH) ** -0.5, 0.1875, ((0, 4),)),
        "cache_k": noise(keys[4], (N_REQ * BLK_DEV, BLK, HEADS * DH), 1.0, 6.0, ((0, 8), (2, 4))),
        "cache_v": noise(keys[5], (N_REQ * BLK_DEV, BLK, HEADS * DH), 0.25, 1.5, ((0, 8), (2, 4))),
        "hist_len": draw_hist_len(jax.random.fold_in(keys[10], 71), 0),
        "hist_home": place_ends(jax.random.randint(keys[7], (REQS,), 0, N_REQ), jax.random.fold_in(keys[7], 1), 0, N_REQ - 1).astype(jnp.int32),
        "hist_slot": place_ends(jax.random.randint(keys[8], (REQS, MAXBLK), 0, BLK_DEV), jax.random.fold_in(keys[8], 1), 0, BLK_DEV - 1).astype(jnp.int32),
        "hist_mask": place_ends((jax.random.randint(keys[9], (REQS, CGRP, MAXBLK), 0, 4) < 3).astype(jnp.int32), jax.random.fold_in(keys[9], 1), 0, 1),
    }


EPS = 1e-05

def reference(cand_feats, cand_perm, w_in, w_out, cache_k, cache_v, hist_len, hist_home, hist_slot, hist_mask):
    cand_slot = CANDS // N_REQ
    key_count = MAXBLK * BLK
    width_all = HEADS * DH
    score_scale = DH ** (-0.5)
    w_flat = w_in.reshape(D, 4 * width_all)

    def per_request(request):
        position = cand_perm[request]
        row_index = position // cand_slot * (N_REQ * cand_slot) + request * cand_slot + position % cand_slot
        features = cand_feats[row_index].astype(jnp.float32)
        centred = features - lax.optimization_barrier(jnp.mean(features, axis=1, keepdims=True))
        spread = lax.optimization_barrier(jnp.mean(centred * centred, axis=1, keepdims=True))
        normed = (centred * lax.rsqrt(spread + EPS)).astype(jnp.bfloat16)
        parts = jax.nn.silu(jnp.dot(normed, w_flat, preferred_element_type=jnp.float32)).astype(jnp.bfloat16)
        parts = parts.reshape(CANDS, 4, width_all)
        gate_u, value_v, query_q, key_k = (parts[:, 0], parts[:, 1], parts[:, 2], parts[:, 3])
        block_order = jnp.arange(MAXBLK, dtype=jnp.int32)
        source = (hist_home[request] + block_order) % N_REQ
        blocks = (source * BLK_DEV + hist_slot[request]).astype(jnp.int32)
        hist_keys = cache_k[blocks].reshape(key_count, width_all)
        hist_values = cache_v[blocks].reshape(key_count, width_all)
        live_keys = (jnp.arange(key_count, dtype=jnp.int32) < hist_len[request]).astype(jnp.float32)
        block_mask = jnp.repeat(hist_mask[request].astype(jnp.float32), BLK, axis=1) * live_keys[None, :]
        outputs = []
        for head_index in range(HEADS):
            lo_col = head_index * DH
            q_head = query_q[:, lo_col:lo_col + DH]
            scores = jnp.dot(q_head, hist_keys[:, lo_col:lo_col + DH].T, preferred_element_type=jnp.float32) * score_scale
            weights = jax.nn.silu(scores).reshape(CANDS // GROUP, GROUP, key_count) * block_mask[:, None, :]
            weights = weights.reshape(CANDS, key_count).astype(jnp.bfloat16)
            own_score = lax.optimization_barrier(jnp.sum(q_head.astype(jnp.float32) * key_k[:, lo_col:lo_col + DH].astype(jnp.float32), axis=1, keepdims=True)) * score_scale
            own_term = jax.nn.silu(own_score) * value_v[:, lo_col:lo_col + DH].astype(jnp.float32)
            outputs.append(jnp.dot(weights, hist_values[:, lo_col:lo_col + DH], preferred_element_type=jnp.float32) + own_term)
        attn = jnp.concatenate(outputs, axis=1)
        attn_centred = attn - lax.optimization_barrier(jnp.mean(attn, axis=1, keepdims=True))
        attn_spread = lax.optimization_barrier(jnp.mean(attn_centred * attn_centred, axis=1, keepdims=True))
        hidden = (attn_centred * lax.rsqrt(attn_spread + EPS) * gate_u.astype(jnp.float32)).astype(jnp.bfloat16)
        mixed = jnp.dot(hidden, w_out, preferred_element_type=jnp.float32)
        return (features + mixed).astype(jnp.bfloat16)
    scored = lax.map(per_request, jnp.arange(N_REQ, dtype=jnp.int32))
    return scored.reshape(N_REQ * CANDS, D)
```

```python
import functools

import jax
import jax.numpy as jnp
from jax import lax
from jax.experimental import pallas as pl
from jax.experimental.pallas import tpu as pltpu
from jax.sharding import PartitionSpec as P

HEADS = 8
DH = 128
BLK = 32
MAXBLK = 128
GROUP = 128


EPS = 1e-05


def move_blocks(
    cand_feats, cand_perm, w_in, w_out, cache_k, cache_v, hist_len, hist_home, hist_slot, hist_mask
):
    shards = lax.axis_size("req")
    own_index = lax.axis_index("req")
    columns = cand_feats.shape[1]
    cand_slot = cand_feats.shape[0] // shards
    arrived = lax.all_to_all(
        cand_feats.reshape(shards, cand_slot, columns),
        "req",
        split_axis=0,
        concat_axis=0,
        tiled=True,
    )
    arrived = arrived.reshape(shards * cand_slot, columns)
    own_rows = jnp.take(arrived, cand_perm[0], axis=0)
    full_rows = lax.all_gather(own_rows, "mp", axis=1, tiled=True)
    cand_count = full_rows.shape[0]
    features = full_rows.astype(jnp.float32)
    centred = features - jnp.mean(features, axis=1, keepdims=True)
    spread = jnp.mean(centred * centred, axis=1, keepdims=True)
    normed = (centred * lax.rsqrt(spread + EPS)).astype(jnp.bfloat16)
    local_width = w_in.shape[2]
    parts = jax.nn.silu(
        jnp.dot(
            normed, w_in.reshape(w_in.shape[0], 4 * local_width), preferred_element_type=jnp.float32
        )
    ).astype(jnp.bfloat16)
    parts = parts.reshape(cand_count, 4, local_width)
    gate_u, value_v, query_q, key_k = (parts[:, 0], parts[:, 1], parts[:, 2], parts[:, 3])
    rounds_here = MAXBLK // shards
    offsets = (own_index - hist_home) % shards
    wanted = offsets[:, None] + jnp.arange(rounds_here, dtype=jnp.int32)[None, :] * shards
    slots = jnp.take_along_axis(hist_slot, wanted, axis=1)
    send_keys = jnp.take(cache_k, slots, axis=0)
    send_values = jnp.take(cache_v, slots, axis=0)
    key_count = MAXBLK * BLK
    own_len = hist_len[0]
    got_keys, got_values = (
        lax.all_to_all(send_keys, "req", split_axis=0, concat_axis=0, tiled=True),
        lax.all_to_all(send_values, "req", split_axis=0, concat_axis=0, tiled=True),
    )
    live_keys = (jnp.arange(key_count, dtype=jnp.int32) < own_len).astype(jnp.float32)
    home_block = hist_home[own_index]
    block_order = jnp.arange(MAXBLK, dtype=jnp.int32)
    source = (home_block + block_order % shards) % shards
    round_at = block_order // shards
    hist_keys = got_keys[source, round_at].reshape(key_count, local_width)
    hist_values = got_values[source, round_at].reshape(key_count, local_width)
    block_mask = jnp.repeat(hist_mask[0].astype(jnp.float32), BLK, axis=1) * live_keys[None, :]
    score_scale = DH ** (-0.5)
    outputs = []
    for head_index in range(local_width // DH):
        lo_col = head_index * DH
        q_head = query_q[:, lo_col : lo_col + DH]
        scores = (
            lax.dot_general(
                q_head,
                hist_keys[:, lo_col : lo_col + DH],
                (((1,), (1,)), ((), ())),
                preferred_element_type=jnp.float32,
            )
            * score_scale
        )
        weights = (
            jax.nn.silu(scores).reshape(cand_count // GROUP, GROUP, key_count)
            * block_mask[:, None, :]
        )
        weights = weights.reshape(cand_count, key_count).astype(jnp.bfloat16)
        own_score = (
            jnp.sum(
                q_head.astype(jnp.float32) * key_k[:, lo_col : lo_col + DH].astype(jnp.float32),
                axis=1,
                keepdims=True,
            )
            * score_scale
        )
        own_term = jax.nn.silu(own_score) * value_v[:, lo_col : lo_col + DH].astype(jnp.float32)
        outputs.append(
            jnp.dot(
                weights, hist_values[:, lo_col : lo_col + DH], preferred_element_type=jnp.float32
            )
            + own_term
        )
    attn = jnp.concatenate(outputs, axis=1)
    width_all = HEADS * DH
    row_total = lax.psum(jnp.sum(attn, axis=1, keepdims=True), "mp")
    attn_mean = row_total / width_all
    attn_centred = attn - attn_mean
    square_total = lax.psum(jnp.sum(attn_centred * attn_centred, axis=1, keepdims=True), "mp")
    attn_spread = square_total / width_all
    hidden = (attn_centred * lax.rsqrt(attn_spread + EPS) * gate_u.astype(jnp.float32)).astype(
        jnp.bfloat16
    )
    mixed = lax.psum_scatter(
        lax.dot_general(
            w_out, hidden, (((0,), (1,)), ((), ())), preferred_element_type=jnp.float32
        ),
        "mp",
        scatter_dimension=0,
        tiled=True,
    ).T
    return (own_rows.astype(jnp.float32) + mixed).astype(jnp.bfloat16)


def remote(src, dst, send_sem, recv_sem, device):
    return pltpu.make_async_remote_copy(
        src_ref=src,
        dst_ref=dst,
        send_sem=send_sem,
        recv_sem=recv_sem,
        device_id=device,
        device_id_type=pl.DeviceIdType.MESH,
    )


def half_silu(half):
    return half + half * jnp.tanh(half)


def kernel(
    shards,
    feats,
    perm,
    w_in,
    w_out,
    cache_k,
    cache_v,
    counts,
    home,
    slot,
    out,
    rows_all,
    normed,
    own_rows,
    q_all,
    u_all,
    v_own,
    k_own,
    wo_all,
    other_k,
    other_v,
    counts_all,
    hist_k,
    hist_v,
    mask,
    part_out,
    part_in,
    total,
    attn_all,
    row_s,
    row_r,
    core_s,
    core_r,
    x_s,
    x_r,
    fwd_s,
    fwd_r,
    kv_s,
    kv_r,
    cnt_s,
    cnt_r,
    wo_s,
    wo_r,
    q_s,
    q_r,
    p_s,
    p_r,
    u_s,
    u_r,
    a_s,
    a_r,
):
    me = lax.axis_index("req")
    mp = lax.axis_index("mp")
    lines = shards // 2
    line, side = me // 2, me % 2
    mate = line * 2 + (1 - side)
    core_mp = (mp // 2) * 2 + (1 - mp % 2)
    x_mp = (1 - mp // 2) * 2 + mp % 2
    far_mp = (1 - mp // 2) * 2 + (1 - mp % 2)
    slots = feats.shape[1]
    width = feats.shape[2]
    cands = shards * slots
    groups = cands // GROUP
    rounds = MAXBLK // shards
    keys_here = rounds * BLK
    core, across, side_mate = (me, core_mp), (me, x_mp), (mate, mp)

    barrier = pltpu.get_barrier_semaphore()
    for step in range(1, shards):
        pl.semaphore_signal(
            barrier, inc=1, device_id=((me + step) % shards, mp), device_id_type=pl.DeviceIdType.MESH
        )
    for step in range(1, 4):
        pl.semaphore_signal(
            barrier, inc=1, device_id=(me, (mp + step) % 4), device_id_type=pl.DeviceIdType.MESH
        )
    pl.semaphore_wait(barrier, shards + 2)

    def row_copy(source, target):
        return remote(
            feats.at[target],
            rows_all.at[mp, pl.ds(source * slots, slots)],
            row_s.at[target],
            row_r.at[source],
            (target, mp),
        )

    def count_copy(source, target):
        return remote(
            counts, counts_all.at[source], cnt_s.at[target], cnt_r.at[source], (target * 2 + side, mp)
        )

    def out_weight_copy(source, target):
        return remote(
            w_out.at[:, pl.ds(pl.multiple_of(target * width, width), width)],
            wo_all.at[source],
            wo_s.at[target],
            wo_r.at[source],
            (me, target),
        )

    def chunk(part, source):
        return rows_all.at[part, pl.ds(source * slots, slots)]

    def core_copy(source):
        return remote(chunk(mp, source), chunk(mp, source), core_s.at[source], core_r.at[source], core)

    def x_copy(source):
        return remote(chunk(mp, source), chunk(mp, source), x_s.at[source], x_r.at[source], across)

    def fwd_copy(source):
        return remote(chunk(x_mp, source), chunk(x_mp, source), fwd_s.at[source], fwd_r.at[source], core)

    def core_got(source):
        return remote(
            chunk(core_mp, source), chunk(core_mp, source), core_s.at[source], core_r.at[source], core
        )

    def x_got(source):
        return remote(chunk(x_mp, source), chunk(x_mp, source), x_s.at[source], x_r.at[source], across)

    def fwd_got(source):
        return remote(
            chunk(far_mp, source), chunk(far_mp, source), fwd_s.at[source], fwd_r.at[source], core
        )

    keys_copy = remote(cache_k, other_k, kv_s.at[0], kv_r.at[0], side_mate)
    values_copy = remote(cache_v, other_v, kv_s.at[1], kv_r.at[1], side_mate)

    @pl.loop(1, shards)
    def _(step):
        row_copy(me, (me + step) % shards).start()

    for step in range(1, lines):
        count_copy(line, (line + step) % lines).start()
    keys_copy.start()
    values_copy.start()
    rows_all[mp, pl.ds(me * slots, slots), :] = feats[me]
    counts_all[line] = counts[...]
    core_copy(me).start()
    x_copy(me).start()

    @pl.loop(1, shards)
    def _(step):
        source = (me + step) % shards
        row_copy(source, me).wait_recv()
        core_copy(source).start()
        x_copy(source).start()

    for step in range(1, 4):
        out_weight_copy(mp, (mp + step) % 4).start()
    wo_all[mp] = w_out[:, pl.ds(pl.multiple_of(mp * width, width), width)]

    def gather(keys_ref, values_ref, shard, half):
        @pl.loop(0, lines)
        def _(at):
            request = at * 2 + side
            first = lax.rem(shard - home[request] + shards, shards)

            @pl.loop(0, rounds)
            def _(turn):
                place = slot[request, first + turn * shards]
                rows = pl.ds(half * keys_here + turn * BLK, BLK)
                hist_k[at, rows, :] = keys_ref[place]
                hist_v[at, rows, :] = values_ref[place]

    gather(cache_k, cache_v, me, 0)

    @pl.loop(0, shards)
    def _(step):
        source = (me + step) % shards
        x_got(source).wait_recv()
        fwd_copy(source).start()

    for step in range(1, lines):
        count_copy((line + step) % lines, line).wait_recv()

    @pl.loop(0, lines)
    def _(at):
        request = at * 2 + side
        number = counts_all[at].astype(jnp.bfloat16)
        for half, shard in enumerate((me, mate)):
            first = lax.rem(shard - home[request] + shards, shards)
            key_at = lax.broadcasted_iota(jnp.int32, (MAXBLK, keys_here), 1)
            block_at = lax.broadcasted_iota(jnp.int32, (MAXBLK, keys_here), 0)
            spread = (block_at == first + (key_at // BLK) * shards).astype(jnp.float32)
            live = jnp.dot(number, spread.astype(jnp.bfloat16), preferred_element_type=jnp.float32)
            place = lax.broadcasted_iota(jnp.int32, live.shape, 1) % BLK
            mask[at, :, half * keys_here : (half + 1) * keys_here] = jnp.where(
                place.astype(jnp.float32) < live, 0.5 * DH ** (-0.5), 0.0
            )

    @pl.loop(0, shards)
    def _(step):
        source = (me + step) % shards
        core_got(source).wait_recv()
        fwd_got(source).wait_recv()

    def q_copy(source, target, group):
        rows = pl.ds(group * GROUP, GROUP)
        return remote(
            q_all.at[source, rows],
            q_all.at[source, rows],
            q_s.at[target * groups + group],
            q_r.at[source * groups + group],
            (target * 2 + side, mp),
        )

    def project(part, group):
        rows = pl.ds(group * GROUP, GROUP)
        scores = jnp.dot(normed[rows, :], w_in[part], preferred_element_type=jnp.float32)
        return half_silu(0.5 * scores).astype(jnp.bfloat16)

    @pl.loop(0, groups)
    def _(group):
        rows = pl.ds(group * GROUP, GROUP)
        wanted = perm[rows, :]
        pick = (lax.broadcasted_iota(jnp.int32, (GROUP, cands), 1) == wanted).astype(jnp.float32)
        pick = pick.astype(jnp.bfloat16)
        features = jnp.concatenate(
            [jnp.dot(pick, rows_all[part], preferred_element_type=jnp.float32) for part in range(4)],
            axis=1,
        )
        own_rows[rows, :] = jnp.dot(pick, rows_all[mp], preferred_element_type=jnp.float32)
        centred = features - jnp.mean(features, axis=1, keepdims=True)
        variance = jnp.mean(centred * centred, axis=1, keepdims=True)
        normed[rows, :] = (centred * lax.rsqrt(variance + EPS)).astype(jnp.bfloat16)
        q_all[line, rows, :] = project(2, group)
        for step in range(1, lines):
            q_copy(line, (line + step) % lines, group).start()

    @pl.loop(0, groups)
    def _(group):
        u_all[mp, pl.ds(group * GROUP, GROUP), :] = project(0, group)

    def part_copy(buffer, part, sems, index, device):
        send, receive = sems
        return remote(buffer.at[part], buffer.at[part], send.at[index], receive.at[index], device)

    u_sems = (u_s, u_r)
    part_copy(u_all, mp, u_sems, 0, core).start()
    part_copy(u_all, mp, u_sems, 1, across).start()

    @pl.loop(0, groups)
    def _(group):
        rows = pl.ds(group * GROUP, GROUP)
        v_own[rows, :] = project(1, group)
        k_own[rows, :] = project(3, group)

    keys_copy.wait_recv()
    values_copy.wait_recv()
    gather(other_k, other_v, mate, 1)

    def attend(at, group):
        rows = pl.ds(group * GROUP, GROUP)
        scale = mask[at, pl.ds(group, 1), :]
        heads = []
        for lo in range(0, width, DH):
            query = q_all[at, rows, lo : lo + DH]
            summed = None
            for first in range(0, 2 * keys_here, keys_here):
                scores = lax.dot_general(
                    query,
                    hist_k[at, first : first + keys_here, lo : lo + DH],
                    (((1,), (1,)), ((), ())),
                    preferred_element_type=jnp.float32,
                )
                weights = half_silu(scores * scale[:, first : first + keys_here]).astype(jnp.bfloat16)
                term = jnp.dot(
                    weights,
                    hist_v[at, first : first + keys_here, lo : lo + DH],
                    preferred_element_type=jnp.float32,
                )
                summed = term if summed is None else summed + term
            heads.append(summed)
        return jnp.concatenate(heads, axis=1)

    def p_copy(source, target, group):
        rows = pl.ds(group * GROUP, GROUP)
        return remote(
            part_out.at[target, rows],
            part_in.at[source, rows],
            p_s.at[target * groups + group],
            p_r.at[source * groups + group],
            (target * 2 + side, mp),
        )

    @pl.loop(0, groups)
    def _(group):
        for step in range(1, lines):
            at = (line + step) % lines
            q_copy(at, line, group).wait_recv()
            part_out[at, pl.ds(group * GROUP, GROUP), :] = attend(at, group).astype(jnp.bfloat16)
            p_copy(line, at, group).start()

    part_copy(u_all, x_mp, u_sems, 1, across).wait_recv()
    part_copy(u_all, x_mp, u_sems, 2, core).start()

    @pl.loop(0, groups)
    def _(group):
        rows = pl.ds(group * GROUP, GROUP)
        own = []
        for lo in range(0, width, DH):
            query = q_all[line, rows, lo : lo + DH].astype(jnp.float32)
            key = k_own[rows, lo : lo + DH].astype(jnp.float32)
            half = jnp.sum(query * key, axis=1, keepdims=True) * (0.5 * DH ** (-0.5))
            own.append(half_silu(half) * v_own[rows, lo : lo + DH].astype(jnp.float32))
        total[rows, :] = attend(line, group) + jnp.concatenate(own, axis=1)

    part_copy(u_all, core_mp, u_sems, 0, core).wait_recv()
    part_copy(u_all, far_mp, u_sems, 2, core).wait_recv()
    for step in range(1, 4):
        out_weight_copy((mp + step) % 4, mp).wait_recv()

    def attn_copy(part, kind, group, device):
        piece = attn_all.at[part, pl.ds(group * GROUP, GROUP)]
        index = kind * groups + group
        return remote(piece, piece, a_s.at[index], a_r.at[index], device)

    def collect(group):
        rows = pl.ds(group * GROUP, GROUP)
        summed = total[rows, :]
        for step in range(1, lines):
            at = (line + step) % lines
            p_copy(at, line, group).wait_recv()
            summed = summed + part_in[at, rows, :].astype(jnp.float32)
        attn_all[mp, rows, :] = summed.astype(jnp.bfloat16)
        attn_copy(mp, 0, group, core).start()
        attn_copy(mp, 1, group, across).start()

    def pass_on(group):
        attn_copy(x_mp, 1, group, across).wait_recv()
        attn_copy(x_mp, 2, group, core).start()

    def finish(group):
        rows = pl.ds(group * GROUP, GROUP)
        attn_copy(core_mp, 0, group, core).wait_recv()
        attn_copy(far_mp, 2, group, core).wait_recv()
        attn = jnp.concatenate([attn_all[part, rows, :].astype(jnp.float32) for part in range(4)], axis=1)
        gate = jnp.concatenate([u_all[part, rows, :].astype(jnp.float32) for part in range(4)], axis=1)
        centred = attn - jnp.mean(attn, axis=1, keepdims=True)
        variance = jnp.mean(centred * centred, axis=1, keepdims=True)
        hidden = (centred * lax.rsqrt(variance + EPS) * gate).astype(jnp.bfloat16)
        mixed = own_rows[rows, :]
        for part in range(4):
            mixed = mixed + jnp.dot(
                hidden[:, part * width : (part + 1) * width],
                wo_all[part],
                preferred_element_type=jnp.float32,
            )
        out[rows, :] = mixed.astype(jnp.bfloat16)

    @pl.loop(0, groups + 2)
    def _(turn):
        @pl.when(turn < groups)
        def _():
            collect(turn)

        @pl.when((turn >= 1) & (turn < groups + 1))
        def _():
            pass_on(turn - 1)

        @pl.when(turn >= 2)
        def _():
            finish(turn - 2)

    @pl.loop(1, shards)
    def _(step):
        row_copy(me, (me + step) % shards).wait_send()

    @pl.loop(0, shards)
    def _(source):
        core_copy(source).wait_send()
        x_copy(source).wait_send()
        fwd_copy(source).wait_send()

    keys_copy.wait_send()
    values_copy.wait_send()
    for step in range(1, lines):
        count_copy(line, (line + step) % lines).wait_send()
    for step in range(1, 4):
        out_weight_copy(mp, (mp + step) % 4).wait_send()
    part_copy(u_all, mp, u_sems, 0, core).wait_send()
    part_copy(u_all, mp, u_sems, 1, across).wait_send()
    part_copy(u_all, x_mp, u_sems, 2, core).wait_send()

    @pl.loop(0, groups)
    def _(group):
        for step in range(1, lines):
            q_copy(line, (line + step) % lines, group).wait_send()
            p_copy(line, (line + step) % lines, group).wait_send()
        attn_copy(mp, 0, group, core).wait_send()
        attn_copy(mp, 1, group, across).wait_send()
        attn_copy(x_mp, 2, group, core).wait_send()


def move_queries(
    cand_feats, cand_perm, w_in, w_out, cache_k, cache_v, hist_len, hist_home, hist_slot, hist_mask
):
    shards = lax.axis_size("req")
    cands, width = cand_feats.shape
    full = w_in.shape[0]
    lines = shards // 2
    groups = cands // GROUP
    keys = 2 * (MAXBLK // shards) * BLK
    lengths = jnp.clip(hist_len[0] - BLK * jnp.arange(MAXBLK, dtype=jnp.int32), 0, BLK)
    counts = jnp.pad((hist_mask[0] * lengths[None, :]).astype(jnp.float32), ((0, 8 - groups), (0, 0)))
    bf16, f32 = jnp.bfloat16, jnp.float32
    vmem = pl.BlockSpec(memory_space=pltpu.VMEM)
    smem = pl.BlockSpec(memory_space=pltpu.SMEM)
    pairs = [shards, shards, shards, shards, 2, lines, 4, lines * groups, lines * groups, 3, 3 * groups]
    return pl.pallas_call(
        functools.partial(kernel, shards),
        out_shape=jax.ShapeDtypeStruct((cands, width), bf16),
        in_specs=[vmem] * 7 + [smem] * 2,
        out_specs=vmem,
        scratch_shapes=[
            pltpu.VMEM((4, cands, width), bf16),
            pltpu.VMEM((cands, full), bf16),
            pltpu.VMEM((cands, width), f32),
            pltpu.VMEM((lines, cands, width), bf16),
            pltpu.VMEM((4, cands, width), bf16),
            pltpu.VMEM((cands, width), bf16),
            pltpu.VMEM((cands, width), bf16),
            pltpu.VMEM((4, width, width), bf16),
            pltpu.VMEM(cache_k.shape, bf16),
            pltpu.VMEM(cache_v.shape, bf16),
            pltpu.VMEM((lines, 8, MAXBLK), f32),
            pltpu.VMEM((lines, keys, width), bf16),
            pltpu.VMEM((lines, keys, width), bf16),
            pltpu.VMEM((lines, 8, keys), f32),
            pltpu.VMEM((lines, cands, width), bf16),
            pltpu.VMEM((lines, cands, width), bf16),
            pltpu.VMEM((cands, width), f32),
            pltpu.VMEM((4, cands, width), bf16),
        ]
        + [pltpu.SemaphoreType.DMA((count,)) for count in pairs for _ in range(2)],
        compiler_params=pltpu.CompilerParams(
            collective_id=0, has_side_effects=True, vmem_limit_bytes=48 * 1024 * 1024
        ),
        cost_estimate=pl.CostEstimate(flops=8 * 10**9, bytes_accessed=2**23, transcendentals=2**22),
    )(
        cand_feats.reshape(shards, cands // shards, width),
        cand_perm.reshape(cands, 1),
        w_in.transpose(1, 0, 2),
        w_out,
        cache_k,
        cache_v,
        counts,
        hist_home,
        hist_slot,
    )


def local(cand_feats, cand_perm, w_in, *rest):
    shards = lax.axis_size("req")
    shard_keys = MAXBLK // shards * BLK
    queries_fit = cand_perm.shape[1] <= shard_keys and shards % 2 == 0
    plan = move_queries if queries_fit and lax.axis_size("mp") == 4 else move_blocks
    return plan(cand_feats, cand_perm, w_in, *rest)


def solution(mesh):
    in_specs = (
        P("req", "mp"),
        P("req", None),
        P(None, None, "mp"),
        P("mp", None),
        P("req", None, "mp"),
        P("req", None, "mp"),
        P("req"),
        P(),
        P(),
        P("req", None, None),
    )
    out_specs = P("req", "mp")
    return jax.shard_map(local, mesh=mesh, in_specs=in_specs, out_specs=out_specs, check_vma=False)
```

```python
import functools

import jax
import jax.numpy as jnp
from jax import lax
from jax.experimental import pallas as pl
from jax.experimental.pallas import tpu as pltpu
from jax.sharding import PartitionSpec as P

HEADS = 8
DH = 128
BLK = 32
MAXBLK = 128
GROUP = 128


EPS = 1e-05


def move_blocks(
    cand_feats, cand_perm, w_in, w_out, cache_k, cache_v, hist_len, hist_home, hist_slot, hist_mask
):
    shards = lax.axis_size("req")
    own_index = lax.axis_index("req")
    columns = cand_feats.shape[1]
    cand_slot = cand_feats.shape[0] // shards
    arrived = lax.all_to_all(
        cand_feats.reshape(shards, cand_slot, columns),
        "req",
        split_axis=0,
        concat_axis=0,
        tiled=True,
    )
    arrived = arrived.reshape(shards * cand_slot, columns)
    own_rows = jnp.take(arrived, cand_perm[0], axis=0)
    full_rows = lax.all_gather(own_rows, "mp", axis=1, tiled=True)
    cand_count = full_rows.shape[0]
    features = full_rows.astype(jnp.float32)
    centred = features - jnp.mean(features, axis=1, keepdims=True)
    spread = jnp.mean(centred * centred, axis=1, keepdims=True)
    normed = (centred * lax.rsqrt(spread + EPS)).astype(jnp.bfloat16)
    local_width = w_in.shape[2]
    parts = jax.nn.silu(
        jnp.dot(
            normed, w_in.reshape(w_in.shape[0], 4 * local_width), preferred_element_type=jnp.float32
        )
    ).astype(jnp.bfloat16)
    parts = parts.reshape(cand_count, 4, local_width)
    gate_u, value_v, query_q, key_k = (parts[:, 0], parts[:, 1], parts[:, 2], parts[:, 3])
    rounds_here = MAXBLK // shards
    offsets = (own_index - hist_home) % shards
    wanted = offsets[:, None] + jnp.arange(rounds_here, dtype=jnp.int32)[None, :] * shards
    slots = jnp.take_along_axis(hist_slot, wanted, axis=1)
    send_keys = jnp.take(cache_k, slots, axis=0)
    send_values = jnp.take(cache_v, slots, axis=0)
    key_count = MAXBLK * BLK
    own_len = hist_len[0]
    got_keys, got_values = (
        lax.all_to_all(send_keys, "req", split_axis=0, concat_axis=0, tiled=True),
        lax.all_to_all(send_values, "req", split_axis=0, concat_axis=0, tiled=True),
    )
    live_keys = (jnp.arange(key_count, dtype=jnp.int32) < own_len).astype(jnp.float32)
    home_block = hist_home[own_index]
    block_order = jnp.arange(MAXBLK, dtype=jnp.int32)
    source = (home_block + block_order % shards) % shards
    round_at = block_order // shards
    hist_keys = got_keys[source, round_at].reshape(key_count, local_width)
    hist_values = got_values[source, round_at].reshape(key_count, local_width)
    block_mask = jnp.repeat(hist_mask[0].astype(jnp.float32), BLK, axis=1) * live_keys[None, :]
    score_scale = DH ** (-0.5)
    outputs = []
    for head_index in range(local_width // DH):
        lo_col = head_index * DH
        q_head = query_q[:, lo_col : lo_col + DH]
        scores = (
            lax.dot_general(
                q_head,
                hist_keys[:, lo_col : lo_col + DH],
                (((1,), (1,)), ((), ())),
                preferred_element_type=jnp.float32,
            )
            * score_scale
        )
        weights = (
            jax.nn.silu(scores).reshape(cand_count // GROUP, GROUP, key_count)
            * block_mask[:, None, :]
        )
        weights = weights.reshape(cand_count, key_count).astype(jnp.bfloat16)
        own_score = (
            jnp.sum(
                q_head.astype(jnp.float32) * key_k[:, lo_col : lo_col + DH].astype(jnp.float32),
                axis=1,
                keepdims=True,
            )
            * score_scale
        )
        own_term = jax.nn.silu(own_score) * value_v[:, lo_col : lo_col + DH].astype(jnp.float32)
        outputs.append(
            jnp.dot(
                weights, hist_values[:, lo_col : lo_col + DH], preferred_element_type=jnp.float32
            )
            + own_term
        )
    attn = jnp.concatenate(outputs, axis=1)
    width_all = HEADS * DH
    row_total = lax.psum(jnp.sum(attn, axis=1, keepdims=True), "mp")
    attn_mean = row_total / width_all
    attn_centred = attn - attn_mean
    square_total = lax.psum(jnp.sum(attn_centred * attn_centred, axis=1, keepdims=True), "mp")
    attn_spread = square_total / width_all
    hidden = (attn_centred * lax.rsqrt(attn_spread + EPS) * gate_u.astype(jnp.float32)).astype(
        jnp.bfloat16
    )
    mixed = lax.psum_scatter(
        lax.dot_general(
            w_out, hidden, (((0,), (1,)), ((), ())), preferred_element_type=jnp.float32
        ),
        "mp",
        scatter_dimension=0,
        tiled=True,
    ).T
    return (own_rows.astype(jnp.float32) + mixed).astype(jnp.bfloat16)


def remote(src, dst, send_sem, recv_sem, device):
    return pltpu.make_async_remote_copy(
        src_ref=src,
        dst_ref=dst,
        send_sem=send_sem,
        recv_sem=recv_sem,
        device_id=device,
        device_id_type=pl.DeviceIdType.MESH,
    )


def half_silu(half):
    return half + half * jnp.tanh(half)


def kernel(
    shards,
    feats,
    perm,
    w_in,
    w_out,
    cache_k,
    cache_v,
    block_mask,
    length,
    home,
    slot,
    out,
    w_parts,
    counts,
    rows_all,
    normed,
    own_rows,
    q_all,
    u_all,
    v_own,
    k_own,
    wo_all,
    other_k,
    other_v,
    counts_all,
    hist_k,
    hist_v,
    mask,
    part_out,
    part_in,
    part_own,
    total,
    attn_all,
    row_s,
    row_r,
    core_s,
    core_r,
    x_s,
    x_r,
    fwd_s,
    fwd_r,
    kv_s,
    kv_r,
    cnt_s,
    cnt_r,
    wo_s,
    wo_r,
    q_s,
    q_r,
    p_s,
    p_r,
    u_s,
    u_r,
    a_s,
    a_r,
):
    me = lax.axis_index("req")
    mp = lax.axis_index("mp")
    lines = shards // 2
    line, side = me // 2, me % 2
    lines_by_distance = (line, line + 1 - 2 * (line % 2), (line + 2) % 4, 3 - line)
    others = [(side + turn) % 2 + 2 * at for at in lines_by_distance for turn in range(2)][1:]
    mate = line * 2 + (1 - side)
    core_mp = (mp // 2) * 2 + (1 - mp % 2)
    x_mp = (1 - mp // 2) * 2 + mp % 2
    far_mp = (1 - mp // 2) * 2 + (1 - mp % 2)
    slots = feats.shape[1]
    width = feats.shape[2]
    cands = shards * slots
    groups = cands // GROUP
    rounds = MAXBLK // shards
    keys_here = rounds * BLK
    core, across, side_mate = (me, core_mp), (me, x_mp), (mate, mp)

    barrier = pltpu.get_barrier_semaphore()
    for step in range(1, shards):
        pl.semaphore_signal(
            barrier, inc=1, device_id=((me + step) % shards, mp), device_id_type=pl.DeviceIdType.MESH
        )
    for step in range(1, 4):
        pl.semaphore_signal(
            barrier, inc=1, device_id=(me, (mp + step) % 4), device_id_type=pl.DeviceIdType.MESH
        )
    pl.semaphore_wait(barrier, shards + 2)

    def row_copy(source, target):
        return remote(
            feats.at[target],
            rows_all.at[mp, pl.ds(source * slots, slots)],
            row_s.at[target],
            row_r.at[source],
            (target, mp),
        )

    def count_copy(source, target):
        return remote(
            counts, counts_all.at[source], cnt_s.at[target], cnt_r.at[source], (target * 2 + side, mp)
        )

    def out_weight_copy(source, target):
        return remote(
            w_out.at[:, pl.ds(pl.multiple_of(target * width, width), width)],
            wo_all.at[source],
            wo_s.at[target],
            wo_r.at[source],
            (me, target),
        )

    def chunk(part, source):
        return rows_all.at[part, pl.ds(source * slots, slots)]

    def core_copy(source):
        return remote(chunk(mp, source), chunk(mp, source), core_s.at[source], core_r.at[source], core)

    def x_copy(source):
        return remote(chunk(mp, source), chunk(mp, source), x_s.at[source], x_r.at[source], across)

    def fwd_copy(source):
        return remote(chunk(x_mp, source), chunk(x_mp, source), fwd_s.at[source], fwd_r.at[source], core)

    def core_got(source):
        return remote(
            chunk(core_mp, source), chunk(core_mp, source), core_s.at[source], core_r.at[source], core
        )

    def x_got(source):
        return remote(chunk(x_mp, source), chunk(x_mp, source), x_s.at[source], x_r.at[source], across)

    def fwd_got(source):
        return remote(
            chunk(far_mp, source), chunk(far_mp, source), fwd_s.at[source], fwd_r.at[source], core
        )

    keys_copy = remote(cache_k, other_k, kv_s.at[0], kv_r.at[0], side_mate)
    values_copy = remote(cache_v, other_v, kv_s.at[1], kv_r.at[1], side_mate)

    for target in others[::-1]:
        row_copy(me, target).start()

    places = lax.broadcasted_iota(jnp.int32, (groups, MAXBLK), 1) * BLK
    counts[...] = jnp.zeros_like(counts)
    counts[0:groups, :] = (block_mask[0] * jnp.clip(length[0] - places, 0, BLK)).astype(jnp.float32)
    for step in range(1, lines):
        count_copy(line, (line + step) % lines).start()
    keys_copy.start()
    values_copy.start()
    rows_all[mp, pl.ds(me * slots, slots), :] = feats[me]
    counts_all[line] = counts[...]
    core_copy(me).start()
    x_copy(me).start()

    @pl.loop(0, w_in.shape[0], step=GROUP)
    def _(first):
        rows = pl.ds(pl.multiple_of(first, GROUP), GROUP)
        for part in range(4):
            w_parts[part, rows, :] = w_in[rows, part, :]

    for source in others:
        row_copy(source, me).wait_recv()
        core_copy(source).start()
        x_copy(source).start()

    for step in range(1, 4):
        out_weight_copy(mp, (mp + step) % 4).start()
    wo_all[mp] = w_out[:, pl.ds(pl.multiple_of(mp * width, width), width)]

    def gather(keys_ref, values_ref, shard, half):
        @pl.loop(0, lines)
        def _(at):
            request = at * 2 + side
            first = lax.rem(shard - home[request] + shards, shards)

            @pl.loop(0, rounds)
            def _(turn):
                place = slot[request, first + turn * shards]
                rows = pl.ds(half * keys_here + turn * BLK, BLK)
                hist_k[at, rows, :] = keys_ref[place]
                hist_v[at, rows, :] = values_ref[place]

    gather(cache_k, cache_v, me, 0)

    for source in [me] + others:
        x_got(source).wait_recv()
        fwd_copy(source).start()

    for step in range(1, lines):
        count_copy((line + step) % lines, line).wait_recv()

    @pl.loop(0, lines)
    def _(at):
        request = at * 2 + side
        number = counts_all[at].astype(jnp.bfloat16)
        for half, shard in enumerate((me, mate)):
            first = lax.rem(shard - home[request] + shards, shards)
            key_at = lax.broadcasted_iota(jnp.int32, (MAXBLK, keys_here), 1)
            block_at = lax.broadcasted_iota(jnp.int32, (MAXBLK, keys_here), 0)
            spread = (block_at == first + (key_at // BLK) * shards).astype(jnp.float32)
            live = jnp.dot(number, spread.astype(jnp.bfloat16), preferred_element_type=jnp.float32)
            place = lax.broadcasted_iota(jnp.int32, live.shape, 1) % BLK
            mask[at, :, half * keys_here : (half + 1) * keys_here] = jnp.where(
                place.astype(jnp.float32) < live, 0.5 * DH ** (-0.5), 0.0
            )

    for source in [me] + others:
        core_got(source).wait_recv()
        fwd_got(source).wait_recv()


    def q_copy(source, device_line, group, index):
        rows = pl.ds(group * GROUP, GROUP)
        return remote(
            q_all.at[source, rows],
            q_all.at[source, rows],
            q_s.at[index * groups + group],
            q_r.at[source * groups + group],
            (device_line * 2 + side, mp),
        )

    below, above = line > 0, line < lines - 1

    def project(part, group):
        rows = pl.ds(group * GROUP, GROUP)
        scores = jnp.dot(normed[rows, :], w_parts[part], preferred_element_type=jnp.float32)
        return half_silu(0.5 * scores).astype(jnp.bfloat16)

    @pl.loop(0, groups)
    def _(group):
        rows = pl.ds(group * GROUP, GROUP)
        wanted = perm[:, pl.ds(pl.multiple_of(group * GROUP, GROUP), GROUP)]
        chosen = lax.broadcasted_iota(jnp.int32, (cands, GROUP), 0) == wanted
        pick = jnp.transpose(chosen.astype(jnp.float32)).astype(jnp.bfloat16)
        features = jnp.concatenate(
            [jnp.dot(pick, rows_all[part], preferred_element_type=jnp.float32) for part in range(4)],
            axis=1,
        )
        own_rows[rows, :] = jnp.dot(pick, rows_all[mp], preferred_element_type=jnp.float32)
        centred = features - jnp.mean(features, axis=1, keepdims=True)
        variance = jnp.mean(centred * centred, axis=1, keepdims=True)
        normed[rows, :] = (centred * lax.rsqrt(variance + EPS)).astype(jnp.bfloat16)
        q_all[line, rows, :] = project(2, group)

        @pl.when(above)
        def _():
            q_copy(line, line + 1, group, line).start()

        @pl.when(below)
        def _():
            q_copy(line, line - 1, group, lines).start()

    @pl.loop(0, groups)
    def _(group):
        u_all[mp, pl.ds(group * GROUP, GROUP), :] = project(0, group)

    def part_copy(buffer, part, sems, index, device):
        send, receive = sems
        return remote(buffer.at[part], buffer.at[part], send.at[index], receive.at[index], device)

    u_sems = (u_s, u_r)
    part_copy(u_all, mp, u_sems, 0, core).start()
    part_copy(u_all, mp, u_sems, 1, across).start()

    @pl.loop(0, groups)
    def _(group):
        rows = pl.ds(group * GROUP, GROUP)
        v_own[rows, :] = project(1, group)
        k_own[rows, :] = project(3, group)

    keys_copy.wait_recv()
    values_copy.wait_recv()
    gather(other_k, other_v, mate, 1)

    def attend(at, group):
        rows = pl.ds(group * GROUP, GROUP)
        scale = mask[at, pl.ds(group, 1), :]
        heads = []
        for lo in range(0, width, DH):
            query = q_all[at, rows, lo : lo + DH]
            summed = None
            for first in range(0, 2 * keys_here, keys_here):
                scores = lax.dot_general(
                    query,
                    hist_k[at, first : first + keys_here, lo : lo + DH],
                    (((1,), (1,)), ((), ())),
                    preferred_element_type=jnp.float32,
                )
                weights = half_silu(scores * scale[:, first : first + keys_here]).astype(jnp.bfloat16)
                term = jnp.dot(
                    weights,
                    hist_v[at, first : first + keys_here, lo : lo + DH],
                    preferred_element_type=jnp.float32,
                )
                summed = term if summed is None else summed + term
            heads.append(summed)
        return jnp.concatenate(heads, axis=1)

    def p_copy(target, nearer, place, group):
        rows = pl.ds(group * GROUP, GROUP)
        return remote(
            part_out.at[target, rows],
            part_in.at[place, rows],
            p_s.at[target * groups + group],
            p_r.at[place * groups + group],
            (nearer * 2 + side, mp),
        )

    def send_part(target, group):
        rows = pl.ds(group * GROUP, GROUP)

        @pl.when(target > line)
        def _():
            p_copy(target, line + 1, target, group).start()

        @pl.when(target < line - 1)
        def _():
            p_copy(target, line - 1, target, group).start()

        @pl.when(target == line - 1)
        def _():
            p_copy(target, line - 1, lines, group).start()

    def visit(at, onward, group):
        rows = pl.ds(group * GROUP, GROUP)
        last = (onward < 0) | (onward >= lines)
        q_copy(at, line, group, at).wait_recv()

        @pl.when(jnp.logical_not(last))
        def _():
            q_copy(at, onward, group, at).start()

        found = attend(at, group)

        @pl.when(last)
        def _():
            part_out[at, rows, :] = found.astype(jnp.bfloat16)
            send_part(at, group)

        @pl.when(jnp.logical_not(last))
        def _():
            part_own[at, rows, :] = found

    for distance in range(1, lines):

        @pl.loop(0, groups)
        def _(group):
            @pl.when(line + distance < lines)
            def _():
                visit(line + distance, line - 1, group)

            @pl.when(line - distance >= 0)
            def _():
                visit(line - distance, line + 1, group)

    def relay(turn):
        inner = (2, 3, 0)[turn]
        at = jnp.where(line == 1, inner, 3 - inner)

        @pl.loop(0, groups)
        def _(group):
            rows = pl.ds(group * GROUP, GROUP)
            p_copy(at, line, at, group).wait_recv()
            part_out[at, rows, :] = (
                part_own[at, rows, :] + part_in[at, rows, :].astype(jnp.float32)
            ).astype(jnp.bfloat16)
            send_part(at, group)

    @pl.when(above & below)
    def _():
        relay(0)
        relay(1)
        relay(2)

    part_copy(u_all, x_mp, u_sems, 1, across).wait_recv()
    part_copy(u_all, x_mp, u_sems, 2, core).start()

    @pl.loop(0, groups)
    def _(group):
        rows = pl.ds(group * GROUP, GROUP)
        own = []
        for lo in range(0, width, DH):
            query = q_all[line, rows, lo : lo + DH].astype(jnp.float32)
            key = k_own[rows, lo : lo + DH].astype(jnp.float32)
            half = jnp.sum(query * key, axis=1, keepdims=True) * (0.5 * DH ** (-0.5))
            own.append(half_silu(half) * v_own[rows, lo : lo + DH].astype(jnp.float32))
        total[rows, :] = attend(line, group) + jnp.concatenate(own, axis=1)

    part_copy(u_all, core_mp, u_sems, 0, core).wait_recv()
    part_copy(u_all, far_mp, u_sems, 2, core).wait_recv()
    for step in range(1, 4):
        out_weight_copy((mp + step) % 4, mp).wait_recv()

    def attn_copy(part, kind, group, device):
        piece = attn_all.at[part, pl.ds(group * GROUP, GROUP)]
        index = kind * groups + group
        return remote(piece, piece, a_s.at[index], a_r.at[index], device)

    def collect(group):
        rows = pl.ds(group * GROUP, GROUP)

        @pl.when(below)
        def _():
            p_copy(line, line, line, group).wait_recv()
            total[rows, :] += part_in[line, rows, :].astype(jnp.float32)

        @pl.when(above)
        def _():
            p_copy(line, line, lines, group).wait_recv()
            total[rows, :] += part_in[lines, rows, :].astype(jnp.float32)

        attn_all[mp, rows, :] = total[rows, :].astype(jnp.bfloat16)
        attn_copy(mp, 0, group, core).start()
        attn_copy(mp, 1, group, across).start()

    def pass_on(group):
        attn_copy(x_mp, 1, group, across).wait_recv()
        attn_copy(x_mp, 2, group, core).start()

    def finish(group):
        rows = pl.ds(group * GROUP, GROUP)
        attn_copy(core_mp, 0, group, core).wait_recv()
        attn_copy(far_mp, 2, group, core).wait_recv()
        attn = jnp.concatenate([attn_all[part, rows, :].astype(jnp.float32) for part in range(4)], axis=1)
        gate = jnp.concatenate([u_all[part, rows, :].astype(jnp.float32) for part in range(4)], axis=1)
        centred = attn - jnp.mean(attn, axis=1, keepdims=True)
        variance = jnp.mean(centred * centred, axis=1, keepdims=True)
        hidden = (centred * lax.rsqrt(variance + EPS) * gate).astype(jnp.bfloat16)
        mixed = own_rows[rows, :]
        for part in range(4):
            mixed = mixed + jnp.dot(
                hidden[:, part * width : (part + 1) * width],
                wo_all[part],
                preferred_element_type=jnp.float32,
            )
        out[rows, :] = mixed.astype(jnp.bfloat16)

    @pl.loop(0, groups + 2)
    def _(turn):
        @pl.when(turn < groups)
        def _():
            collect(turn)

        @pl.when((turn >= 1) & (turn < groups + 1))
        def _():
            pass_on(turn - 1)

        @pl.when(turn >= 2)
        def _():
            finish(turn - 2)

    for target in others:
        row_copy(me, target).wait_send()

    @pl.loop(0, shards)
    def _(source):
        core_copy(source).wait_send()
        x_copy(source).wait_send()
        fwd_copy(source).wait_send()

    keys_copy.wait_send()
    values_copy.wait_send()
    for step in range(1, lines):
        count_copy(line, (line + step) % lines).wait_send()
    for step in range(1, 4):
        out_weight_copy(mp, (mp + step) % 4).wait_send()
    part_copy(u_all, mp, u_sems, 0, core).wait_send()
    part_copy(u_all, mp, u_sems, 1, across).wait_send()
    part_copy(u_all, x_mp, u_sems, 2, core).wait_send()

    @pl.loop(0, groups)
    def _(group):
        for step in range(1, lines):
            at = (line + step) % lines
            p_copy(at, line, at, group).wait_send()

            @pl.when(jnp.where(at > line, below, above))
            def _():
                q_copy(at, line, group, at).wait_send()

        @pl.when(above)
        def _():
            q_copy(line, line, group, line).wait_send()

        @pl.when(below)
        def _():
            q_copy(line, line, group, lines).wait_send()

        attn_copy(mp, 0, group, core).wait_send()
        attn_copy(mp, 1, group, across).wait_send()
        attn_copy(x_mp, 2, group, core).wait_send()


def move_queries(
    cand_feats, cand_perm, w_in, w_out, cache_k, cache_v, hist_len, hist_home, hist_slot, hist_mask
):
    shards = lax.axis_size("req")
    cands, width = cand_feats.shape
    full = w_in.shape[0]
    lines = shards // 2
    groups = cands // GROUP
    keys = 2 * (MAXBLK // shards) * BLK
    bf16, f32 = jnp.bfloat16, jnp.float32
    vmem = pl.BlockSpec(memory_space=pltpu.VMEM)
    smem = pl.BlockSpec(memory_space=pltpu.SMEM)
    lots = (lines + 1) * groups
    pairs = [shards, shards, shards, shards, 2, lines, 4, lots, lots, 3, 3 * groups]
    return pl.pallas_call(
        functools.partial(kernel, shards),
        out_shape=jax.ShapeDtypeStruct((cands, width), bf16),
        in_specs=[vmem] * 7 + [smem] * 3,
        out_specs=vmem,
        scratch_shapes=[
            pltpu.VMEM((4, full, width), bf16),
            pltpu.VMEM((8, MAXBLK), f32),
            pltpu.VMEM((4, cands, width), bf16),
            pltpu.VMEM((cands, full), bf16),
            pltpu.VMEM((cands, width), f32),
            pltpu.VMEM((lines, cands, width), bf16),
            pltpu.VMEM((4, cands, width), bf16),
            pltpu.VMEM((cands, width), bf16),
            pltpu.VMEM((cands, width), bf16),
            pltpu.VMEM((4, width, width), bf16),
            pltpu.VMEM(cache_k.shape, bf16),
            pltpu.VMEM(cache_v.shape, bf16),
            pltpu.VMEM((lines, 8, MAXBLK), f32),
            pltpu.VMEM((lines, keys, width), bf16),
            pltpu.VMEM((lines, keys, width), bf16),
            pltpu.VMEM((lines, 8, keys), f32),
            pltpu.VMEM((lines, cands, width), bf16),
            pltpu.VMEM((lines + 1, cands, width), bf16),
            pltpu.VMEM((lines, cands, width), f32),
            pltpu.VMEM((cands, width), f32),
            pltpu.VMEM((4, cands, width), bf16),
        ]
        + [pltpu.SemaphoreType.DMA((count,)) for count in pairs for _ in range(2)],
        compiler_params=pltpu.CompilerParams(
            collective_id=0, has_side_effects=True, vmem_limit_bytes=48 * 1024 * 1024
        ),
        cost_estimate=pl.CostEstimate(flops=8 * 10**9, bytes_accessed=2**23, transcendentals=2**22),
    )(
        cand_feats.reshape(shards, cands // shards, width),
        cand_perm,
        w_in,
        w_out,
        cache_k,
        cache_v,
        hist_mask,
        hist_len,
        hist_home,
        hist_slot,
    )


def local(cand_feats, cand_perm, w_in, *rest):
    shards = lax.axis_size("req")
    shard_keys = MAXBLK // shards * BLK
    queries_fit = cand_perm.shape[1] <= shard_keys and shards == 8
    plan = move_queries if queries_fit and lax.axis_size("mp") == 4 else move_blocks
    return plan(cand_feats, cand_perm, w_in, *rest)


def solution(mesh):
    in_specs = (
        P("req", "mp"),
        P("req", None),
        P(None, None, "mp"),
        P("mp", None),
        P("req", None, "mp"),
        P("req", None, "mp"),
        P("req"),
        P(),
        P(),
        P("req", None, None),
    )
    out_specs = P("req", "mp")
    return jax.shard_map(local, mesh=mesh, in_specs=in_specs, out_specs=out_specs, check_vma=False)
```

```python
import functools

import jax
import jax.numpy as jnp
from jax import lax
from jax.experimental import pallas as pl
from jax.experimental.pallas import tpu as pltpu
from jax.sharding import PartitionSpec as P

HEADS = 8
DH = 128
BLK = 32
MAXBLK = 128
GROUP = 128


EPS = 1e-05


def move_blocks(
    cand_feats, cand_perm, w_in, w_out, cache_k, cache_v, hist_len, hist_home, hist_slot, hist_mask
):
    shards = lax.axis_size("req")
    own_index = lax.axis_index("req")
    columns = cand_feats.shape[1]
    cand_slot = cand_feats.shape[0] // shards
    arrived = lax.all_to_all(
        cand_feats.reshape(shards, cand_slot, columns),
        "req",
        split_axis=0,
        concat_axis=0,
        tiled=True,
    )
    arrived = arrived.reshape(shards * cand_slot, columns)
    own_rows = jnp.take(arrived, cand_perm[0], axis=0)
    full_rows = lax.all_gather(own_rows, "mp", axis=1, tiled=True)
    cand_count = full_rows.shape[0]
    features = full_rows.astype(jnp.float32)
    centred = features - jnp.mean(features, axis=1, keepdims=True)
    spread = jnp.mean(centred * centred, axis=1, keepdims=True)
    normed = (centred * lax.rsqrt(spread + EPS)).astype(jnp.bfloat16)
    local_width = w_in.shape[2]
    parts = jax.nn.silu(
        jnp.dot(
            normed, w_in.reshape(w_in.shape[0], 4 * local_width), preferred_element_type=jnp.float32
        )
    ).astype(jnp.bfloat16)
    parts = parts.reshape(cand_count, 4, local_width)
    gate_u, value_v, query_q, key_k = (parts[:, 0], parts[:, 1], parts[:, 2], parts[:, 3])
    rounds_here = MAXBLK // shards
    offsets = (own_index - hist_home) % shards
    wanted = offsets[:, None] + jnp.arange(rounds_here, dtype=jnp.int32)[None, :] * shards
    slots = jnp.take_along_axis(hist_slot, wanted, axis=1)
    send_keys = jnp.take(cache_k, slots, axis=0)
    send_values = jnp.take(cache_v, slots, axis=0)
    key_count = MAXBLK * BLK
    own_len = hist_len[0]
    got_keys, got_values = (
        lax.all_to_all(send_keys, "req", split_axis=0, concat_axis=0, tiled=True),
        lax.all_to_all(send_values, "req", split_axis=0, concat_axis=0, tiled=True),
    )
    live_keys = (jnp.arange(key_count, dtype=jnp.int32) < own_len).astype(jnp.float32)
    home_block = hist_home[own_index]
    block_order = jnp.arange(MAXBLK, dtype=jnp.int32)
    source = (home_block + block_order % shards) % shards
    round_at = block_order // shards
    hist_keys = got_keys[source, round_at].reshape(key_count, local_width)
    hist_values = got_values[source, round_at].reshape(key_count, local_width)
    block_mask = jnp.repeat(hist_mask[0].astype(jnp.float32), BLK, axis=1) * live_keys[None, :]
    score_scale = DH ** (-0.5)
    outputs = []
    for head_index in range(local_width // DH):
        lo_col = head_index * DH
        q_head = query_q[:, lo_col : lo_col + DH]
        scores = (
            lax.dot_general(
                q_head,
                hist_keys[:, lo_col : lo_col + DH],
                (((1,), (1,)), ((), ())),
                preferred_element_type=jnp.float32,
            )
            * score_scale
        )
        weights = (
            jax.nn.silu(scores).reshape(cand_count // GROUP, GROUP, key_count)
            * block_mask[:, None, :]
        )
        weights = weights.reshape(cand_count, key_count).astype(jnp.bfloat16)
        own_score = (
            jnp.sum(
                q_head.astype(jnp.float32) * key_k[:, lo_col : lo_col + DH].astype(jnp.float32),
                axis=1,
                keepdims=True,
            )
            * score_scale
        )
        own_term = jax.nn.silu(own_score) * value_v[:, lo_col : lo_col + DH].astype(jnp.float32)
        outputs.append(
            jnp.dot(
                weights, hist_values[:, lo_col : lo_col + DH], preferred_element_type=jnp.float32
            )
            + own_term
        )
    attn = jnp.concatenate(outputs, axis=1)
    width_all = HEADS * DH
    row_total = lax.psum(jnp.sum(attn, axis=1, keepdims=True), "mp")
    attn_mean = row_total / width_all
    attn_centred = attn - attn_mean
    square_total = lax.psum(jnp.sum(attn_centred * attn_centred, axis=1, keepdims=True), "mp")
    attn_spread = square_total / width_all
    hidden = (attn_centred * lax.rsqrt(attn_spread + EPS) * gate_u.astype(jnp.float32)).astype(
        jnp.bfloat16
    )
    mixed = lax.psum_scatter(
        lax.dot_general(
            w_out, hidden, (((0,), (1,)), ((), ())), preferred_element_type=jnp.float32
        ),
        "mp",
        scatter_dimension=0,
        tiled=True,
    ).T
    return (own_rows.astype(jnp.float32) + mixed).astype(jnp.bfloat16)


def remote(src, dst, send_sem, recv_sem, device):
    return pltpu.make_async_remote_copy(
        src_ref=src,
        dst_ref=dst,
        send_sem=send_sem,
        recv_sem=recv_sem,
        device_id=device,
        device_id_type=pl.DeviceIdType.MESH,
    )


def half_silu(half):
    return half + half * jnp.tanh(half)


SPAN = 256
TILE = 256


def kernel(
    shards,
    feats,
    perm,
    w_in_far,
    w_out,
    cache_k_far,
    cache_v_far,
    block_mask,
    length,
    home,
    slot,
    out,
    w_in,
    cache_k,
    cache_v,
    w_parts,
    counts,
    picked,
    rows_all,
    normed,
    own_rows,
    q_all,
    u_all,
    v_own,
    k_own,
    wo_all,
    other_k,
    other_v,
    counts_all,
    hist_k,
    hist_v,
    mask,
    part_out,
    part_in,
    part_own,
    total,
    attn_all,
    row_s,
    row_r,
    core_s,
    core_r,
    x_s,
    x_r,
    fwd_s,
    fwd_r,
    kv_s,
    kv_r,
    cnt_s,
    cnt_r,
    wo_s,
    wo_r,
    q_s,
    q_r,
    p_s,
    p_r,
    u_s,
    u_r,
    a_s,
    a_r,
    in_s,
):
    me = lax.axis_index("req")
    mp = lax.axis_index("mp")
    lines = shards // 2
    line, side = me // 2, me % 2
    lines_by_distance = (line, line + 1 - 2 * (line % 2), (line + 2) % 4, 3 - line)
    others = [(side + turn) % 2 + 2 * at for at in lines_by_distance for turn in range(2)][1:]
    mate = line * 2 + (1 - side)
    core_mp = (mp // 2) * 2 + (1 - mp % 2)
    x_mp = (1 - mp // 2) * 2 + mp % 2
    far_mp = (1 - mp // 2) * 2 + (1 - mp % 2)
    slots = feats.shape[1]
    width = feats.shape[2]
    cands = shards * slots
    groups, pieces = cands // GROUP, cands // SPAN
    rounds = MAXBLK // shards
    keys_here = rounds * BLK
    core, across, side_mate = (me, core_mp), (me, x_mp), (mate, mp)

    loads = [
        pltpu.make_async_copy(far, near, in_s.at[index])
        for index, (far, near) in enumerate(
            (
                (feats.at[me], rows_all.at[mp, pl.ds(me * slots, slots)]),
                (w_in_far, w_in),
                (cache_k_far, cache_k),
                (cache_v_far, cache_v),
                (w_out.at[:, pl.ds(pl.multiple_of(mp * width, width), width)], wo_all.at[mp]),
            )
        )
    ]
    for load in loads:
        load.start()

    barrier = pltpu.get_barrier_semaphore()
    for step in range(1, shards):
        pl.semaphore_signal(
            barrier, inc=1, device_id=((me + step) % shards, mp), device_id_type=pl.DeviceIdType.MESH
        )
    for step in range(1, 4):
        pl.semaphore_signal(
            barrier, inc=1, device_id=(me, (mp + step) % 4), device_id_type=pl.DeviceIdType.MESH
        )
    pl.semaphore_wait(barrier, shards + 2)

    def row_copy(source, target):
        return remote(
            feats.at[target],
            rows_all.at[mp, pl.ds(source * slots, slots)],
            row_s.at[target],
            row_r.at[source],
            (target, mp),
        )

    def count_copy(source, target):
        return remote(
            counts, counts_all.at[source], cnt_s.at[target], cnt_r.at[source], (target * 2 + side, mp)
        )

    def out_weight_copy(source, target):
        return remote(
            w_out.at[:, pl.ds(pl.multiple_of(target * width, width), width)],
            wo_all.at[source],
            wo_s.at[target],
            wo_r.at[source],
            (me, target),
        )

    def chunk(part, source):
        return rows_all.at[part, pl.ds(source * slots, slots)]

    def core_copy(source):
        return remote(chunk(mp, source), chunk(mp, source), core_s.at[source], core_r.at[source], core)

    def x_copy(source):
        return remote(chunk(mp, source), chunk(mp, source), x_s.at[source], x_r.at[source], across)

    def fwd_copy(source):
        return remote(chunk(x_mp, source), chunk(x_mp, source), fwd_s.at[source], fwd_r.at[source], core)

    def core_got(source):
        return remote(
            chunk(core_mp, source), chunk(core_mp, source), core_s.at[source], core_r.at[source], core
        )

    def x_got(source):
        return remote(chunk(x_mp, source), chunk(x_mp, source), x_s.at[source], x_r.at[source], across)

    def fwd_got(source):
        return remote(
            chunk(far_mp, source), chunk(far_mp, source), fwd_s.at[source], fwd_r.at[source], core
        )

    keys_copy = remote(cache_k_far, other_k, kv_s.at[0], kv_r.at[0], side_mate)
    values_copy = remote(cache_v_far, other_v, kv_s.at[1], kv_r.at[1], side_mate)

    for target in others[::-1]:
        row_copy(me, target).start()

    places = lax.broadcasted_iota(jnp.int32, (groups, MAXBLK), 1) * BLK
    counts[...] = jnp.zeros_like(counts)
    counts[0:groups, :] = (block_mask[0] * jnp.clip(length[0] - places, 0, BLK)).astype(jnp.float32)
    for step in range(1, lines):
        count_copy(line, (line + step) % lines).start()
    keys_copy.start()
    values_copy.start()
    loads[0].wait()
    counts_all[line] = counts[...]
    core_copy(me).start()
    x_copy(me).start()

    loads[1].wait()

    @pl.loop(0, w_in.shape[0], step=GROUP)
    def _(first):
        rows = pl.ds(pl.multiple_of(first, GROUP), GROUP)
        for part in range(4):
            w_parts[part, rows, :] = w_in[rows, part, :]

    for source in others:
        row_copy(source, me).wait_recv()
        core_copy(source).start()
        x_copy(source).start()

    for step in range(1, 4):
        out_weight_copy(mp, (mp + step) % 4).start()

    def gather(keys_ref, values_ref, shard, half):
        @pl.loop(0, lines)
        def _(at):
            request = at * 2 + side
            first = lax.rem(shard - home[request] + shards, shards)

            @pl.loop(0, rounds)
            def _(turn):
                place = slot[request, first + turn * shards]
                picked[pl.ds(turn * BLK, BLK), :] = keys_ref[place]
                hist_v[at, pl.ds(half * keys_here + turn * BLK, BLK), :] = values_ref[place]

            hist_k[at, :, half * keys_here : (half + 1) * keys_here] = jnp.transpose(picked[...])

    loads[2].wait()
    loads[3].wait()
    loads[4].wait()
    gather(cache_k, cache_v, me, 0)

    for source in [me] + others:
        x_got(source).wait_recv()
        fwd_copy(source).start()

    for step in range(1, lines):
        count_copy((line + step) % lines, line).wait_recv()

    @pl.loop(0, lines)
    def _(at):
        request = at * 2 + side
        number = counts_all[at].astype(jnp.bfloat16)
        for half, shard in enumerate((me, mate)):
            first = lax.rem(shard - home[request] + shards, shards)
            key_at = lax.broadcasted_iota(jnp.int32, (MAXBLK, keys_here), 1)
            block_at = lax.broadcasted_iota(jnp.int32, (MAXBLK, keys_here), 0)
            spread = (block_at == first + (key_at // BLK) * shards).astype(jnp.float32)
            live = jnp.dot(number, spread.astype(jnp.bfloat16), preferred_element_type=jnp.float32)
            place = lax.broadcasted_iota(jnp.int32, live.shape, 1) % BLK
            mask[at, :, half * keys_here : (half + 1) * keys_here] = jnp.where(
                place.astype(jnp.float32) < live, 0.5 * DH ** (-0.5), 0.0
            )

    for source in [me] + others:
        core_got(source).wait_recv()
        fwd_got(source).wait_recv()


    def q_copy(source, device_line, piece, index):
        rows = pl.ds(piece * SPAN, SPAN)
        return remote(
            q_all.at[source, rows],
            q_all.at[source, rows],
            q_s.at[index * pieces + piece],
            q_r.at[source * pieces + piece],
            (device_line * 2 + side, mp),
        )

    below, above = line > 0, line < lines - 1

    def project(part, piece):
        rows = pl.ds(piece * SPAN, SPAN)
        scores = jnp.dot(normed[rows, :], w_parts[part], preferred_element_type=jnp.float32)
        return half_silu(0.5 * scores).astype(jnp.bfloat16)

    @pl.loop(0, pieces)
    def _(piece):
        rows = pl.ds(piece * SPAN, SPAN)
        wanted = perm[:, pl.ds(pl.multiple_of(piece * SPAN, SPAN), SPAN)]
        chosen = lax.broadcasted_iota(jnp.int32, (cands, SPAN), 0) == wanted
        pick = jnp.transpose(chosen.astype(jnp.float32)).astype(jnp.bfloat16)
        features = jnp.concatenate(
            [jnp.dot(pick, rows_all[part], preferred_element_type=jnp.float32) for part in range(4)],
            axis=1,
        )
        own_rows[rows, :] = jnp.dot(pick, rows_all[mp], preferred_element_type=jnp.float32)
        centred = features - jnp.mean(features, axis=1, keepdims=True)
        variance = jnp.mean(centred * centred, axis=1, keepdims=True)
        normed[rows, :] = (centred * lax.rsqrt(variance + EPS)).astype(jnp.bfloat16)
        q_all[line, rows, :] = project(2, piece)

        @pl.when(above)
        def _():
            q_copy(line, line + 1, piece, line).start()

        @pl.when(below)
        def _():
            q_copy(line, line - 1, piece, lines).start()

    @pl.loop(0, pieces)
    def _(piece):
        u_all[mp, pl.ds(piece * SPAN, SPAN), :] = project(0, piece)

    def part_copy(buffer, part, sems, index, device):
        send, receive = sems
        return remote(buffer.at[part], buffer.at[part], send.at[index], receive.at[index], device)

    u_sems = (u_s, u_r)
    part_copy(u_all, mp, u_sems, 0, core).start()
    part_copy(u_all, mp, u_sems, 1, across).start()

    @pl.loop(0, pieces)
    def _(piece):
        rows = pl.ds(piece * SPAN, SPAN)
        v_own[rows, :] = project(1, piece)
        k_own[rows, :] = project(3, piece)

    keys_copy.wait_recv()
    values_copy.wait_recv()
    gather(other_k, other_v, mate, 1)

    def attend(at, piece):
        rows = pl.ds(piece * SPAN, SPAN)
        heads = []
        for lo in range(0, width, DH):
            query = q_all[at, rows, lo : lo + DH]
            summed = None
            for first in range(0, 2 * keys_here, TILE):
                tile = slice(first, first + TILE)
                scores = jnp.dot(query, hist_k[at, lo : lo + DH, tile], preferred_element_type=jnp.float32)
                halves = [
                    scores[at_row : at_row + GROUP]
                    * mask[at, pl.ds(piece * (SPAN // GROUP) + at_row // GROUP, 1), tile]
                    for at_row in range(0, SPAN, GROUP)
                ]
                weights = half_silu(jnp.concatenate(halves, axis=0).astype(jnp.bfloat16))
                term = jnp.dot(
                    weights, hist_v[at, tile, lo : lo + DH], preferred_element_type=jnp.float32
                )
                summed = term if summed is None else summed + term
            heads.append(summed)
        return jnp.concatenate(heads, axis=1)

    def p_copy(target, nearer, place, piece):
        rows = pl.ds(piece * SPAN, SPAN)
        return remote(
            part_out.at[target, rows],
            part_in.at[place, rows],
            p_s.at[target * pieces + piece],
            p_r.at[place * pieces + piece],
            (nearer * 2 + side, mp),
        )

    def send_part(target, piece):
        rows = pl.ds(piece * SPAN, SPAN)

        @pl.when(target > line)
        def _():
            p_copy(target, line + 1, target, piece).start()

        @pl.when(target < line - 1)
        def _():
            p_copy(target, line - 1, target, piece).start()

        @pl.when(target == line - 1)
        def _():
            p_copy(target, line - 1, lines, piece).start()

    def visit(at, onward, piece):
        rows = pl.ds(piece * SPAN, SPAN)
        last = (onward < 0) | (onward >= lines)
        q_copy(at, line, piece, at).wait_recv()

        @pl.when(jnp.logical_not(last))
        def _():
            q_copy(at, onward, piece, at).start()

        found = attend(at, piece)

        @pl.when(last)
        def _():
            part_out[at, rows, :] = found.astype(jnp.bfloat16)
            send_part(at, piece)

        @pl.when(jnp.logical_not(last))
        def _():
            part_own[at, rows, :] = found

    for distance in range(1, lines):

        @pl.loop(0, pieces)
        def _(piece):
            @pl.when(line + distance < lines)
            def _():
                visit(line + distance, line - 1, piece)

            @pl.when(line - distance >= 0)
            def _():
                visit(line - distance, line + 1, piece)

    @pl.loop(0, pieces)
    def _(piece):
        rows = pl.ds(piece * SPAN, SPAN)
        own = []
        for lo in range(0, width, DH):
            query = q_all[line, rows, lo : lo + DH].astype(jnp.float32)
            key = k_own[rows, lo : lo + DH].astype(jnp.float32)
            half = jnp.sum(query * key, axis=1, keepdims=True) * (0.5 * DH ** (-0.5))
            own.append(half_silu(half) * v_own[rows, lo : lo + DH].astype(jnp.float32))
        total[rows, :] = attend(line, piece) + jnp.concatenate(own, axis=1)

    def relay(turn):
        inner = (2, 3, 0)[turn]
        at = jnp.where(line == 1, inner, 3 - inner)

        @pl.loop(0, pieces)
        def _(piece):
            rows = pl.ds(piece * SPAN, SPAN)
            p_copy(at, line, at, piece).wait_recv()
            part_out[at, rows, :] = (
                part_own[at, rows, :] + part_in[at, rows, :].astype(jnp.float32)
            ).astype(jnp.bfloat16)
            send_part(at, piece)

    @pl.when(above & below)
    def _():
        relay(0)
        relay(1)
        relay(2)

    part_copy(u_all, x_mp, u_sems, 1, across).wait_recv()
    part_copy(u_all, x_mp, u_sems, 2, core).start()

    part_copy(u_all, core_mp, u_sems, 0, core).wait_recv()
    part_copy(u_all, far_mp, u_sems, 2, core).wait_recv()
    for step in range(1, 4):
        out_weight_copy((mp + step) % 4, mp).wait_recv()

    def attn_copy(part, kind, piece, device):
        block = attn_all.at[part, pl.ds(piece * SPAN, SPAN)]
        index = kind * pieces + piece
        return remote(block, block, a_s.at[index], a_r.at[index], device)

    def collect(piece):
        rows = pl.ds(piece * SPAN, SPAN)

        @pl.when(below)
        def _():
            p_copy(line, line, line, piece).wait_recv()
            total[rows, :] += part_in[line, rows, :].astype(jnp.float32)

        @pl.when(above)
        def _():
            p_copy(line, line, lines, piece).wait_recv()
            total[rows, :] += part_in[lines, rows, :].astype(jnp.float32)

        attn_all[mp, rows, :] = total[rows, :].astype(jnp.bfloat16)
        attn_copy(mp, 0, piece, core).start()
        attn_copy(mp, 1, piece, across).start()

    def pass_on(piece):
        attn_copy(x_mp, 1, piece, across).wait_recv()
        attn_copy(x_mp, 2, piece, core).start()

    def finish(piece):
        rows = pl.ds(piece * SPAN, SPAN)
        attn_copy(core_mp, 0, piece, core).wait_recv()
        attn_copy(far_mp, 2, piece, core).wait_recv()
        attn = jnp.concatenate([attn_all[part, rows, :].astype(jnp.float32) for part in range(4)], axis=1)
        gate = jnp.concatenate([u_all[part, rows, :].astype(jnp.float32) for part in range(4)], axis=1)
        centred = attn - jnp.mean(attn, axis=1, keepdims=True)
        variance = jnp.mean(centred * centred, axis=1, keepdims=True)
        hidden = (centred * lax.rsqrt(variance + EPS) * gate).astype(jnp.bfloat16)
        mixed = own_rows[rows, :]
        for part in range(4):
            mixed = mixed + jnp.dot(
                hidden[:, part * width : (part + 1) * width],
                wo_all[part],
                preferred_element_type=jnp.float32,
            )
        out[rows, :] = mixed.astype(jnp.bfloat16)

    @pl.loop(0, pieces + 2)
    def _(turn):
        @pl.when(turn < pieces)
        def _():
            collect(turn)

        @pl.when((turn >= 1) & (turn < pieces + 1))
        def _():
            pass_on(turn - 1)

        @pl.when(turn >= 2)
        def _():
            finish(turn - 2)

    for target in others:
        row_copy(me, target).wait_send()

    @pl.loop(0, shards)
    def _(source):
        core_copy(source).wait_send()
        x_copy(source).wait_send()
        fwd_copy(source).wait_send()

    keys_copy.wait_send()
    values_copy.wait_send()
    for step in range(1, lines):
        count_copy(line, (line + step) % lines).wait_send()
    for step in range(1, 4):
        out_weight_copy(mp, (mp + step) % 4).wait_send()
    part_copy(u_all, mp, u_sems, 0, core).wait_send()
    part_copy(u_all, mp, u_sems, 1, across).wait_send()
    part_copy(u_all, x_mp, u_sems, 2, core).wait_send()

    @pl.loop(0, pieces)
    def _(piece):
        for step in range(1, lines):
            at = (line + step) % lines
            p_copy(at, line, at, piece).wait_send()

            @pl.when(jnp.where(at > line, below, above))
            def _():
                q_copy(at, line, piece, at).wait_send()

        @pl.when(above)
        def _():
            q_copy(line, line, piece, line).wait_send()

        @pl.when(below)
        def _():
            q_copy(line, line, piece, lines).wait_send()

        attn_copy(mp, 0, piece, core).wait_send()
        attn_copy(mp, 1, piece, across).wait_send()
        attn_copy(x_mp, 2, piece, core).wait_send()


def move_queries(
    cand_feats, cand_perm, w_in, w_out, cache_k, cache_v, hist_len, hist_home, hist_slot, hist_mask
):
    shards = lax.axis_size("req")
    cands, width = cand_feats.shape
    full = w_in.shape[0]
    lines = shards // 2
    pieces = cands // SPAN
    keys = 2 * (MAXBLK // shards) * BLK
    bf16, f32 = jnp.bfloat16, jnp.float32
    vmem = pl.BlockSpec(memory_space=pltpu.VMEM)
    smem = pl.BlockSpec(memory_space=pltpu.SMEM)
    far = pl.BlockSpec(memory_space=pl.ANY)
    lots = (lines + 1) * pieces
    pairs = [shards, shards, shards, shards, 2, lines, 4, lots, lots, 3, 3 * pieces]
    return pl.pallas_call(
        functools.partial(kernel, shards),
        out_shape=jax.ShapeDtypeStruct((cands, width), bf16),
        in_specs=[far, vmem] + [far] * 4 + [vmem] + [smem] * 3,
        out_specs=vmem,
        scratch_shapes=[
            pltpu.VMEM(w_in.shape, bf16),
            pltpu.VMEM(cache_k.shape, bf16),
            pltpu.VMEM(cache_v.shape, bf16),
            pltpu.VMEM((4, full, width), bf16),
            pltpu.VMEM((8, MAXBLK), f32),
            pltpu.VMEM((keys // 2, width), bf16),
            pltpu.VMEM((4, cands, width), bf16),
            pltpu.VMEM((cands, full), bf16),
            pltpu.VMEM((cands, width), f32),
            pltpu.VMEM((lines, cands, width), bf16),
            pltpu.VMEM((4, cands, width), bf16),
            pltpu.VMEM((cands, width), bf16),
            pltpu.VMEM((cands, width), bf16),
            pltpu.VMEM((4, width, width), bf16),
            pltpu.VMEM(cache_k.shape, bf16),
            pltpu.VMEM(cache_v.shape, bf16),
            pltpu.VMEM((lines, 8, MAXBLK), f32),
            pltpu.VMEM((lines, width, keys), bf16),
            pltpu.VMEM((lines, keys, width), bf16),
            pltpu.VMEM((lines, 8, keys), f32),
            pltpu.VMEM((lines, cands, width), bf16),
            pltpu.VMEM((lines + 1, cands, width), bf16),
            pltpu.VMEM((lines, cands, width), f32),
            pltpu.VMEM((cands, width), f32),
            pltpu.VMEM((4, cands, width), bf16),
        ]
        + [pltpu.SemaphoreType.DMA((count,)) for count in pairs for _ in range(2)]
        + [pltpu.SemaphoreType.DMA((5,))],
        compiler_params=pltpu.CompilerParams(
            collective_id=0, has_side_effects=True, vmem_limit_bytes=56 * 1024 * 1024
        ),
        cost_estimate=pl.CostEstimate(flops=8 * 10**9, bytes_accessed=2**23, transcendentals=2**22),
    )(
        cand_feats.reshape(shards, cands // shards, width),
        cand_perm,
        w_in,
        w_out,
        cache_k,
        cache_v,
        hist_mask,
        hist_len,
        hist_home,
        hist_slot,
    )


def local(cand_feats, cand_perm, w_in, *rest):
    shards = lax.axis_size("req")
    shard_keys = MAXBLK // shards * BLK
    queries_fit = cand_perm.shape[1] <= shard_keys and shards == 8
    plan = move_queries if queries_fit and lax.axis_size("mp") == 4 else move_blocks
    return plan(cand_feats, cand_perm, w_in, *rest)


def solution(mesh):
    in_specs = (
        P("req", "mp"),
        P("req", None),
        P(None, None, "mp"),
        P("mp", None),
        P("req", None, "mp"),
        P("req", None, "mp"),
        P("req"),
        P(),
        P(),
        P("req", None, None),
    )
    out_specs = P("req", "mp")
    return jax.shard_map(local, mesh=mesh, in_specs=in_specs, out_specs=out_specs, check_vma=False)
```

```python
import functools

import jax
import jax.numpy as jnp
from jax import lax
from jax.experimental import pallas as pl
from jax.experimental.pallas import tpu as pltpu
from jax.sharding import PartitionSpec as P

HEADS = 8
DH = 128
BLK = 32
MAXBLK = 128
GROUP = 128


EPS = 1e-05


def move_blocks(
    cand_feats, cand_perm, w_in, w_out, cache_k, cache_v, hist_len, hist_home, hist_slot, hist_mask
):
    shards = lax.axis_size("req")
    own_index = lax.axis_index("req")
    columns = cand_feats.shape[1]
    cand_slot = cand_feats.shape[0] // shards
    arrived = lax.all_to_all(
        cand_feats.reshape(shards, cand_slot, columns),
        "req",
        split_axis=0,
        concat_axis=0,
        tiled=True,
    )
    arrived = arrived.reshape(shards * cand_slot, columns)
    own_rows = jnp.take(arrived, cand_perm[0], axis=0)
    full_rows = lax.all_gather(own_rows, "mp", axis=1, tiled=True)
    cand_count = full_rows.shape[0]
    features = full_rows.astype(jnp.float32)
    centred = features - jnp.mean(features, axis=1, keepdims=True)
    spread = jnp.mean(centred * centred, axis=1, keepdims=True)
    normed = (centred * lax.rsqrt(spread + EPS)).astype(jnp.bfloat16)
    local_width = w_in.shape[2]
    parts = jax.nn.silu(
        jnp.dot(
            normed, w_in.reshape(w_in.shape[0], 4 * local_width), preferred_element_type=jnp.float32
        )
    ).astype(jnp.bfloat16)
    parts = parts.reshape(cand_count, 4, local_width)
    gate_u, value_v, query_q, key_k = (parts[:, 0], parts[:, 1], parts[:, 2], parts[:, 3])
    rounds_here = MAXBLK // shards
    offsets = (own_index - hist_home) % shards
    wanted = offsets[:, None] + jnp.arange(rounds_here, dtype=jnp.int32)[None, :] * shards
    slots = jnp.take_along_axis(hist_slot, wanted, axis=1)
    send_keys = jnp.take(cache_k, slots, axis=0)
    send_values = jnp.take(cache_v, slots, axis=0)
    key_count = MAXBLK * BLK
    own_len = hist_len[0]
    got_keys, got_values = (
        lax.all_to_all(send_keys, "req", split_axis=0, concat_axis=0, tiled=True),
        lax.all_to_all(send_values, "req", split_axis=0, concat_axis=0, tiled=True),
    )
    live_keys = (jnp.arange(key_count, dtype=jnp.int32) < own_len).astype(jnp.float32)
    home_block = hist_home[own_index]
    block_order = jnp.arange(MAXBLK, dtype=jnp.int32)
    source = (home_block + block_order % shards) % shards
    round_at = block_order // shards
    hist_keys = got_keys[source, round_at].reshape(key_count, local_width)
    hist_values = got_values[source, round_at].reshape(key_count, local_width)
    block_mask = jnp.repeat(hist_mask[0].astype(jnp.float32), BLK, axis=1) * live_keys[None, :]
    score_scale = DH ** (-0.5)
    outputs = []
    for head_index in range(local_width // DH):
        lo_col = head_index * DH
        q_head = query_q[:, lo_col : lo_col + DH]
        scores = (
            lax.dot_general(
                q_head,
                hist_keys[:, lo_col : lo_col + DH],
                (((1,), (1,)), ((), ())),
                preferred_element_type=jnp.float32,
            )
            * score_scale
        )
        weights = (
            jax.nn.silu(scores).reshape(cand_count // GROUP, GROUP, key_count)
            * block_mask[:, None, :]
        )
        weights = weights.reshape(cand_count, key_count).astype(jnp.bfloat16)
        own_score = (
            jnp.sum(
                q_head.astype(jnp.float32) * key_k[:, lo_col : lo_col + DH].astype(jnp.float32),
                axis=1,
                keepdims=True,
            )
            * score_scale
        )
        own_term = jax.nn.silu(own_score) * value_v[:, lo_col : lo_col + DH].astype(jnp.float32)
        outputs.append(
            jnp.dot(
                weights, hist_values[:, lo_col : lo_col + DH], preferred_element_type=jnp.float32
            )
            + own_term
        )
    attn = jnp.concatenate(outputs, axis=1)
    width_all = HEADS * DH
    row_total = lax.psum(jnp.sum(attn, axis=1, keepdims=True), "mp")
    attn_mean = row_total / width_all
    attn_centred = attn - attn_mean
    square_total = lax.psum(jnp.sum(attn_centred * attn_centred, axis=1, keepdims=True), "mp")
    attn_spread = square_total / width_all
    hidden = (attn_centred * lax.rsqrt(attn_spread + EPS) * gate_u.astype(jnp.float32)).astype(
        jnp.bfloat16
    )
    mixed = lax.psum_scatter(
        lax.dot_general(
            w_out, hidden, (((0,), (1,)), ((), ())), preferred_element_type=jnp.float32
        ),
        "mp",
        scatter_dimension=0,
        tiled=True,
    ).T
    return (own_rows.astype(jnp.float32) + mixed).astype(jnp.bfloat16)


def remote(src, dst, send_sem, recv_sem, device):
    return pltpu.make_async_remote_copy(
        src_ref=src,
        dst_ref=dst,
        send_sem=send_sem,
        recv_sem=recv_sem,
        device_id=device,
        device_id_type=pl.DeviceIdType.MESH,
    )


def half_silu(half):
    return half + half * jnp.tanh(half)


SPAN = 256
TILE = 256


def kernel(
    shards,
    feats,
    perm,
    w_in_far,
    w_out,
    cache_k_far,
    cache_v_far,
    block_mask,
    length,
    home,
    slot,
    out,
    w_in,
    cache_k,
    cache_v,
    w_parts,
    counts,
    picked,
    rows_all,
    normed,
    own_rows,
    q_all,
    u_all,
    v_own,
    k_own,
    wo_all,
    other_k,
    other_v,
    counts_all,
    hist_k,
    hist_v,
    mask,
    part_out,
    part_in,
    part_own,
    total,
    attn_all,
    row_s,
    row_r,
    core_s,
    core_r,
    x_s,
    x_r,
    fwd_s,
    fwd_r,
    kv_s,
    kv_r,
    cnt_s,
    cnt_r,
    wo_s,
    wo_r,
    q_s,
    q_r,
    p_s,
    p_r,
    u_s,
    u_r,
    a_s,
    a_r,
    in_s,
):
    me = lax.axis_index("req")
    mp = lax.axis_index("mp")
    lines = shards // 2
    line, side = me // 2, me % 2
    lines_by_distance = (line, line + 1 - 2 * (line % 2), (line + 2) % 4, 3 - line)
    others = [(side + turn) % 2 + 2 * at for at in lines_by_distance for turn in range(2)][1:]
    mate = line * 2 + (1 - side)
    core_mp = (mp // 2) * 2 + (1 - mp % 2)
    x_mp = (1 - mp // 2) * 2 + mp % 2
    far_mp = (1 - mp // 2) * 2 + (1 - mp % 2)
    slots = feats.shape[1]
    width = feats.shape[2]
    cands = shards * slots
    groups, pieces = cands // GROUP, cands // SPAN
    rounds = MAXBLK // shards
    keys_here = rounds * BLK
    core, across, side_mate = (me, core_mp), (me, x_mp), (mate, mp)

    loads = [
        pltpu.make_async_copy(far, near, in_s.at[index])
        for index, (far, near) in enumerate(
            (
                (feats.at[me], rows_all.at[mp, pl.ds(me * slots, slots)]),
                (w_in_far, w_in),
                (cache_k_far, cache_k),
                (cache_v_far, cache_v),
                (w_out.at[:, pl.ds(pl.multiple_of(mp * width, width), width)], wo_all.at[mp]),
            )
        )
    ]
    for load in loads:
        load.start()

    barrier = pltpu.get_barrier_semaphore()
    for step in range(1, shards):
        pl.semaphore_signal(
            barrier, inc=1, device_id=((me + step) % shards, mp), device_id_type=pl.DeviceIdType.MESH
        )
    for step in range(1, 4):
        pl.semaphore_signal(
            barrier, inc=1, device_id=(me, (mp + step) % 4), device_id_type=pl.DeviceIdType.MESH
        )
    pl.semaphore_wait(barrier, shards + 2)

    def row_copy(source, target):
        return remote(
            feats.at[target],
            rows_all.at[mp, pl.ds(source * slots, slots)],
            row_s.at[target],
            row_r.at[source],
            (target, mp),
        )

    def count_copy(source, target):
        return remote(
            counts, counts_all.at[source], cnt_s.at[target], cnt_r.at[source], (target * 2 + side, mp)
        )

    def out_weight_copy(source, target):
        return remote(
            w_out.at[:, pl.ds(pl.multiple_of(target * width, width), width)],
            wo_all.at[source],
            wo_s.at[target],
            wo_r.at[source],
            (me, target),
        )

    def chunk(part, source):
        return rows_all.at[part, pl.ds(source * slots, slots)]

    def core_copy(source):
        return remote(chunk(mp, source), chunk(mp, source), core_s.at[source], core_r.at[source], core)

    def x_copy(source):
        return remote(chunk(mp, source), chunk(mp, source), x_s.at[source], x_r.at[source], across)

    def fwd_copy(source):
        return remote(chunk(x_mp, source), chunk(x_mp, source), fwd_s.at[source], fwd_r.at[source], core)

    def core_got(source):
        return remote(
            chunk(core_mp, source), chunk(core_mp, source), core_s.at[source], core_r.at[source], core
        )

    def x_got(source):
        return remote(chunk(x_mp, source), chunk(x_mp, source), x_s.at[source], x_r.at[source], across)

    def fwd_got(source):
        return remote(
            chunk(far_mp, source), chunk(far_mp, source), fwd_s.at[source], fwd_r.at[source], core
        )

    keys_copy = remote(cache_k_far, other_k, kv_s.at[0], kv_r.at[0], side_mate)
    values_copy = remote(cache_v_far, other_v, kv_s.at[1], kv_r.at[1], side_mate)

    for target in others[::-1]:
        row_copy(me, target).start()

    places = lax.broadcasted_iota(jnp.int32, (groups, MAXBLK), 1) * BLK
    counts[...] = jnp.zeros_like(counts)
    counts[0:groups, :] = (block_mask[0] * jnp.clip(length[0] - places, 0, BLK)).astype(jnp.float32)
    for step in range(1, lines):
        count_copy(line, (line + step) % lines).start()
    keys_copy.start()
    values_copy.start()
    loads[0].wait()
    counts_all[line] = counts[...]
    core_copy(me).start()
    x_copy(me).start()

    loads[1].wait()

    @pl.loop(0, w_in.shape[0], step=GROUP)
    def _(first):
        rows = pl.ds(pl.multiple_of(first, GROUP), GROUP)
        for part in range(4):
            w_parts[part, rows, :] = w_in[rows, part, :]

    for source in others:
        row_copy(source, me).wait_recv()
        core_copy(source).start()
        x_copy(source).start()

    for step in range(1, 4):
        out_weight_copy(mp, (mp + step) % 4).start()

    def gather(at, keys_ref, values_ref, shard, half):
        request = at * 2 + side
        first = lax.rem(shard - home[request] + shards, shards)
        for turn in range(rounds):
            place = slot[request, first + turn * shards]
            picked[turn * BLK : (turn + 1) * BLK, :] = keys_ref[place]
            begin = half * keys_here + turn * BLK
            hist_v[at, begin : begin + BLK, :] = values_ref[place]
        hist_k[at, :, half * keys_here : (half + 1) * keys_here] = jnp.transpose(picked[...])

    loads[2].wait()
    loads[3].wait()
    loads[4].wait()

    @pl.loop(0, lines)
    def _(at):
        gather(at, cache_k, cache_v, me, 0)

    for source in [me] + others:
        x_got(source).wait_recv()
        fwd_copy(source).start()

    for step in range(1, lines):
        count_copy((line + step) % lines, line).wait_recv()

    @pl.loop(0, lines)
    def _(at):
        request = at * 2 + side
        number = counts_all[at].astype(jnp.bfloat16)
        for half, shard in enumerate((me, mate)):
            first = lax.rem(shard - home[request] + shards, shards)
            key_at = lax.broadcasted_iota(jnp.int32, (MAXBLK, keys_here), 1)
            block_at = lax.broadcasted_iota(jnp.int32, (MAXBLK, keys_here), 0)
            spread = (block_at == first + (key_at // BLK) * shards).astype(jnp.float32)
            live = jnp.dot(number, spread.astype(jnp.bfloat16), preferred_element_type=jnp.float32)
            place = lax.broadcasted_iota(jnp.int32, live.shape, 1) % BLK
            mask[at, :, half * keys_here : (half + 1) * keys_here] = jnp.where(
                place.astype(jnp.float32) < live, 0.5 * DH ** (-0.5), 0.0
            )

    for source in [me] + others:
        core_got(source).wait_recv()
        fwd_got(source).wait_recv()


    def q_copy(source, device_line, piece, index):
        rows = pl.ds(piece * SPAN, SPAN)
        return remote(
            q_all.at[source, rows],
            q_all.at[source, rows],
            q_s.at[index * pieces + piece],
            q_r.at[source * pieces + piece],
            (device_line * 2 + side, mp),
        )

    below, above = line > 0, line < lines - 1

    def project(part, piece):
        rows = pl.ds(piece * SPAN, SPAN)
        scores = jnp.dot(normed[rows, :], w_parts[part], preferred_element_type=jnp.float32)
        return half_silu(0.5 * scores).astype(jnp.bfloat16)

    @pl.loop(0, pieces)
    def _(piece):
        rows = pl.ds(piece * SPAN, SPAN)
        wanted = perm[:, pl.ds(pl.multiple_of(piece * SPAN, SPAN), SPAN)]
        chosen = lax.broadcasted_iota(jnp.int32, (cands, SPAN), 0) == wanted
        pick = jnp.transpose(chosen.astype(jnp.float32)).astype(jnp.bfloat16)
        features = jnp.concatenate(
            [jnp.dot(pick, rows_all[part], preferred_element_type=jnp.float32) for part in range(4)],
            axis=1,
        )
        own_rows[rows, :] = jnp.dot(pick, rows_all[mp], preferred_element_type=jnp.float32)
        centred = features - jnp.mean(features, axis=1, keepdims=True)
        variance = jnp.mean(centred * centred, axis=1, keepdims=True)
        normed[rows, :] = (centred * lax.rsqrt(variance + EPS)).astype(jnp.bfloat16)
        q_all[line, rows, :] = project(2, piece)

        @pl.when(above)
        def _():
            q_copy(line, line + 1, piece, line).start()

        @pl.when(below)
        def _():
            q_copy(line, line - 1, piece, lines).start()

    @pl.loop(0, pieces)
    def _(piece):
        u_all[mp, pl.ds(piece * SPAN, SPAN), :] = project(0, piece)

    def part_copy(buffer, part, sems, index, device):
        send, receive = sems
        return remote(buffer.at[part], buffer.at[part], send.at[index], receive.at[index], device)

    u_sems = (u_s, u_r)
    part_copy(u_all, mp, u_sems, 0, core).start()
    part_copy(u_all, mp, u_sems, 1, across).start()

    @pl.loop(0, pieces)
    def _(piece):
        rows = pl.ds(piece * SPAN, SPAN)
        v_own[rows, :] = project(1, piece)
        k_own[rows, :] = project(3, piece)

    def attend(at, piece, half):
        rows = pl.ds(piece * SPAN, SPAN)
        heads = []
        for lo in range(0, width, DH):
            query = q_all[at, rows, lo : lo + DH]
            summed = None
            for first in range(half * keys_here, (half + 1) * keys_here, TILE):
                tile = slice(first, first + TILE)
                scores = jnp.dot(query, hist_k[at, lo : lo + DH, tile], preferred_element_type=jnp.float32)
                halves = [
                    scores[at_row : at_row + GROUP]
                    * mask[at, pl.ds(piece * (SPAN // GROUP) + at_row // GROUP, 1), tile]
                    for at_row in range(0, SPAN, GROUP)
                ]
                weights = half_silu(jnp.concatenate(halves, axis=0).astype(jnp.bfloat16))
                term = jnp.dot(
                    weights, hist_v[at, tile, lo : lo + DH], preferred_element_type=jnp.float32
                )
                summed = term if summed is None else summed + term
            heads.append(summed)
        return jnp.concatenate(heads, axis=1)

    def p_copy(target, nearer, place, piece):
        rows = pl.ds(piece * SPAN, SPAN)
        return remote(
            part_out.at[target, rows],
            part_in.at[place, rows],
            p_s.at[target * pieces + piece],
            p_r.at[place * pieces + piece],
            (nearer * 2 + side, mp),
        )

    def send_part(target, piece):
        rows = pl.ds(piece * SPAN, SPAN)

        @pl.when(target > line)
        def _():
            p_copy(target, line + 1, target, piece).start()

        @pl.when(target < line - 1)
        def _():
            p_copy(target, line - 1, target, piece).start()

        @pl.when(target == line - 1)
        def _():
            p_copy(target, line - 1, lines, piece).start()

    def visit(at, onward, piece):
        rows = pl.ds(piece * SPAN, SPAN)
        q_copy(at, line, piece, at).wait_recv()

        @pl.when((onward >= 0) & (onward < lines))
        def _():
            q_copy(at, onward, piece, at).start()

        part_own[at, rows, :] = attend(at, piece, 0)

    @pl.loop(0, pieces)
    def _(piece):
        rows = pl.ds(piece * SPAN, SPAN)
        own = []
        for lo in range(0, width, DH):
            query = q_all[line, rows, lo : lo + DH].astype(jnp.float32)
            key = k_own[rows, lo : lo + DH].astype(jnp.float32)
            half = jnp.sum(query * key, axis=1, keepdims=True) * (0.5 * DH ** (-0.5))
            own.append(half_silu(half) * v_own[rows, lo : lo + DH].astype(jnp.float32))
        total[rows, :] = attend(line, piece, 0) + jnp.concatenate(own, axis=1)

    for distance in range(1, lines):

        @pl.loop(0, pieces)
        def _(piece):
            @pl.when(line + distance < lines)
            def _():
                visit(line + distance, line - 1, piece)

            @pl.when(line - distance >= 0)
            def _():
                visit(line - distance, line + 1, piece)

    part_copy(u_all, x_mp, u_sems, 1, across).wait_recv()
    part_copy(u_all, x_mp, u_sems, 2, core).start()
    keys_copy.wait_recv()
    values_copy.wait_recv()

    low = line < 2
    for at in (jnp.where(low, 3, 0), jnp.where(low, 2, 1), jnp.where(low, 1 - line, 5 - line)):
        gather(at, other_k, other_v, mate, 1)

        @pl.loop(0, pieces)
        def _(piece):
            rows = pl.ds(piece * SPAN, SPAN)
            part_own[at, rows, :] += attend(at, piece, 1)

            @pl.when(above & below)
            def _():
                p_copy(at, line, at, piece).wait_recv()
                part_own[at, rows, :] += part_in[at, rows, :].astype(jnp.float32)

            part_out[at, rows, :] = part_own[at, rows, :].astype(jnp.bfloat16)
            send_part(at, piece)

    gather(line, other_k, other_v, mate, 1)

    @pl.loop(0, pieces)
    def _(piece):
        total[pl.ds(piece * SPAN, SPAN), :] += attend(line, piece, 1)


    part_copy(u_all, core_mp, u_sems, 0, core).wait_recv()
    part_copy(u_all, far_mp, u_sems, 2, core).wait_recv()
    for step in range(1, 4):
        out_weight_copy((mp + step) % 4, mp).wait_recv()

    def attn_copy(part, kind, piece, device):
        block = attn_all.at[part, pl.ds(piece * SPAN, SPAN)]
        index = kind * pieces + piece
        return remote(block, block, a_s.at[index], a_r.at[index], device)

    def collect(piece):
        rows = pl.ds(piece * SPAN, SPAN)

        @pl.when(below)
        def _():
            p_copy(line, line, line, piece).wait_recv()
            total[rows, :] += part_in[line, rows, :].astype(jnp.float32)

        @pl.when(above)
        def _():
            p_copy(line, line, lines, piece).wait_recv()
            total[rows, :] += part_in[lines, rows, :].astype(jnp.float32)

        attn_all[mp, rows, :] = total[rows, :].astype(jnp.bfloat16)
        attn_copy(mp, 0, piece, core).start()
        attn_copy(mp, 1, piece, across).start()

    def pass_on(piece):
        attn_copy(x_mp, 1, piece, across).wait_recv()
        attn_copy(x_mp, 2, piece, core).start()

    def finish(piece):
        rows = pl.ds(piece * SPAN, SPAN)
        attn_copy(core_mp, 0, piece, core).wait_recv()
        attn_copy(far_mp, 2, piece, core).wait_recv()
        attn = jnp.concatenate([attn_all[part, rows, :].astype(jnp.float32) for part in range(4)], axis=1)
        gate = jnp.concatenate([u_all[part, rows, :].astype(jnp.float32) for part in range(4)], axis=1)
        centred = attn - jnp.mean(attn, axis=1, keepdims=True)
        variance = jnp.mean(centred * centred, axis=1, keepdims=True)
        hidden = (centred * lax.rsqrt(variance + EPS) * gate).astype(jnp.bfloat16)
        mixed = own_rows[rows, :]
        for part in range(4):
            mixed = mixed + jnp.dot(
                hidden[:, part * width : (part + 1) * width],
                wo_all[part],
                preferred_element_type=jnp.float32,
            )
        out[rows, :] = mixed.astype(jnp.bfloat16)

    @pl.loop(0, pieces + 2)
    def _(turn):
        @pl.when(turn < pieces)
        def _():
            collect(turn)

        @pl.when((turn >= 1) & (turn < pieces + 1))
        def _():
            pass_on(turn - 1)

        @pl.when(turn >= 2)
        def _():
            finish(turn - 2)

    for target in others:
        row_copy(me, target).wait_send()

    @pl.loop(0, shards)
    def _(source):
        core_copy(source).wait_send()
        x_copy(source).wait_send()
        fwd_copy(source).wait_send()

    keys_copy.wait_send()
    values_copy.wait_send()
    for step in range(1, lines):
        count_copy(line, (line + step) % lines).wait_send()
    for step in range(1, 4):
        out_weight_copy(mp, (mp + step) % 4).wait_send()
    part_copy(u_all, mp, u_sems, 0, core).wait_send()
    part_copy(u_all, mp, u_sems, 1, across).wait_send()
    part_copy(u_all, x_mp, u_sems, 2, core).wait_send()

    @pl.loop(0, pieces)
    def _(piece):
        for step in range(1, lines):
            at = (line + step) % lines
            p_copy(at, line, at, piece).wait_send()

            @pl.when(jnp.where(at > line, below, above))
            def _():
                q_copy(at, line, piece, at).wait_send()

        @pl.when(above)
        def _():
            q_copy(line, line, piece, line).wait_send()

        @pl.when(below)
        def _():
            q_copy(line, line, piece, lines).wait_send()

        attn_copy(mp, 0, piece, core).wait_send()
        attn_copy(mp, 1, piece, across).wait_send()
        attn_copy(x_mp, 2, piece, core).wait_send()


def move_queries(
    cand_feats, cand_perm, w_in, w_out, cache_k, cache_v, hist_len, hist_home, hist_slot, hist_mask
):
    shards = lax.axis_size("req")
    cands, width = cand_feats.shape
    full = w_in.shape[0]
    lines = shards // 2
    pieces = cands // SPAN
    keys = 2 * (MAXBLK // shards) * BLK
    bf16, f32 = jnp.bfloat16, jnp.float32
    vmem = pl.BlockSpec(memory_space=pltpu.VMEM)
    smem = pl.BlockSpec(memory_space=pltpu.SMEM)
    far = pl.BlockSpec(memory_space=pl.ANY)
    lots = (lines + 1) * pieces
    pairs = [shards, shards, shards, shards, 2, lines, 4, lots, lots, 3, 3 * pieces]
    return pl.pallas_call(
        functools.partial(kernel, shards),
        out_shape=jax.ShapeDtypeStruct((cands, width), bf16),
        in_specs=[far, vmem] + [far] * 4 + [vmem] + [smem] * 3,
        out_specs=vmem,
        scratch_shapes=[
            pltpu.VMEM(w_in.shape, bf16),
            pltpu.VMEM(cache_k.shape, bf16),
            pltpu.VMEM(cache_v.shape, bf16),
            pltpu.VMEM((4, full, width), bf16),
            pltpu.VMEM((8, MAXBLK), f32),
            pltpu.VMEM((keys // 2, width), bf16),
            pltpu.VMEM((4, cands, width), bf16),
            pltpu.VMEM((cands, full), bf16),
            pltpu.VMEM((cands, width), f32),
            pltpu.VMEM((lines, cands, width), bf16),
            pltpu.VMEM((4, cands, width), bf16),
            pltpu.VMEM((cands, width), bf16),
            pltpu.VMEM((cands, width), bf16),
            pltpu.VMEM((4, width, width), bf16),
            pltpu.VMEM(cache_k.shape, bf16),
            pltpu.VMEM(cache_v.shape, bf16),
            pltpu.VMEM((lines, 8, MAXBLK), f32),
            pltpu.VMEM((lines, width, keys), bf16),
            pltpu.VMEM((lines, keys, width), bf16),
            pltpu.VMEM((lines, 8, keys), f32),
            pltpu.VMEM((lines, cands, width), bf16),
            pltpu.VMEM((lines + 1, cands, width), bf16),
            pltpu.VMEM((lines, cands, width), f32),
            pltpu.VMEM((cands, width), f32),
            pltpu.VMEM((4, cands, width), bf16),
        ]
        + [pltpu.SemaphoreType.DMA((count,)) for count in pairs for _ in range(2)]
        + [pltpu.SemaphoreType.DMA((5,))],
        compiler_params=pltpu.CompilerParams(
            collective_id=0, has_side_effects=True, vmem_limit_bytes=56 * 1024 * 1024
        ),
        cost_estimate=pl.CostEstimate(flops=8 * 10**9, bytes_accessed=2**23, transcendentals=2**22),
    )(
        cand_feats.reshape(shards, cands // shards, width),
        cand_perm,
        w_in,
        w_out,
        cache_k,
        cache_v,
        hist_mask,
        hist_len,
        hist_home,
        hist_slot,
    )


def local(cand_feats, cand_perm, w_in, *rest):
    shards = lax.axis_size("req")
    shard_keys = MAXBLK // shards * BLK
    queries_fit = cand_perm.shape[1] <= shard_keys and shards == 8
    plan = move_queries if queries_fit and lax.axis_size("mp") == 4 else move_blocks
    return plan(cand_feats, cand_perm, w_in, *rest)


def solution(mesh):
    in_specs = (
        P("req", "mp"),
        P("req", None),
        P(None, None, "mp"),
        P("mp", None),
        P("req", None, "mp"),
        P("req", None, "mp"),
        P("req"),
        P(),
        P(),
        P("req", None, None),
    )
    out_specs = P("req", "mp")
    return jax.shard_map(local, mesh=mesh, in_specs=in_specs, out_specs=out_specs, check_vma=False)
```

```python
import functools

import jax
import jax.numpy as jnp
from jax import lax
from jax.experimental import pallas as pl
from jax.experimental.pallas import tpu as pltpu
from jax.sharding import PartitionSpec as P

HEADS = 8
DH = 128
BLK = 32
MAXBLK = 128
GROUP = 128


EPS = 1e-05


def move_blocks(
    cand_feats, cand_perm, w_in, w_out, cache_k, cache_v, hist_len, hist_home, hist_slot, hist_mask
):
    shards = lax.axis_size("req")
    own_index = lax.axis_index("req")
    columns = cand_feats.shape[1]
    cand_slot = cand_feats.shape[0] // shards
    arrived = lax.all_to_all(
        cand_feats.reshape(shards, cand_slot, columns),
        "req",
        split_axis=0,
        concat_axis=0,
        tiled=True,
    )
    arrived = arrived.reshape(shards * cand_slot, columns)
    own_rows = jnp.take(arrived, cand_perm[0], axis=0)
    full_rows = lax.all_gather(own_rows, "mp", axis=1, tiled=True)
    cand_count = full_rows.shape[0]
    features = full_rows.astype(jnp.float32)
    centred = features - jnp.mean(features, axis=1, keepdims=True)
    spread = jnp.mean(centred * centred, axis=1, keepdims=True)
    normed = (centred * lax.rsqrt(spread + EPS)).astype(jnp.bfloat16)
    local_width = w_in.shape[2]
    parts = jax.nn.silu(
        jnp.dot(
            normed, w_in.reshape(w_in.shape[0], 4 * local_width), preferred_element_type=jnp.float32
        )
    ).astype(jnp.bfloat16)
    parts = parts.reshape(cand_count, 4, local_width)
    gate_u, value_v, query_q, key_k = (parts[:, 0], parts[:, 1], parts[:, 2], parts[:, 3])
    rounds_here = MAXBLK // shards
    offsets = (own_index - hist_home) % shards
    wanted = offsets[:, None] + jnp.arange(rounds_here, dtype=jnp.int32)[None, :] * shards
    slots = jnp.take_along_axis(hist_slot, wanted, axis=1)
    send_keys = jnp.take(cache_k, slots, axis=0)
    send_values = jnp.take(cache_v, slots, axis=0)
    key_count = MAXBLK * BLK
    own_len = hist_len[0]
    got_keys, got_values = (
        lax.all_to_all(send_keys, "req", split_axis=0, concat_axis=0, tiled=True),
        lax.all_to_all(send_values, "req", split_axis=0, concat_axis=0, tiled=True),
    )
    live_keys = (jnp.arange(key_count, dtype=jnp.int32) < own_len).astype(jnp.float32)
    home_block = hist_home[own_index]
    block_order = jnp.arange(MAXBLK, dtype=jnp.int32)
    source = (home_block + block_order % shards) % shards
    round_at = block_order // shards
    hist_keys = got_keys[source, round_at].reshape(key_count, local_width)
    hist_values = got_values[source, round_at].reshape(key_count, local_width)
    block_mask = jnp.repeat(hist_mask[0].astype(jnp.float32), BLK, axis=1) * live_keys[None, :]
    score_scale = DH ** (-0.5)
    outputs = []
    for head_index in range(local_width // DH):
        lo_col = head_index * DH
        q_head = query_q[:, lo_col : lo_col + DH]
        scores = (
            lax.dot_general(
                q_head,
                hist_keys[:, lo_col : lo_col + DH],
                (((1,), (1,)), ((), ())),
                preferred_element_type=jnp.float32,
            )
            * score_scale
        )
        weights = (
            jax.nn.silu(scores).reshape(cand_count // GROUP, GROUP, key_count)
            * block_mask[:, None, :]
        )
        weights = weights.reshape(cand_count, key_count).astype(jnp.bfloat16)
        own_score = (
            jnp.sum(
                q_head.astype(jnp.float32) * key_k[:, lo_col : lo_col + DH].astype(jnp.float32),
                axis=1,
                keepdims=True,
            )
            * score_scale
        )
        own_term = jax.nn.silu(own_score) * value_v[:, lo_col : lo_col + DH].astype(jnp.float32)
        outputs.append(
            jnp.dot(
                weights, hist_values[:, lo_col : lo_col + DH], preferred_element_type=jnp.float32
            )
            + own_term
        )
    attn = jnp.concatenate(outputs, axis=1)
    width_all = HEADS * DH
    row_total = lax.psum(jnp.sum(attn, axis=1, keepdims=True), "mp")
    attn_mean = row_total / width_all
    attn_centred = attn - attn_mean
    square_total = lax.psum(jnp.sum(attn_centred * attn_centred, axis=1, keepdims=True), "mp")
    attn_spread = square_total / width_all
    hidden = (attn_centred * lax.rsqrt(attn_spread + EPS) * gate_u.astype(jnp.float32)).astype(
        jnp.bfloat16
    )
    mixed = lax.psum_scatter(
        lax.dot_general(
            w_out, hidden, (((0,), (1,)), ((), ())), preferred_element_type=jnp.float32
        ),
        "mp",
        scatter_dimension=0,
        tiled=True,
    ).T
    return (own_rows.astype(jnp.float32) + mixed).astype(jnp.bfloat16)


def remote(src, dst, send_sem, recv_sem, device):
    return pltpu.make_async_remote_copy(
        src_ref=src,
        dst_ref=dst,
        send_sem=send_sem,
        recv_sem=recv_sem,
        device_id=device,
        device_id_type=pl.DeviceIdType.MESH,
    )


def half_silu(half):
    return half + half * jnp.tanh(half)


SPAN = 256
TILE = 256


def kernel(
    shards,
    feats,
    perm,
    w_parts_far,
    w_out,
    cache_k_far,
    cache_v_far,
    block_mask,
    length,
    home,
    slot,
    out,
    cache_k,
    cache_v,
    w_parts,
    counts,
    picked,
    rows_all,
    normed,
    own_rows,
    q_all,
    u_all,
    v_own,
    k_own,
    wo_all,
    other_k,
    other_v,
    counts_all,
    hist_k,
    hist_v,
    mask,
    part_out,
    part_in,
    part_own,
    total,
    attn_all,
    row_s,
    row_r,
    core_s,
    core_r,
    x_s,
    x_r,
    fwd_s,
    fwd_r,
    kv_s,
    kv_r,
    cnt_s,
    cnt_r,
    wo_s,
    wo_r,
    q_s,
    q_r,
    p_s,
    p_r,
    u_s,
    u_r,
    a_s,
    a_r,
    in_s,
):
    me = lax.axis_index("req")
    mp = lax.axis_index("mp")
    lines = shards // 2
    line, side = me // 2, me % 2
    lines_by_distance = (line, line + 1 - 2 * (line % 2), (line + 2) % 4, 3 - line)
    others = [(side + turn) % 2 + 2 * at for at in lines_by_distance for turn in range(2)][1:]
    mate = line * 2 + (1 - side)
    core_mp = (mp // 2) * 2 + (1 - mp % 2)
    x_mp = (1 - mp // 2) * 2 + mp % 2
    far_mp = (1 - mp // 2) * 2 + (1 - mp % 2)
    slots = feats.shape[1]
    width = feats.shape[2]
    cands = shards * slots
    groups, pieces = cands // GROUP, cands // SPAN
    rounds = MAXBLK // shards
    keys_here = rounds * BLK
    core, across, side_mate = (me, core_mp), (me, x_mp), (mate, mp)

    loads = [
        pltpu.make_async_copy(far, near, in_s.at[index])
        for index, (far, near) in enumerate(
            (
                (feats.at[me], rows_all.at[mp, pl.ds(me * slots, slots)]),
                (w_parts_far, w_parts),
                (cache_k_far, cache_k),
                (cache_v_far, cache_v),
                (w_out.at[:, pl.ds(pl.multiple_of(mp * width, width), width)], wo_all.at[mp]),
            )
        )
    ]
    for load in loads:
        load.start()

    barrier = pltpu.get_barrier_semaphore()
    for step in range(1, shards):
        pl.semaphore_signal(
            barrier, inc=1, device_id=((me + step) % shards, mp), device_id_type=pl.DeviceIdType.MESH
        )
    for step in range(1, 4):
        pl.semaphore_signal(
            barrier, inc=1, device_id=(me, (mp + step) % 4), device_id_type=pl.DeviceIdType.MESH
        )
    pl.semaphore_wait(barrier, shards + 2)

    def row_copy(source, target):
        return remote(
            feats.at[target],
            rows_all.at[mp, pl.ds(source * slots, slots)],
            row_s.at[target],
            row_r.at[source],
            (target, mp),
        )

    def count_copy(source, target):
        return remote(
            counts, counts_all.at[source], cnt_s.at[target], cnt_r.at[source], (target * 2 + side, mp)
        )

    def out_weight_copy(source, target):
        return remote(
            w_out.at[:, pl.ds(pl.multiple_of(target * width, width), width)],
            wo_all.at[source],
            wo_s.at[target],
            wo_r.at[source],
            (me, target),
        )

    def chunk(part, source):
        return rows_all.at[part, pl.ds(source * slots, slots)]

    def core_copy(source):
        return remote(chunk(mp, source), chunk(mp, source), core_s.at[source], core_r.at[source], core)

    def x_copy(source):
        return remote(chunk(mp, source), chunk(mp, source), x_s.at[source], x_r.at[source], across)

    def fwd_copy(source):
        return remote(chunk(x_mp, source), chunk(x_mp, source), fwd_s.at[source], fwd_r.at[source], core)

    def core_got(source):
        return remote(
            chunk(core_mp, source), chunk(core_mp, source), core_s.at[source], core_r.at[source], core
        )

    def x_got(source):
        return remote(chunk(x_mp, source), chunk(x_mp, source), x_s.at[source], x_r.at[source], across)

    def fwd_got(source):
        return remote(
            chunk(far_mp, source), chunk(far_mp, source), fwd_s.at[source], fwd_r.at[source], core
        )

    keys_copy = remote(cache_k_far, other_k, kv_s.at[0], kv_r.at[0], side_mate)
    values_copy = remote(cache_v_far, other_v, kv_s.at[1], kv_r.at[1], side_mate)

    for target in others[::-1]:
        row_copy(me, target).start()

    places = lax.broadcasted_iota(jnp.int32, (groups, MAXBLK), 1) * BLK
    counts[...] = jnp.zeros_like(counts)
    counts[0:groups, :] = (block_mask[0] * jnp.clip(length[0] - places, 0, BLK)).astype(jnp.float32)
    for step in range(1, lines):
        count_copy(line, (line + step) % lines).start()
    keys_copy.start()
    values_copy.start()
    loads[0].wait()
    counts_all[line] = counts[...]
    core_copy(me).start()
    x_copy(me).start()

    for source in others:
        row_copy(source, me).wait_recv()
        core_copy(source).start()
        x_copy(source).start()

    for step in range(1, 4):
        out_weight_copy(mp, (mp + step) % 4).start()

    def gather(at, keys_ref, values_ref, shard, half):
        request = at * 2 + side
        first = lax.rem(shard - home[request] + shards, shards)
        for turn in range(rounds):
            place = slot[request, first + turn * shards]
            picked[turn * BLK : (turn + 1) * BLK, :] = keys_ref[place]
            begin = half * keys_here + turn * BLK
            hist_v[at, begin : begin + BLK, :] = values_ref[place]
        hist_k[at, :, half * keys_here : (half + 1) * keys_here] = jnp.transpose(picked[...])

    loads[1].wait()
    loads[2].wait()
    loads[3].wait()
    loads[4].wait()

    @pl.loop(0, lines)
    def _(at):
        gather(at, cache_k, cache_v, me, 0)

    for source in [me] + others:
        x_got(source).wait_recv()
        fwd_copy(source).start()

    for step in range(1, lines):
        count_copy((line + step) % lines, line).wait_recv()

    @pl.loop(0, lines)
    def _(at):
        request = at * 2 + side
        number = counts_all[at].astype(jnp.bfloat16)
        for half, shard in enumerate((me, mate)):
            first = lax.rem(shard - home[request] + shards, shards)
            key_at = lax.broadcasted_iota(jnp.int32, (MAXBLK, keys_here), 1)
            block_at = lax.broadcasted_iota(jnp.int32, (MAXBLK, keys_here), 0)
            spread = (block_at == first + (key_at // BLK) * shards).astype(jnp.float32)
            live = jnp.dot(number, spread.astype(jnp.bfloat16), preferred_element_type=jnp.float32)
            place = lax.broadcasted_iota(jnp.int32, live.shape, 1) % BLK
            mask[at, :, half * keys_here : (half + 1) * keys_here] = jnp.where(
                place.astype(jnp.float32) < live, 0.5 * DH ** (-0.5), 0.0
            )

    for source in [me] + others:
        core_got(source).wait_recv()
        fwd_got(source).wait_recv()


    def q_copy(source, device_line, piece, index):
        rows = pl.ds(piece * SPAN, SPAN)
        return remote(
            q_all.at[source, rows],
            q_all.at[source, rows],
            q_s.at[index * pieces + piece],
            q_r.at[source * pieces + piece],
            (device_line * 2 + side, mp),
        )

    below, above = line > 0, line < lines - 1

    def project(part, piece):
        rows = pl.ds(piece * SPAN, SPAN)
        scores = jnp.dot(normed[rows, :], w_parts[part], preferred_element_type=jnp.float32)
        return half_silu(0.5 * scores).astype(jnp.bfloat16)

    @pl.loop(0, pieces)
    def _(piece):
        rows = pl.ds(piece * SPAN, SPAN)
        wanted = perm[:, pl.ds(pl.multiple_of(piece * SPAN, SPAN), SPAN)]
        chosen = lax.broadcasted_iota(jnp.int32, (cands, SPAN), 0) == wanted
        pick = jnp.transpose(chosen.astype(jnp.float32)).astype(jnp.bfloat16)
        features = jnp.concatenate(
            [jnp.dot(pick, rows_all[part], preferred_element_type=jnp.float32) for part in range(4)],
            axis=1,
        )
        own_rows[rows, :] = jnp.dot(pick, rows_all[mp], preferred_element_type=jnp.float32)
        centred = features - jnp.mean(features, axis=1, keepdims=True)
        variance = jnp.mean(centred * centred, axis=1, keepdims=True)
        normed[rows, :] = (centred * lax.rsqrt(variance + EPS)).astype(jnp.bfloat16)
        q_all[line, rows, :] = project(2, piece)

        @pl.when(above)
        def _():
            q_copy(line, line + 1, piece, line).start()

        @pl.when(below)
        def _():
            q_copy(line, line - 1, piece, lines).start()

    @pl.loop(0, pieces)
    def _(piece):
        u_all[mp, pl.ds(piece * SPAN, SPAN), :] = project(0, piece)

    def part_copy(buffer, part, sems, index, device):
        send, receive = sems
        return remote(buffer.at[part], buffer.at[part], send.at[index], receive.at[index], device)

    u_sems = (u_s, u_r)
    part_copy(u_all, mp, u_sems, 0, core).start()
    part_copy(u_all, mp, u_sems, 1, across).start()

    @pl.loop(0, pieces)
    def _(piece):
        rows = pl.ds(piece * SPAN, SPAN)
        v_own[rows, :] = project(1, piece)
        k_own[rows, :] = project(3, piece)

    def attend(at, piece, half):
        rows = pl.ds(piece * SPAN, SPAN)
        heads = []
        for lo in range(0, width, DH):
            query = q_all[at, rows, lo : lo + DH]
            summed = None
            for first in range(half * keys_here, (half + 1) * keys_here, TILE):
                tile = slice(first, first + TILE)
                scores = jnp.dot(query, hist_k[at, lo : lo + DH, tile], preferred_element_type=jnp.float32)
                halves = [
                    scores[at_row : at_row + GROUP]
                    * mask[at, pl.ds(piece * (SPAN // GROUP) + at_row // GROUP, 1), tile]
                    for at_row in range(0, SPAN, GROUP)
                ]
                weights = half_silu(jnp.concatenate(halves, axis=0).astype(jnp.bfloat16))
                term = jnp.dot(
                    weights, hist_v[at, tile, lo : lo + DH], preferred_element_type=jnp.float32
                )
                summed = term if summed is None else summed + term
            heads.append(summed)
        return jnp.concatenate(heads, axis=1)

    def p_copy(target, nearer, place, piece):
        rows = pl.ds(piece * SPAN, SPAN)
        return remote(
            part_out.at[target, rows],
            part_in.at[place, rows],
            p_s.at[target * pieces + piece],
            p_r.at[place * pieces + piece],
            (nearer * 2 + side, mp),
        )

    def send_part(target, piece):
        rows = pl.ds(piece * SPAN, SPAN)

        @pl.when(target > line)
        def _():
            p_copy(target, line + 1, target, piece).start()

        @pl.when(target < line - 1)
        def _():
            p_copy(target, line - 1, target, piece).start()

        @pl.when(target == line - 1)
        def _():
            p_copy(target, line - 1, lines, piece).start()

    def visit(at, onward, piece):
        rows = pl.ds(piece * SPAN, SPAN)
        q_copy(at, line, piece, at).wait_recv()

        @pl.when((onward >= 0) & (onward < lines))
        def _():
            q_copy(at, onward, piece, at).start()

        part_own[at, rows, :] = attend(at, piece, 0)

    @pl.loop(0, pieces)
    def _(piece):
        rows = pl.ds(piece * SPAN, SPAN)
        own = []
        for lo in range(0, width, DH):
            query = q_all[line, rows, lo : lo + DH].astype(jnp.float32)
            key = k_own[rows, lo : lo + DH].astype(jnp.float32)
            half = jnp.sum(query * key, axis=1, keepdims=True) * (0.5 * DH ** (-0.5))
            own.append(half_silu(half) * v_own[rows, lo : lo + DH].astype(jnp.float32))
        total[rows, :] = attend(line, piece, 0) + jnp.concatenate(own, axis=1)

    for distance in range(1, lines):

        @pl.loop(0, pieces)
        def _(piece):
            @pl.when(line + distance < lines)
            def _():
                visit(line + distance, line - 1, piece)

            @pl.when(line - distance >= 0)
            def _():
                visit(line - distance, line + 1, piece)

    part_copy(u_all, x_mp, u_sems, 1, across).wait_recv()
    part_copy(u_all, x_mp, u_sems, 2, core).start()
    keys_copy.wait_recv()
    values_copy.wait_recv()

    low = line < 2
    for at in (jnp.where(low, 3, 0), jnp.where(low, 2, 1), jnp.where(low, 1 - line, 5 - line)):
        gather(at, other_k, other_v, mate, 1)

        @pl.loop(0, pieces)
        def _(piece):
            rows = pl.ds(piece * SPAN, SPAN)
            part_own[at, rows, :] += attend(at, piece, 1)

            @pl.when(above & below)
            def _():
                p_copy(at, line, at, piece).wait_recv()
                part_own[at, rows, :] += part_in[at, rows, :].astype(jnp.float32)

            part_out[at, rows, :] = part_own[at, rows, :].astype(jnp.bfloat16)
            send_part(at, piece)

    gather(line, other_k, other_v, mate, 1)

    @pl.loop(0, pieces)
    def _(piece):
        total[pl.ds(piece * SPAN, SPAN), :] += attend(line, piece, 1)


    part_copy(u_all, core_mp, u_sems, 0, core).wait_recv()
    part_copy(u_all, far_mp, u_sems, 2, core).wait_recv()
    for step in range(1, 4):
        out_weight_copy((mp + step) % 4, mp).wait_recv()

    def attn_copy(part, kind, piece, device):
        block = attn_all.at[part, pl.ds(piece * SPAN, SPAN)]
        index = kind * pieces + piece
        return remote(block, block, a_s.at[index], a_r.at[index], device)

    def collect(piece):
        rows = pl.ds(piece * SPAN, SPAN)

        @pl.when(below)
        def _():
            p_copy(line, line, line, piece).wait_recv()
            total[rows, :] += part_in[line, rows, :].astype(jnp.float32)

        @pl.when(above)
        def _():
            p_copy(line, line, lines, piece).wait_recv()
            total[rows, :] += part_in[lines, rows, :].astype(jnp.float32)

        attn_all[mp, rows, :] = total[rows, :].astype(jnp.bfloat16)
        attn_copy(mp, 0, piece, core).start()
        attn_copy(mp, 1, piece, across).start()

    def pass_on(piece):
        attn_copy(x_mp, 1, piece, across).wait_recv()
        attn_copy(x_mp, 2, piece, core).start()

    def finish(piece):
        rows = pl.ds(piece * SPAN, SPAN)
        attn_copy(core_mp, 0, piece, core).wait_recv()
        attn_copy(far_mp, 2, piece, core).wait_recv()
        attn = jnp.concatenate([attn_all[part, rows, :].astype(jnp.float32) for part in range(4)], axis=1)
        gate = jnp.concatenate([u_all[part, rows, :].astype(jnp.float32) for part in range(4)], axis=1)
        centred = attn - jnp.mean(attn, axis=1, keepdims=True)
        variance = jnp.mean(centred * centred, axis=1, keepdims=True)
        hidden = (centred * lax.rsqrt(variance + EPS) * gate).astype(jnp.bfloat16)
        mixed = own_rows[rows, :]
        for part in range(4):
            mixed = mixed + jnp.dot(
                hidden[:, part * width : (part + 1) * width],
                wo_all[part],
                preferred_element_type=jnp.float32,
            )
        out[rows, :] = mixed.astype(jnp.bfloat16)

    @pl.loop(0, pieces + 2)
    def _(turn):
        @pl.when(turn < pieces)
        def _():
            collect(turn)

        @pl.when((turn >= 1) & (turn < pieces + 1))
        def _():
            pass_on(turn - 1)

        @pl.when(turn >= 2)
        def _():
            finish(turn - 2)

    for target in others:
        row_copy(me, target).wait_send()

    @pl.loop(0, shards)
    def _(source):
        core_copy(source).wait_send()
        x_copy(source).wait_send()
        fwd_copy(source).wait_send()

    keys_copy.wait_send()
    values_copy.wait_send()
    for step in range(1, lines):
        count_copy(line, (line + step) % lines).wait_send()
    for step in range(1, 4):
        out_weight_copy(mp, (mp + step) % 4).wait_send()
    part_copy(u_all, mp, u_sems, 0, core).wait_send()
    part_copy(u_all, mp, u_sems, 1, across).wait_send()
    part_copy(u_all, x_mp, u_sems, 2, core).wait_send()

    @pl.loop(0, pieces)
    def _(piece):
        for step in range(1, lines):
            at = (line + step) % lines
            p_copy(at, line, at, piece).wait_send()

            @pl.when(jnp.where(at > line, below, above))
            def _():
                q_copy(at, line, piece, at).wait_send()

        @pl.when(above)
        def _():
            q_copy(line, line, piece, line).wait_send()

        @pl.when(below)
        def _():
            q_copy(line, line, piece, lines).wait_send()

        attn_copy(mp, 0, piece, core).wait_send()
        attn_copy(mp, 1, piece, across).wait_send()
        attn_copy(x_mp, 2, piece, core).wait_send()


def move_queries(
    cand_feats, cand_perm, w_in, w_out, cache_k, cache_v, hist_len, hist_home, hist_slot, hist_mask
):
    shards = lax.axis_size("req")
    cands, width = cand_feats.shape
    full = w_in.shape[0]
    lines = shards // 2
    pieces = cands // SPAN
    keys = 2 * (MAXBLK // shards) * BLK
    bf16, f32 = jnp.bfloat16, jnp.float32
    vmem = pl.BlockSpec(memory_space=pltpu.VMEM)
    smem = pl.BlockSpec(memory_space=pltpu.SMEM)
    far = pl.BlockSpec(memory_space=pl.ANY)
    lots = (lines + 1) * pieces
    pairs = [shards, shards, shards, shards, 2, lines, 4, lots, lots, 3, 3 * pieces]
    return pl.pallas_call(
        functools.partial(kernel, shards),
        out_shape=jax.ShapeDtypeStruct((cands, width), bf16),
        in_specs=[far, vmem] + [far] * 4 + [vmem] + [smem] * 3,
        out_specs=vmem,
        scratch_shapes=[
            pltpu.VMEM(cache_k.shape, bf16),
            pltpu.VMEM(cache_v.shape, bf16),
            pltpu.VMEM((4, full, width), bf16),
            pltpu.VMEM((8, MAXBLK), f32),
            pltpu.VMEM((keys // 2, width), bf16),
            pltpu.VMEM((4, cands, width), bf16),
            pltpu.VMEM((cands, full), bf16),
            pltpu.VMEM((cands, width), f32),
            pltpu.VMEM((lines, cands, width), bf16),
            pltpu.VMEM((4, cands, width), bf16),
            pltpu.VMEM((cands, width), bf16),
            pltpu.VMEM((cands, width), bf16),
            pltpu.VMEM((4, width, width), bf16),
            pltpu.VMEM(cache_k.shape, bf16),
            pltpu.VMEM(cache_v.shape, bf16),
            pltpu.VMEM((lines, 8, MAXBLK), f32),
            pltpu.VMEM((lines, width, keys), bf16),
            pltpu.VMEM((lines, keys, width), bf16),
            pltpu.VMEM((lines, 8, keys), f32),
            pltpu.VMEM((lines, cands, width), bf16),
            pltpu.VMEM((lines + 1, cands, width), bf16),
            pltpu.VMEM((lines, cands, width), f32),
            pltpu.VMEM((cands, width), f32),
            pltpu.VMEM((4, cands, width), bf16),
        ]
        + [pltpu.SemaphoreType.DMA((count,)) for count in pairs for _ in range(2)]
        + [pltpu.SemaphoreType.DMA((5,))],
        compiler_params=pltpu.CompilerParams(
            collective_id=0, has_side_effects=True, vmem_limit_bytes=56 * 1024 * 1024
        ),
        cost_estimate=pl.CostEstimate(flops=8 * 10**9, bytes_accessed=2**23, transcendentals=2**22),
    )(
        cand_feats.reshape(shards, cands // shards, width),
        cand_perm,
        w_in.transpose(1, 0, 2),
        w_out,
        cache_k,
        cache_v,
        hist_mask,
        hist_len,
        hist_home,
        hist_slot,
    )


def local(cand_feats, cand_perm, w_in, *rest):
    shards = lax.axis_size("req")
    shard_keys = MAXBLK // shards * BLK
    queries_fit = cand_perm.shape[1] <= shard_keys and shards == 8
    plan = move_queries if queries_fit and lax.axis_size("mp") == 4 else move_blocks
    return plan(cand_feats, cand_perm, w_in, *rest)


def solution(mesh):
    in_specs = (
        P("req", "mp"),
        P("req", None),
        P(None, None, "mp"),
        P("mp", None),
        P("req", None, "mp"),
        P("req", None, "mp"),
        P("req"),
        P(),
        P(),
        P("req", None, None),
    )
    out_specs = P("req", "mp")
    return jax.shard_map(local, mesh=mesh, in_specs=in_specs, out_specs=out_specs, check_vma=False)
```

```python
import functools

import jax
import jax.numpy as jnp
from jax import lax
from jax.experimental import pallas as pl
from jax.experimental.pallas import tpu as pltpu
from jax.sharding import PartitionSpec as P

HEADS = 8
DH = 128
BLK = 32
MAXBLK = 128
GROUP = 128


EPS = 1e-05


def move_blocks(
    cand_feats, cand_perm, w_in, w_out, cache_k, cache_v, hist_len, hist_home, hist_slot, hist_mask
):
    shards = lax.axis_size("req")
    own_index = lax.axis_index("req")
    columns = cand_feats.shape[1]
    cand_slot = cand_feats.shape[0] // shards
    arrived = lax.all_to_all(
        cand_feats.reshape(shards, cand_slot, columns),
        "req",
        split_axis=0,
        concat_axis=0,
        tiled=True,
    )
    arrived = arrived.reshape(shards * cand_slot, columns)
    own_rows = jnp.take(arrived, cand_perm[0], axis=0)
    full_rows = lax.all_gather(own_rows, "mp", axis=1, tiled=True)
    cand_count = full_rows.shape[0]
    features = full_rows.astype(jnp.float32)
    centred = features - jnp.mean(features, axis=1, keepdims=True)
    spread = jnp.mean(centred * centred, axis=1, keepdims=True)
    normed = (centred * lax.rsqrt(spread + EPS)).astype(jnp.bfloat16)
    local_width = w_in.shape[2]
    parts = jax.nn.silu(
        jnp.dot(
            normed, w_in.reshape(w_in.shape[0], 4 * local_width), preferred_element_type=jnp.float32
        )
    ).astype(jnp.bfloat16)
    parts = parts.reshape(cand_count, 4, local_width)
    gate_u, value_v, query_q, key_k = (parts[:, 0], parts[:, 1], parts[:, 2], parts[:, 3])
    rounds_here = MAXBLK // shards
    offsets = (own_index - hist_home) % shards
    wanted = offsets[:, None] + jnp.arange(rounds_here, dtype=jnp.int32)[None, :] * shards
    slots = jnp.take_along_axis(hist_slot, wanted, axis=1)
    send_keys = jnp.take(cache_k, slots, axis=0)
    send_values = jnp.take(cache_v, slots, axis=0)
    key_count = MAXBLK * BLK
    own_len = hist_len[0]
    got_keys, got_values = (
        lax.all_to_all(send_keys, "req", split_axis=0, concat_axis=0, tiled=True),
        lax.all_to_all(send_values, "req", split_axis=0, concat_axis=0, tiled=True),
    )
    live_keys = (jnp.arange(key_count, dtype=jnp.int32) < own_len).astype(jnp.float32)
    home_block = hist_home[own_index]
    block_order = jnp.arange(MAXBLK, dtype=jnp.int32)
    source = (home_block + block_order % shards) % shards
    round_at = block_order // shards
    hist_keys = got_keys[source, round_at].reshape(key_count, local_width)
    hist_values = got_values[source, round_at].reshape(key_count, local_width)
    block_mask = jnp.repeat(hist_mask[0].astype(jnp.float32), BLK, axis=1) * live_keys[None, :]
    score_scale = DH ** (-0.5)
    outputs = []
    for head_index in range(local_width // DH):
        lo_col = head_index * DH
        q_head = query_q[:, lo_col : lo_col + DH]
        scores = (
            lax.dot_general(
                q_head,
                hist_keys[:, lo_col : lo_col + DH],
                (((1,), (1,)), ((), ())),
                preferred_element_type=jnp.float32,
            )
            * score_scale
        )
        weights = (
            jax.nn.silu(scores).reshape(cand_count // GROUP, GROUP, key_count)
            * block_mask[:, None, :]
        )
        weights = weights.reshape(cand_count, key_count).astype(jnp.bfloat16)
        own_score = (
            jnp.sum(
                q_head.astype(jnp.float32) * key_k[:, lo_col : lo_col + DH].astype(jnp.float32),
                axis=1,
                keepdims=True,
            )
            * score_scale
        )
        own_term = jax.nn.silu(own_score) * value_v[:, lo_col : lo_col + DH].astype(jnp.float32)
        outputs.append(
            jnp.dot(
                weights, hist_values[:, lo_col : lo_col + DH], preferred_element_type=jnp.float32
            )
            + own_term
        )
    attn = jnp.concatenate(outputs, axis=1)
    width_all = HEADS * DH
    row_total = lax.psum(jnp.sum(attn, axis=1, keepdims=True), "mp")
    attn_mean = row_total / width_all
    attn_centred = attn - attn_mean
    square_total = lax.psum(jnp.sum(attn_centred * attn_centred, axis=1, keepdims=True), "mp")
    attn_spread = square_total / width_all
    hidden = (attn_centred * lax.rsqrt(attn_spread + EPS) * gate_u.astype(jnp.float32)).astype(
        jnp.bfloat16
    )
    mixed = lax.psum_scatter(
        lax.dot_general(
            w_out, hidden, (((0,), (1,)), ((), ())), preferred_element_type=jnp.float32
        ),
        "mp",
        scatter_dimension=0,
        tiled=True,
    ).T
    return (own_rows.astype(jnp.float32) + mixed).astype(jnp.bfloat16)


def remote(src, dst, send_sem, recv_sem, device):
    return pltpu.make_async_remote_copy(
        src_ref=src,
        dst_ref=dst,
        send_sem=send_sem,
        recv_sem=recv_sem,
        device_id=device,
        device_id_type=pl.DeviceIdType.MESH,
    )


def half_silu(half):
    return half + half * jnp.tanh(half)


SPAN = 256
TILE = 256


def kernel(
    shards,
    feats,
    perm,
    w_in_far,
    w_out,
    cache_k_far,
    cache_v_far,
    block_mask,
    length,
    home,
    slot,
    out,
    w_in,
    cache_k,
    cache_v,
    w_parts,
    counts,
    picked,
    rows_all,
    normed,
    own_rows,
    q_all,
    u_all,
    v_own,
    k_own,
    wo_all,
    other_k,
    other_v,
    counts_all,
    hist_k,
    hist_v,
    mask,
    part_out,
    part_in,
    part_own,
    total,
    attn_all,
    row_s,
    row_r,
    core_s,
    core_r,
    x_s,
    x_r,
    fwd_s,
    fwd_r,
    kv_s,
    kv_r,
    cnt_s,
    cnt_r,
    wo_s,
    wo_r,
    q_s,
    q_r,
    p_s,
    p_r,
    u_s,
    u_r,
    a_s,
    a_r,
    in_s,
):
    me = lax.axis_index("req")
    mp = lax.axis_index("mp")
    lines = shards // 2
    line, side = me // 2, me % 2
    lines_by_distance = (line, line + 1 - 2 * (line % 2), (line + 2) % 4, 3 - line)
    others = [(side + turn) % 2 + 2 * at for at in lines_by_distance for turn in range(2)][1:]
    mate = line * 2 + (1 - side)
    core_mp = (mp // 2) * 2 + (1 - mp % 2)
    x_mp = (1 - mp // 2) * 2 + mp % 2
    far_mp = (1 - mp // 2) * 2 + (1 - mp % 2)
    slots = feats.shape[1]
    width = feats.shape[2]
    cands = shards * slots
    groups, pieces = cands // GROUP, cands // SPAN
    rounds = MAXBLK // shards
    keys_here = rounds * BLK
    core, across, side_mate = (me, core_mp), (me, x_mp), (mate, mp)

    loads = [
        pltpu.make_async_copy(far, near, in_s.at[index])
        for index, (far, near) in enumerate(
            (
                (feats.at[me], rows_all.at[mp, pl.ds(me * slots, slots)]),
                (w_in_far, w_in),
                (cache_k_far, cache_k),
                (cache_v_far, cache_v),
                (w_out.at[:, pl.ds(pl.multiple_of(mp * width, width), width)], wo_all.at[mp]),
            )
        )
    ]
    for load in loads:
        load.start()

    barrier = pltpu.get_barrier_semaphore()
    for step in range(1, shards):
        pl.semaphore_signal(
            barrier, inc=1, device_id=((me + step) % shards, mp), device_id_type=pl.DeviceIdType.MESH
        )
    for step in range(1, 4):
        pl.semaphore_signal(
            barrier, inc=1, device_id=(me, (mp + step) % 4), device_id_type=pl.DeviceIdType.MESH
        )
    pl.semaphore_wait(barrier, shards + 2)

    def row_copy(source, target):
        return remote(
            feats.at[target],
            rows_all.at[mp, pl.ds(source * slots, slots)],
            row_s.at[target],
            row_r.at[source],
            (target, mp),
        )

    def count_copy(source, target):
        return remote(
            counts, counts_all.at[source], cnt_s.at[target], cnt_r.at[source], (target * 2 + side, mp)
        )

    def out_weight_copy(source, target):
        return remote(
            w_out.at[:, pl.ds(pl.multiple_of(target * width, width), width)],
            wo_all.at[source],
            wo_s.at[target],
            wo_r.at[source],
            (me, target),
        )

    def chunk(part, source):
        return rows_all.at[part, pl.ds(source * slots, slots)]

    def core_copy(source):
        return remote(chunk(mp, source), chunk(mp, source), core_s.at[source], core_r.at[source], core)

    def x_copy(source):
        return remote(chunk(mp, source), chunk(mp, source), x_s.at[source], x_r.at[source], across)

    def fwd_copy(source):
        return remote(chunk(x_mp, source), chunk(x_mp, source), fwd_s.at[source], fwd_r.at[source], core)

    def core_got(source):
        return remote(
            chunk(core_mp, source), chunk(core_mp, source), core_s.at[source], core_r.at[source], core
        )

    def x_got(source):
        return remote(chunk(x_mp, source), chunk(x_mp, source), x_s.at[source], x_r.at[source], across)

    def fwd_got(source):
        return remote(
            chunk(far_mp, source), chunk(far_mp, source), fwd_s.at[source], fwd_r.at[source], core
        )

    share = cache_k.shape[0] // 8

    def cache_copy(index):
        near, other = ((cache_k_far, other_k), (cache_v_far, other_v))[index // 8]
        blocks = pl.ds(index % 8 * share, share)
        return remote(near.at[blocks], other.at[blocks], kv_s.at[index], kv_r.at[index], side_mate)

    for target in others[::-1]:
        row_copy(me, target).start()

    places = lax.broadcasted_iota(jnp.int32, (groups, MAXBLK), 1) * BLK
    counts[...] = jnp.zeros_like(counts)
    counts[0:groups, :] = (block_mask[0] * jnp.clip(length[0] - places, 0, BLK)).astype(jnp.float32)
    for step in range(1, lines):
        count_copy(line, (line + step) % lines).start()
    for index in range(4):
        cache_copy(index).start()
    loads[0].wait()
    counts_all[line] = counts[...]
    core_copy(me).start()
    x_copy(me).start()

    loads[1].wait()

    @pl.loop(0, w_in.shape[0], step=GROUP)
    def _(first):
        rows = pl.ds(pl.multiple_of(first, GROUP), GROUP)
        for part in range(4):
            w_parts[part, rows, :] = w_in[rows, part, :]

    for index, source in enumerate(others, 4):
        row_copy(source, me).wait_recv()
        core_copy(source).start()
        x_copy(source).start()
        cache_copy(index).start()

    for step in range(1, 4):
        out_weight_copy(mp, (mp + step) % 4).start()

    def gather(at, keys_ref, values_ref, shard, half):
        request = at * 2 + side
        first = lax.rem(shard - home[request] + shards, shards)
        for turn in range(rounds):
            place = slot[request, first + turn * shards]
            picked[turn * BLK : (turn + 1) * BLK, :] = keys_ref[place]
            begin = half * keys_here + turn * BLK
            hist_v[at, begin : begin + BLK, :] = values_ref[place]
        hist_k[at, :, half * keys_here : (half + 1) * keys_here] = jnp.transpose(picked[...])

    loads[2].wait()
    loads[3].wait()
    loads[4].wait()

    @pl.loop(0, lines)
    def _(at):
        gather(at, cache_k, cache_v, me, 0)

    for index, source in enumerate([me] + others, 11):
        x_got(source).wait_recv()
        fwd_copy(source).start()
        if index < 16:
            cache_copy(index).start()

    for step in range(1, lines):
        count_copy((line + step) % lines, line).wait_recv()

    @pl.loop(0, lines)
    def _(at):
        request = at * 2 + side
        number = counts_all[at].astype(jnp.bfloat16)
        for half, shard in enumerate((me, mate)):
            first = lax.rem(shard - home[request] + shards, shards)
            key_at = lax.broadcasted_iota(jnp.int32, (MAXBLK, keys_here), 1)
            block_at = lax.broadcasted_iota(jnp.int32, (MAXBLK, keys_here), 0)
            spread = (block_at == first + (key_at // BLK) * shards).astype(jnp.float32)
            live = jnp.dot(number, spread.astype(jnp.bfloat16), preferred_element_type=jnp.float32)
            place = lax.broadcasted_iota(jnp.int32, live.shape, 1) % BLK
            mask[at, :, half * keys_here : (half + 1) * keys_here] = jnp.where(
                place.astype(jnp.float32) < live, 0.5 * DH ** (-0.5), 0.0
            )

    for source in [me] + others:
        core_got(source).wait_recv()
        fwd_got(source).wait_recv()


    def q_copy(source, device_line, piece, index):
        rows = pl.ds(piece * SPAN, SPAN)
        return remote(
            q_all.at[source, rows],
            q_all.at[source, rows],
            q_s.at[index * pieces + piece],
            q_r.at[source * pieces + piece],
            (device_line * 2 + side, mp),
        )

    below, above = line > 0, line < lines - 1

    def project(part, piece):
        rows = pl.ds(piece * SPAN, SPAN)
        scores = jnp.dot(normed[rows, :], w_parts[part], preferred_element_type=jnp.float32)
        return half_silu(0.5 * scores).astype(jnp.bfloat16)

    @pl.loop(0, pieces)
    def _(piece):
        rows = pl.ds(piece * SPAN, SPAN)
        wanted = perm[:, pl.ds(pl.multiple_of(piece * SPAN, SPAN), SPAN)]
        chosen = lax.broadcasted_iota(jnp.int32, (cands, SPAN), 0) == wanted
        pick = jnp.transpose(chosen.astype(jnp.float32)).astype(jnp.bfloat16)
        features = jnp.concatenate(
            [jnp.dot(pick, rows_all[part], preferred_element_type=jnp.float32) for part in range(4)],
            axis=1,
        )
        own_rows[rows, :] = jnp.dot(pick, rows_all[mp], preferred_element_type=jnp.float32)
        centred = features - jnp.mean(features, axis=1, keepdims=True)
        variance = jnp.mean(centred * centred, axis=1, keepdims=True)
        normed[rows, :] = (centred * lax.rsqrt(variance + EPS)).astype(jnp.bfloat16)
        q_all[line, rows, :] = project(2, piece)

        @pl.when(above)
        def _():
            q_copy(line, line + 1, piece, line).start()

        @pl.when(below)
        def _():
            q_copy(line, line - 1, piece, lines).start()

    @pl.loop(0, pieces)
    def _(piece):
        u_all[mp, pl.ds(piece * SPAN, SPAN), :] = project(0, piece)

    def part_copy(buffer, part, sems, index, device):
        send, receive = sems
        return remote(buffer.at[part], buffer.at[part], send.at[index], receive.at[index], device)

    u_sems = (u_s, u_r)
    part_copy(u_all, mp, u_sems, 0, core).start()
    part_copy(u_all, mp, u_sems, 1, across).start()

    @pl.loop(0, pieces)
    def _(piece):
        rows = pl.ds(piece * SPAN, SPAN)
        v_own[rows, :] = project(1, piece)
        k_own[rows, :] = project(3, piece)

    def attend(at, piece, half):
        rows = pl.ds(piece * SPAN, SPAN)
        heads = []
        for lo in range(0, width, DH):
            query = q_all[at, rows, lo : lo + DH]
            summed = None
            for first in range(half * keys_here, (half + 1) * keys_here, TILE):
                tile = slice(first, first + TILE)
                scores = jnp.dot(query, hist_k[at, lo : lo + DH, tile], preferred_element_type=jnp.float32)
                halves = [
                    scores[at_row : at_row + GROUP]
                    * mask[at, pl.ds(piece * (SPAN // GROUP) + at_row // GROUP, 1), tile]
                    for at_row in range(0, SPAN, GROUP)
                ]
                weights = half_silu(jnp.concatenate(halves, axis=0).astype(jnp.bfloat16))
                term = jnp.dot(
                    weights, hist_v[at, tile, lo : lo + DH], preferred_element_type=jnp.float32
                )
                summed = term if summed is None else summed + term
            heads.append(summed)
        return jnp.concatenate(heads, axis=1)

    def p_copy(target, nearer, place, piece):
        rows = pl.ds(piece * SPAN, SPAN)
        return remote(
            part_out.at[target, rows],
            part_in.at[place, rows],
            p_s.at[target * pieces + piece],
            p_r.at[place * pieces + piece],
            (nearer * 2 + side, mp),
        )

    def send_part(target, piece):
        rows = pl.ds(piece * SPAN, SPAN)

        @pl.when(target > line)
        def _():
            p_copy(target, line + 1, target, piece).start()

        @pl.when(target < line - 1)
        def _():
            p_copy(target, line - 1, target, piece).start()

        @pl.when(target == line - 1)
        def _():
            p_copy(target, line - 1, lines, piece).start()

    def visit(at, onward, piece):
        rows = pl.ds(piece * SPAN, SPAN)
        q_copy(at, line, piece, at).wait_recv()

        @pl.when((onward >= 0) & (onward < lines))
        def _():
            q_copy(at, onward, piece, at).start()

        part_own[at, rows, :] = attend(at, piece, 0)

    @pl.loop(0, pieces)
    def _(piece):
        rows = pl.ds(piece * SPAN, SPAN)
        own = []
        for lo in range(0, width, DH):
            query = q_all[line, rows, lo : lo + DH].astype(jnp.float32)
            key = k_own[rows, lo : lo + DH].astype(jnp.float32)
            half = jnp.sum(query * key, axis=1, keepdims=True) * (0.5 * DH ** (-0.5))
            own.append(half_silu(half) * v_own[rows, lo : lo + DH].astype(jnp.float32))
        total[rows, :] = attend(line, piece, 0) + jnp.concatenate(own, axis=1)

    for distance in range(1, lines):

        @pl.loop(0, pieces)
        def _(piece):
            @pl.when(line + distance < lines)
            def _():
                visit(line + distance, line - 1, piece)

            @pl.when(line - distance >= 0)
            def _():
                visit(line - distance, line + 1, piece)

    part_copy(u_all, x_mp, u_sems, 1, across).wait_recv()
    part_copy(u_all, x_mp, u_sems, 2, core).start()
    for index in range(16):
        cache_copy(index).wait_recv()

    low = line < 2
    for at in (jnp.where(low, 3, 0), jnp.where(low, 2, 1), jnp.where(low, 1 - line, 5 - line)):
        gather(at, other_k, other_v, mate, 1)

        @pl.loop(0, pieces)
        def _(piece):
            rows = pl.ds(piece * SPAN, SPAN)
            part_own[at, rows, :] += attend(at, piece, 1)

            @pl.when(above & below)
            def _():
                p_copy(at, line, at, piece).wait_recv()
                part_own[at, rows, :] += part_in[at, rows, :].astype(jnp.float32)

            part_out[at, rows, :] = part_own[at, rows, :].astype(jnp.bfloat16)
            send_part(at, piece)

    gather(line, other_k, other_v, mate, 1)

    @pl.loop(0, pieces)
    def _(piece):
        total[pl.ds(piece * SPAN, SPAN), :] += attend(line, piece, 1)


    part_copy(u_all, core_mp, u_sems, 0, core).wait_recv()
    part_copy(u_all, far_mp, u_sems, 2, core).wait_recv()
    for step in range(1, 4):
        out_weight_copy((mp + step) % 4, mp).wait_recv()

    def attn_copy(part, kind, piece, device):
        block = attn_all.at[part, pl.ds(piece * SPAN, SPAN)]
        index = kind * pieces + piece
        return remote(block, block, a_s.at[index], a_r.at[index], device)

    def collect(piece):
        rows = pl.ds(piece * SPAN, SPAN)

        @pl.when(below)
        def _():
            p_copy(line, line, line, piece).wait_recv()
            total[rows, :] += part_in[line, rows, :].astype(jnp.float32)

        @pl.when(above)
        def _():
            p_copy(line, line, lines, piece).wait_recv()
            total[rows, :] += part_in[lines, rows, :].astype(jnp.float32)

        attn_all[mp, rows, :] = total[rows, :].astype(jnp.bfloat16)
        attn_copy(mp, 0, piece, core).start()
        attn_copy(mp, 1, piece, across).start()

    def pass_on(piece):
        attn_copy(x_mp, 1, piece, across).wait_recv()
        attn_copy(x_mp, 2, piece, core).start()

    def finish(piece):
        rows = pl.ds(piece * SPAN, SPAN)
        attn_copy(core_mp, 0, piece, core).wait_recv()
        attn_copy(far_mp, 2, piece, core).wait_recv()
        attn = jnp.concatenate([attn_all[part, rows, :].astype(jnp.float32) for part in range(4)], axis=1)
        gate = jnp.concatenate([u_all[part, rows, :].astype(jnp.float32) for part in range(4)], axis=1)
        centred = attn - jnp.mean(attn, axis=1, keepdims=True)
        variance = jnp.mean(centred * centred, axis=1, keepdims=True)
        hidden = (centred * lax.rsqrt(variance + EPS) * gate).astype(jnp.bfloat16)
        mixed = own_rows[rows, :]
        for part in range(4):
            mixed = mixed + jnp.dot(
                hidden[:, part * width : (part + 1) * width],
                wo_all[part],
                preferred_element_type=jnp.float32,
            )
        out[rows, :] = mixed.astype(jnp.bfloat16)

    @pl.loop(0, pieces + 2)
    def _(turn):
        @pl.when(turn < pieces)
        def _():
            collect(turn)

        @pl.when((turn >= 1) & (turn < pieces + 1))
        def _():
            pass_on(turn - 1)

        @pl.when(turn >= 2)
        def _():
            finish(turn - 2)

    for target in others:
        row_copy(me, target).wait_send()

    @pl.loop(0, shards)
    def _(source):
        core_copy(source).wait_send()
        x_copy(source).wait_send()
        fwd_copy(source).wait_send()

    for index in range(16):
        cache_copy(index).wait_send()
    for step in range(1, lines):
        count_copy(line, (line + step) % lines).wait_send()
    for step in range(1, 4):
        out_weight_copy(mp, (mp + step) % 4).wait_send()
    part_copy(u_all, mp, u_sems, 0, core).wait_send()
    part_copy(u_all, mp, u_sems, 1, across).wait_send()
    part_copy(u_all, x_mp, u_sems, 2, core).wait_send()

    @pl.loop(0, pieces)
    def _(piece):
        for step in range(1, lines):
            at = (line + step) % lines
            p_copy(at, line, at, piece).wait_send()

            @pl.when(jnp.where(at > line, below, above))
            def _():
                q_copy(at, line, piece, at).wait_send()

        @pl.when(above)
        def _():
            q_copy(line, line, piece, line).wait_send()

        @pl.when(below)
        def _():
            q_copy(line, line, piece, lines).wait_send()

        attn_copy(mp, 0, piece, core).wait_send()
        attn_copy(mp, 1, piece, across).wait_send()
        attn_copy(x_mp, 2, piece, core).wait_send()


def move_queries(
    cand_feats, cand_perm, w_in, w_out, cache_k, cache_v, hist_len, hist_home, hist_slot, hist_mask
):
    shards = lax.axis_size("req")
    cands, width = cand_feats.shape
    full = w_in.shape[0]
    lines = shards // 2
    pieces = cands // SPAN
    keys = 2 * (MAXBLK // shards) * BLK
    bf16, f32 = jnp.bfloat16, jnp.float32
    vmem = pl.BlockSpec(memory_space=pltpu.VMEM)
    smem = pl.BlockSpec(memory_space=pltpu.SMEM)
    far = pl.BlockSpec(memory_space=pl.ANY)
    lots = (lines + 1) * pieces
    pairs = [shards, shards, shards, shards, 16, lines, 4, lots, lots, 3, 3 * pieces]
    return pl.pallas_call(
        functools.partial(kernel, shards),
        out_shape=jax.ShapeDtypeStruct((cands, width), bf16),
        in_specs=[far, vmem] + [far] * 4 + [vmem] + [smem] * 3,
        out_specs=vmem,
        scratch_shapes=[
            pltpu.VMEM(w_in.shape, bf16),
            pltpu.VMEM(cache_k.shape, bf16),
            pltpu.VMEM(cache_v.shape, bf16),
            pltpu.VMEM((4, full, width), bf16),
            pltpu.VMEM((8, MAXBLK), f32),
            pltpu.VMEM((keys // 2, width), bf16),
            pltpu.VMEM((4, cands, width), bf16),
            pltpu.VMEM((cands, full), bf16),
            pltpu.VMEM((cands, width), f32),
            pltpu.VMEM((lines, cands, width), bf16),
            pltpu.VMEM((4, cands, width), bf16),
            pltpu.VMEM((cands, width), bf16),
            pltpu.VMEM((cands, width), bf16),
            pltpu.VMEM((4, width, width), bf16),
            pltpu.VMEM(cache_k.shape, bf16),
            pltpu.VMEM(cache_v.shape, bf16),
            pltpu.VMEM((lines, 8, MAXBLK), f32),
            pltpu.VMEM((lines, width, keys), bf16),
            pltpu.VMEM((lines, keys, width), bf16),
            pltpu.VMEM((lines, 8, keys), f32),
            pltpu.VMEM((lines, cands, width), bf16),
            pltpu.VMEM((lines + 1, cands, width), bf16),
            pltpu.VMEM((lines, cands, width), f32),
            pltpu.VMEM((cands, width), f32),
            pltpu.VMEM((4, cands, width), bf16),
        ]
        + [pltpu.SemaphoreType.DMA((count,)) for count in pairs for _ in range(2)]
        + [pltpu.SemaphoreType.DMA((5,))],
        compiler_params=pltpu.CompilerParams(
            collective_id=0, has_side_effects=True, vmem_limit_bytes=56 * 1024 * 1024
        ),
        cost_estimate=pl.CostEstimate(flops=8 * 10**9, bytes_accessed=2**23, transcendentals=2**22),
    )(
        cand_feats.reshape(shards, cands // shards, width),
        cand_perm,
        w_in,
        w_out,
        cache_k,
        cache_v,
        hist_mask,
        hist_len,
        hist_home,
        hist_slot,
    )


def local(cand_feats, cand_perm, w_in, *rest):
    shards = lax.axis_size("req")
    shard_keys = MAXBLK // shards * BLK
    queries_fit = cand_perm.shape[1] <= shard_keys and shards == 8
    plan = move_queries if queries_fit and lax.axis_size("mp") == 4 else move_blocks
    return plan(cand_feats, cand_perm, w_in, *rest)


def solution(mesh):
    in_specs = (
        P("req", "mp"),
        P("req", None),
        P(None, None, "mp"),
        P("mp", None),
        P("req", None, "mp"),
        P("req", None, "mp"),
        P("req"),
        P(),
        P(),
        P("req", None, None),
    )
    out_specs = P("req", "mp")
    return jax.shard_map(local, mesh=mesh, in_specs=in_specs, out_specs=out_specs, check_vma=False)
```

```python
import functools

import jax
import jax.numpy as jnp
from jax import lax
from jax.experimental import pallas as pl
from jax.experimental.pallas import tpu as pltpu
from jax.sharding import PartitionSpec as P

HEADS = 8
DH = 128
BLK = 32
MAXBLK = 128
GROUP = 128


EPS = 1e-05


def move_blocks(
    cand_feats, cand_perm, w_in, w_out, cache_k, cache_v, hist_len, hist_home, hist_slot, hist_mask
):
    shards = lax.axis_size("req")
    own_index = lax.axis_index("req")
    columns = cand_feats.shape[1]
    cand_slot = cand_feats.shape[0] // shards
    arrived = lax.all_to_all(
        cand_feats.reshape(shards, cand_slot, columns),
        "req",
        split_axis=0,
        concat_axis=0,
        tiled=True,
    )
    arrived = arrived.reshape(shards * cand_slot, columns)
    own_rows = jnp.take(arrived, cand_perm[0], axis=0)
    full_rows = lax.all_gather(own_rows, "mp", axis=1, tiled=True)
    cand_count = full_rows.shape[0]
    features = full_rows.astype(jnp.float32)
    centred = features - jnp.mean(features, axis=1, keepdims=True)
    spread = jnp.mean(centred * centred, axis=1, keepdims=True)
    normed = (centred * lax.rsqrt(spread + EPS)).astype(jnp.bfloat16)
    local_width = w_in.shape[2]
    parts = jax.nn.silu(
        jnp.dot(
            normed, w_in.reshape(w_in.shape[0], 4 * local_width), preferred_element_type=jnp.float32
        )
    ).astype(jnp.bfloat16)
    parts = parts.reshape(cand_count, 4, local_width)
    gate_u, value_v, query_q, key_k = (parts[:, 0], parts[:, 1], parts[:, 2], parts[:, 3])
    rounds_here = MAXBLK // shards
    offsets = (own_index - hist_home) % shards
    wanted = offsets[:, None] + jnp.arange(rounds_here, dtype=jnp.int32)[None, :] * shards
    slots = jnp.take_along_axis(hist_slot, wanted, axis=1)
    send_keys = jnp.take(cache_k, slots, axis=0)
    send_values = jnp.take(cache_v, slots, axis=0)
    key_count = MAXBLK * BLK
    own_len = hist_len[0]
    got_keys, got_values = (
        lax.all_to_all(send_keys, "req", split_axis=0, concat_axis=0, tiled=True),
        lax.all_to_all(send_values, "req", split_axis=0, concat_axis=0, tiled=True),
    )
    live_keys = (jnp.arange(key_count, dtype=jnp.int32) < own_len).astype(jnp.float32)
    home_block = hist_home[own_index]
    block_order = jnp.arange(MAXBLK, dtype=jnp.int32)
    source = (home_block + block_order % shards) % shards
    round_at = block_order // shards
    hist_keys = got_keys[source, round_at].reshape(key_count, local_width)
    hist_values = got_values[source, round_at].reshape(key_count, local_width)
    block_mask = jnp.repeat(hist_mask[0].astype(jnp.float32), BLK, axis=1) * live_keys[None, :]
    score_scale = DH ** (-0.5)
    outputs = []
    for head_index in range(local_width // DH):
        lo_col = head_index * DH
        q_head = query_q[:, lo_col : lo_col + DH]
        scores = (
            lax.dot_general(
                q_head,
                hist_keys[:, lo_col : lo_col + DH],
                (((1,), (1,)), ((), ())),
                preferred_element_type=jnp.float32,
            )
            * score_scale
        )
        weights = (
            jax.nn.silu(scores).reshape(cand_count // GROUP, GROUP, key_count)
            * block_mask[:, None, :]
        )
        weights = weights.reshape(cand_count, key_count).astype(jnp.bfloat16)
        own_score = (
            jnp.sum(
                q_head.astype(jnp.float32) * key_k[:, lo_col : lo_col + DH].astype(jnp.float32),
                axis=1,
                keepdims=True,
            )
            * score_scale
        )
        own_term = jax.nn.silu(own_score) * value_v[:, lo_col : lo_col + DH].astype(jnp.float32)
        outputs.append(
            jnp.dot(
                weights, hist_values[:, lo_col : lo_col + DH], preferred_element_type=jnp.float32
            )
            + own_term
        )
    attn = jnp.concatenate(outputs, axis=1)
    width_all = HEADS * DH
    row_total = lax.psum(jnp.sum(attn, axis=1, keepdims=True), "mp")
    attn_mean = row_total / width_all
    attn_centred = attn - attn_mean
    square_total = lax.psum(jnp.sum(attn_centred * attn_centred, axis=1, keepdims=True), "mp")
    attn_spread = square_total / width_all
    hidden = (attn_centred * lax.rsqrt(attn_spread + EPS) * gate_u.astype(jnp.float32)).astype(
        jnp.bfloat16
    )
    mixed = lax.psum_scatter(
        lax.dot_general(
            w_out, hidden, (((0,), (1,)), ((), ())), preferred_element_type=jnp.float32
        ),
        "mp",
        scatter_dimension=0,
        tiled=True,
    ).T
    return (own_rows.astype(jnp.float32) + mixed).astype(jnp.bfloat16)


def remote(src, dst, send_sem, recv_sem, device):
    return pltpu.make_async_remote_copy(
        src_ref=src,
        dst_ref=dst,
        send_sem=send_sem,
        recv_sem=recv_sem,
        device_id=device,
        device_id_type=pl.DeviceIdType.MESH,
    )


def half_silu(half):
    return half + half * jnp.tanh(half)


SPAN = 128
TILE = 256


def kernel(
    shards,
    feats,
    perm,
    w_in_far,
    w_out,
    cache_k_far,
    cache_v_far,
    block_mask,
    length,
    home,
    slot,
    out,
    w_in,
    cache_k,
    cache_v,
    w_parts,
    counts,
    picked,
    rows_all,
    normed,
    own_rows,
    q_all,
    u_all,
    v_own,
    k_own,
    wo_all,
    other_k,
    other_v,
    counts_all,
    hist_k,
    hist_v,
    mask,
    part_out,
    part_in,
    part_own,
    total,
    attn_all,
    row_s,
    row_r,
    core_s,
    core_r,
    x_s,
    x_r,
    fwd_s,
    fwd_r,
    kv_s,
    kv_r,
    cnt_s,
    cnt_r,
    wo_s,
    wo_r,
    q_s,
    q_r,
    p_s,
    p_r,
    u_s,
    u_r,
    a_s,
    a_r,
    in_s,
):
    me = lax.axis_index("req")
    mp = lax.axis_index("mp")
    lines = shards // 2
    line, side = me // 2, me % 2
    lines_by_distance = (line, line + 1 - 2 * (line % 2), (line + 2) % 4, 3 - line)
    others = [(side + turn) % 2 + 2 * at for at in lines_by_distance for turn in range(2)][1:]
    mate = line * 2 + (1 - side)
    core_mp = (mp // 2) * 2 + (1 - mp % 2)
    x_mp = (1 - mp // 2) * 2 + mp % 2
    far_mp = (1 - mp // 2) * 2 + (1 - mp % 2)
    slots = feats.shape[1]
    width = feats.shape[2]
    cands = shards * slots
    groups, pieces = cands // GROUP, cands // SPAN
    rounds = MAXBLK // shards
    keys_here = rounds * BLK
    core, across, side_mate = (me, core_mp), (me, x_mp), (mate, mp)

    loads = [
        pltpu.make_async_copy(far, near, in_s.at[index])
        for index, (far, near) in enumerate(
            (
                (feats.at[me], rows_all.at[mp, pl.ds(me * slots, slots)]),
                (w_in_far, w_in),
                (cache_k_far, cache_k),
                (cache_v_far, cache_v),
                (w_out.at[:, pl.ds(pl.multiple_of(mp * width, width), width)], wo_all.at[mp]),
            )
        )
    ]
    for load in loads:
        load.start()

    barrier = pltpu.get_barrier_semaphore()
    for step in range(1, shards):
        pl.semaphore_signal(
            barrier, inc=1, device_id=((me + step) % shards, mp), device_id_type=pl.DeviceIdType.MESH
        )
    for step in range(1, 4):
        pl.semaphore_signal(
            barrier, inc=1, device_id=(me, (mp + step) % 4), device_id_type=pl.DeviceIdType.MESH
        )
    pl.semaphore_wait(barrier, shards + 2)

    def row_copy(source, target):
        return remote(
            feats.at[target],
            rows_all.at[mp, pl.ds(source * slots, slots)],
            row_s.at[target],
            row_r.at[source],
            (target, mp),
        )

    def count_copy(source, target):
        return remote(
            counts, counts_all.at[source], cnt_s.at[target], cnt_r.at[source], (target * 2 + side, mp)
        )

    def out_weight_copy(source, target):
        return remote(
            w_out.at[:, pl.ds(pl.multiple_of(target * width, width), width)],
            wo_all.at[source],
            wo_s.at[target],
            wo_r.at[source],
            (me, target),
        )

    def chunk(part, source):
        return rows_all.at[part, pl.ds(source * slots, slots)]

    def core_copy(source):
        return remote(chunk(mp, source), chunk(mp, source), core_s.at[source], core_r.at[source], core)

    def x_copy(source):
        return remote(chunk(mp, source), chunk(mp, source), x_s.at[source], x_r.at[source], across)

    def fwd_copy(source):
        return remote(chunk(x_mp, source), chunk(x_mp, source), fwd_s.at[source], fwd_r.at[source], core)

    def core_got(source):
        return remote(
            chunk(core_mp, source), chunk(core_mp, source), core_s.at[source], core_r.at[source], core
        )

    def x_got(source):
        return remote(chunk(x_mp, source), chunk(x_mp, source), x_s.at[source], x_r.at[source], across)

    def fwd_got(source):
        return remote(
            chunk(far_mp, source), chunk(far_mp, source), fwd_s.at[source], fwd_r.at[source], core
        )

    keys_copy = remote(cache_k_far, other_k, kv_s.at[0], kv_r.at[0], side_mate)
    values_copy = remote(cache_v_far, other_v, kv_s.at[1], kv_r.at[1], side_mate)

    for target in others[::-1]:
        row_copy(me, target).start()

    places = lax.broadcasted_iota(jnp.int32, (groups, MAXBLK), 1) * BLK
    counts[...] = jnp.zeros_like(counts)
    counts[0:groups, :] = (block_mask[0] * jnp.clip(length[0] - places, 0, BLK)).astype(jnp.float32)
    for step in range(1, lines):
        count_copy(line, (line + step) % lines).start()
    keys_copy.start()
    values_copy.start()
    loads[0].wait()
    counts_all[line] = counts[...]
    core_copy(me).start()
    x_copy(me).start()

    loads[1].wait()

    @pl.loop(0, w_in.shape[0], step=GROUP)
    def _(first):
        rows = pl.ds(pl.multiple_of(first, GROUP), GROUP)
        for part in range(4):
            w_parts[part, rows, :] = w_in[rows, part, :]

    for source in others:
        row_copy(source, me).wait_recv()
        core_copy(source).start()
        x_copy(source).start()

    for step in range(1, 4):
        out_weight_copy(mp, (mp + step) % 4).start()

    def gather(at, keys_ref, values_ref, shard, half):
        request = at * 2 + side
        first = lax.rem(shard - home[request] + shards, shards)
        for turn in range(rounds):
            place = slot[request, first + turn * shards]
            picked[turn * BLK : (turn + 1) * BLK, :] = keys_ref[place]
            begin = half * keys_here + turn * BLK
            hist_v[at, begin : begin + BLK, :] = values_ref[place]
        hist_k[at, :, half * keys_here : (half + 1) * keys_here] = jnp.transpose(picked[...])

    loads[2].wait()
    loads[3].wait()
    loads[4].wait()

    @pl.loop(0, lines)
    def _(at):
        gather(at, cache_k, cache_v, me, 0)

    for source in [me] + others:
        x_got(source).wait_recv()
        fwd_copy(source).start()

    for step in range(1, lines):
        count_copy((line + step) % lines, line).wait_recv()

    @pl.loop(0, lines)
    def _(at):
        request = at * 2 + side
        number = counts_all[at].astype(jnp.bfloat16)
        for half, shard in enumerate((me, mate)):
            first = lax.rem(shard - home[request] + shards, shards)
            key_at = lax.broadcasted_iota(jnp.int32, (MAXBLK, keys_here), 1)
            block_at = lax.broadcasted_iota(jnp.int32, (MAXBLK, keys_here), 0)
            spread = (block_at == first + (key_at // BLK) * shards).astype(jnp.float32)
            live = jnp.dot(number, spread.astype(jnp.bfloat16), preferred_element_type=jnp.float32)
            place = lax.broadcasted_iota(jnp.int32, live.shape, 1) % BLK
            mask[at, :, half * keys_here : (half + 1) * keys_here] = jnp.where(
                place.astype(jnp.float32) < live, 0.5 * DH ** (-0.5), 0.0
            )

    for source in [me] + others:
        core_got(source).wait_recv()
        fwd_got(source).wait_recv()


    def q_copy(source, device_line, piece, index):
        rows = pl.ds(piece * SPAN, SPAN)
        return remote(
            q_all.at[source, rows],
            q_all.at[source, rows],
            q_s.at[index * pieces + piece],
            q_r.at[source * pieces + piece],
            (device_line * 2 + side, mp),
        )

    below, above = line > 0, line < lines - 1

    def project(part, piece):
        rows = pl.ds(piece * SPAN, SPAN)
        scores = jnp.dot(normed[rows, :], w_parts[part], preferred_element_type=jnp.float32)
        return half_silu(0.5 * scores).astype(jnp.bfloat16)

    @pl.loop(0, pieces)
    def _(piece):
        rows = pl.ds(piece * SPAN, SPAN)
        wanted = perm[:, pl.ds(pl.multiple_of(piece * SPAN, SPAN), SPAN)]
        chosen = lax.broadcasted_iota(jnp.int32, (cands, SPAN), 0) == wanted
        pick = jnp.transpose(chosen.astype(jnp.float32)).astype(jnp.bfloat16)
        features = jnp.concatenate(
            [jnp.dot(pick, rows_all[part], preferred_element_type=jnp.float32) for part in range(4)],
            axis=1,
        )
        own_rows[rows, :] = jnp.dot(pick, rows_all[mp], preferred_element_type=jnp.float32)
        centred = features - jnp.mean(features, axis=1, keepdims=True)
        variance = jnp.mean(centred * centred, axis=1, keepdims=True)
        normed[rows, :] = (centred * lax.rsqrt(variance + EPS)).astype(jnp.bfloat16)
        q_all[line, rows, :] = project(2, piece)

        @pl.when(above)
        def _():
            q_copy(line, line + 1, piece, line).start()

        @pl.when(below)
        def _():
            q_copy(line, line - 1, piece, lines).start()

    @pl.loop(0, pieces)
    def _(piece):
        u_all[mp, pl.ds(piece * SPAN, SPAN), :] = project(0, piece)

    def part_copy(buffer, part, sems, index, device):
        send, receive = sems
        return remote(buffer.at[part], buffer.at[part], send.at[index], receive.at[index], device)

    u_sems = (u_s, u_r)
    part_copy(u_all, mp, u_sems, 0, core).start()
    part_copy(u_all, mp, u_sems, 1, across).start()

    @pl.loop(0, pieces)
    def _(piece):
        rows = pl.ds(piece * SPAN, SPAN)
        v_own[rows, :] = project(1, piece)
        k_own[rows, :] = project(3, piece)

    def attend(at, piece, half):
        rows = pl.ds(piece * SPAN, SPAN)
        heads = []
        for lo in range(0, width, DH):
            query = q_all[at, rows, lo : lo + DH]
            summed = None
            for first in range(half * keys_here, (half + 1) * keys_here, TILE):
                tile = slice(first, first + TILE)
                scores = jnp.dot(query, hist_k[at, lo : lo + DH, tile], preferred_element_type=jnp.float32)
                halves = [
                    scores[at_row : at_row + GROUP]
                    * mask[at, pl.ds(piece * (SPAN // GROUP) + at_row // GROUP, 1), tile]
                    for at_row in range(0, SPAN, GROUP)
                ]
                weights = half_silu(jnp.concatenate(halves, axis=0).astype(jnp.bfloat16))
                term = jnp.dot(
                    weights, hist_v[at, tile, lo : lo + DH], preferred_element_type=jnp.float32
                )
                summed = term if summed is None else summed + term
            heads.append(summed)
        return jnp.concatenate(heads, axis=1)

    def p_copy(target, nearer, place, piece):
        rows = pl.ds(piece * SPAN, SPAN)
        return remote(
            part_out.at[target, rows],
            part_in.at[place, rows],
            p_s.at[target * pieces + piece],
            p_r.at[place * pieces + piece],
            (nearer * 2 + side, mp),
        )

    def send_part(target, piece):
        rows = pl.ds(piece * SPAN, SPAN)

        @pl.when(target > line)
        def _():
            p_copy(target, line + 1, target, piece).start()

        @pl.when(target < line - 1)
        def _():
            p_copy(target, line - 1, target, piece).start()

        @pl.when(target == line - 1)
        def _():
            p_copy(target, line - 1, lines, piece).start()

    def visit(at, onward, piece):
        rows = pl.ds(piece * SPAN, SPAN)
        q_copy(at, line, piece, at).wait_recv()

        @pl.when((onward >= 0) & (onward < lines))
        def _():
            q_copy(at, onward, piece, at).start()

        part_own[at, rows, :] = attend(at, piece, 0)

    @pl.loop(0, pieces)
    def _(piece):
        rows = pl.ds(piece * SPAN, SPAN)
        own = []
        for lo in range(0, width, DH):
            query = q_all[line, rows, lo : lo + DH].astype(jnp.float32)
            key = k_own[rows, lo : lo + DH].astype(jnp.float32)
            half = jnp.sum(query * key, axis=1, keepdims=True) * (0.5 * DH ** (-0.5))
            own.append(half_silu(half) * v_own[rows, lo : lo + DH].astype(jnp.float32))
        total[rows, :] = attend(line, piece, 0) + jnp.concatenate(own, axis=1)

    mid = above & below

    def meet(distance):
        @pl.loop(0, pieces)
        def _(piece):
            @pl.when(line + distance < lines)
            def _():
                visit(line + distance, line - 1, piece)

            @pl.when(line - distance >= 0)
            def _():
                visit(line - distance, line + 1, piece)

    def complete(at):
        gather(at, other_k, other_v, mate, 1)

        @pl.loop(0, pieces)
        def _(piece):
            rows = pl.ds(piece * SPAN, SPAN)
            part_own[at, rows, :] += attend(at, piece, 1)

            @pl.when(mid)
            def _():
                p_copy(at, line, at, piece).wait_recv()
                part_own[at, rows, :] += part_in[at, rows, :].astype(jnp.float32)

            part_out[at, rows, :] = part_own[at, rows, :].astype(jnp.bfloat16)
            send_part(at, piece)

    def complete_own():
        gather(line, other_k, other_v, mate, 1)

        @pl.loop(0, pieces)
        def _(piece):
            total[pl.ds(piece * SPAN, SPAN), :] += attend(line, piece, 1)

    meet(1)
    meet(2)
    part_copy(u_all, x_mp, u_sems, 1, across).wait_recv()
    part_copy(u_all, x_mp, u_sems, 2, core).start()
    keys_copy.wait_recv()
    values_copy.wait_recv()
    low = line < 2

    @pl.when(mid)
    def _():
        complete_own()

    complete(jnp.where(low, line + 1, line - 1))
    complete(jnp.where(low, line + 2, line - 2))
    meet(3)
    complete(jnp.where(mid, 3 * (line - 1), 3 - line))

    @pl.when(jnp.logical_not(mid))
    def _():
        complete_own()

    part_copy(u_all, core_mp, u_sems, 0, core).wait_recv()
    part_copy(u_all, far_mp, u_sems, 2, core).wait_recv()
    for step in range(1, 4):
        out_weight_copy((mp + step) % 4, mp).wait_recv()

    def attn_copy(part, kind, piece, device):
        block = attn_all.at[part, pl.ds(piece * SPAN, SPAN)]
        index = kind * pieces + piece
        return remote(block, block, a_s.at[index], a_r.at[index], device)

    def collect(piece):
        rows = pl.ds(piece * SPAN, SPAN)

        @pl.when(below)
        def _():
            p_copy(line, line, line, piece).wait_recv()
            total[rows, :] += part_in[line, rows, :].astype(jnp.float32)

        @pl.when(above)
        def _():
            p_copy(line, line, lines, piece).wait_recv()
            total[rows, :] += part_in[lines, rows, :].astype(jnp.float32)

        attn_all[mp, rows, :] = total[rows, :].astype(jnp.bfloat16)
        attn_copy(mp, 0, piece, core).start()
        attn_copy(mp, 1, piece, across).start()

    def pass_on(piece):
        attn_copy(x_mp, 1, piece, across).wait_recv()
        attn_copy(x_mp, 2, piece, core).start()

    def finish(piece):
        rows = pl.ds(piece * SPAN, SPAN)
        attn_copy(core_mp, 0, piece, core).wait_recv()
        attn_copy(far_mp, 2, piece, core).wait_recv()
        attn = jnp.concatenate([attn_all[part, rows, :].astype(jnp.float32) for part in range(4)], axis=1)
        gate = jnp.concatenate([u_all[part, rows, :].astype(jnp.float32) for part in range(4)], axis=1)
        centred = attn - jnp.mean(attn, axis=1, keepdims=True)
        variance = jnp.mean(centred * centred, axis=1, keepdims=True)
        hidden = (centred * lax.rsqrt(variance + EPS) * gate).astype(jnp.bfloat16)
        mixed = own_rows[rows, :]
        for part in range(4):
            mixed = mixed + jnp.dot(
                hidden[:, part * width : (part + 1) * width],
                wo_all[part],
                preferred_element_type=jnp.float32,
            )
        out[rows, :] = mixed.astype(jnp.bfloat16)

    @pl.loop(0, pieces + 2)
    def _(turn):
        @pl.when(turn < pieces)
        def _():
            collect(turn)

        @pl.when((turn >= 1) & (turn < pieces + 1))
        def _():
            pass_on(turn - 1)

        @pl.when(turn >= 2)
        def _():
            finish(turn - 2)

    for target in others:
        row_copy(me, target).wait_send()

    @pl.loop(0, shards)
    def _(source):
        core_copy(source).wait_send()
        x_copy(source).wait_send()
        fwd_copy(source).wait_send()

    keys_copy.wait_send()
    values_copy.wait_send()
    for step in range(1, lines):
        count_copy(line, (line + step) % lines).wait_send()
    for step in range(1, 4):
        out_weight_copy(mp, (mp + step) % 4).wait_send()
    part_copy(u_all, mp, u_sems, 0, core).wait_send()
    part_copy(u_all, mp, u_sems, 1, across).wait_send()
    part_copy(u_all, x_mp, u_sems, 2, core).wait_send()

    @pl.loop(0, pieces)
    def _(piece):
        for step in range(1, lines):
            at = (line + step) % lines
            p_copy(at, line, at, piece).wait_send()

            @pl.when(jnp.where(at > line, below, above))
            def _():
                q_copy(at, line, piece, at).wait_send()

        @pl.when(above)
        def _():
            q_copy(line, line, piece, line).wait_send()

        @pl.when(below)
        def _():
            q_copy(line, line, piece, lines).wait_send()

        attn_copy(mp, 0, piece, core).wait_send()
        attn_copy(mp, 1, piece, across).wait_send()
        attn_copy(x_mp, 2, piece, core).wait_send()


def move_queries(
    cand_feats, cand_perm, w_in, w_out, cache_k, cache_v, hist_len, hist_home, hist_slot, hist_mask
):
    shards = lax.axis_size("req")
    cands, width = cand_feats.shape
    full = w_in.shape[0]
    lines = shards // 2
    pieces = cands // SPAN
    keys = 2 * (MAXBLK // shards) * BLK
    bf16, f32 = jnp.bfloat16, jnp.float32
    vmem = pl.BlockSpec(memory_space=pltpu.VMEM)
    smem = pl.BlockSpec(memory_space=pltpu.SMEM)
    far = pl.BlockSpec(memory_space=pl.ANY)
    lots = (lines + 1) * pieces
    pairs = [shards, shards, shards, shards, 2, lines, 4, lots, lots, 3, 3 * pieces]
    return pl.pallas_call(
        functools.partial(kernel, shards),
        out_shape=jax.ShapeDtypeStruct((cands, width), bf16),
        in_specs=[far, vmem] + [far] * 4 + [vmem] + [smem] * 3,
        out_specs=vmem,
        scratch_shapes=[
            pltpu.VMEM(w_in.shape, bf16),
            pltpu.VMEM(cache_k.shape, bf16),
            pltpu.VMEM(cache_v.shape, bf16),
            pltpu.VMEM((4, full, width), bf16),
            pltpu.VMEM((8, MAXBLK), f32),
            pltpu.VMEM((keys // 2, width), bf16),
            pltpu.VMEM((4, cands, width), bf16),
            pltpu.VMEM((cands, full), bf16),
            pltpu.VMEM((cands, width), f32),
            pltpu.VMEM((lines, cands, width), bf16),
            pltpu.VMEM((4, cands, width), bf16),
            pltpu.VMEM((cands, width), bf16),
            pltpu.VMEM((cands, width), bf16),
            pltpu.VMEM((4, width, width), bf16),
            pltpu.VMEM(cache_k.shape, bf16),
            pltpu.VMEM(cache_v.shape, bf16),
            pltpu.VMEM((lines, 8, MAXBLK), f32),
            pltpu.VMEM((lines, width, keys), bf16),
            pltpu.VMEM((lines, keys, width), bf16),
            pltpu.VMEM((lines, 8, keys), f32),
            pltpu.VMEM((lines, cands, width), bf16),
            pltpu.VMEM((lines + 1, cands, width), bf16),
            pltpu.VMEM((lines, cands, width), f32),
            pltpu.VMEM((cands, width), f32),
            pltpu.VMEM((4, cands, width), bf16),
        ]
        + [pltpu.SemaphoreType.DMA((count,)) for count in pairs for _ in range(2)]
        + [pltpu.SemaphoreType.DMA((5,))],
        compiler_params=pltpu.CompilerParams(
            collective_id=0, has_side_effects=True, vmem_limit_bytes=56 * 1024 * 1024
        ),
        cost_estimate=pl.CostEstimate(flops=8 * 10**9, bytes_accessed=2**23, transcendentals=2**22),
    )(
        cand_feats.reshape(shards, cands // shards, width),
        cand_perm,
        w_in,
        w_out,
        cache_k,
        cache_v,
        hist_mask,
        hist_len,
        hist_home,
        hist_slot,
    )


def local(cand_feats, cand_perm, w_in, *rest):
    shards = lax.axis_size("req")
    shard_keys = MAXBLK // shards * BLK
    queries_fit = cand_perm.shape[1] <= shard_keys and shards == 8
    plan = move_queries if queries_fit and lax.axis_size("mp") == 4 else move_blocks
    return plan(cand_feats, cand_perm, w_in, *rest)


def solution(mesh):
    in_specs = (
        P("req", "mp"),
        P("req", None),
        P(None, None, "mp"),
        P("mp", None),
        P("req", None, "mp"),
        P("req", None, "mp"),
        P("req"),
        P(),
        P(),
        P("req", None, None),
    )
    out_specs = P("req", "mp")
    return jax.shard_map(local, mesh=mesh, in_specs=in_specs, out_specs=out_specs, check_vma=False)
```

```python
import functools

import jax
import jax.numpy as jnp
from jax import lax
from jax.experimental import pallas as pl
from jax.experimental.pallas import tpu as pltpu
from jax.sharding import PartitionSpec as P

HEADS = 8
DH = 128
BLK = 32
MAXBLK = 128
GROUP = 128


EPS = 1e-05


def move_blocks(
    cand_feats, cand_perm, w_in, w_out, cache_k, cache_v, hist_len, hist_home, hist_slot, hist_mask
):
    shards = lax.axis_size("req")
    own_index = lax.axis_index("req")
    columns = cand_feats.shape[1]
    cand_slot = cand_feats.shape[0] // shards
    arrived = lax.all_to_all(
        cand_feats.reshape(shards, cand_slot, columns),
        "req",
        split_axis=0,
        concat_axis=0,
        tiled=True,
    )
    arrived = arrived.reshape(shards * cand_slot, columns)
    own_rows = jnp.take(arrived, cand_perm[0], axis=0)
    full_rows = lax.all_gather(own_rows, "mp", axis=1, tiled=True)
    cand_count = full_rows.shape[0]
    features = full_rows.astype(jnp.float32)
    centred = features - jnp.mean(features, axis=1, keepdims=True)
    spread = jnp.mean(centred * centred, axis=1, keepdims=True)
    normed = (centred * lax.rsqrt(spread + EPS)).astype(jnp.bfloat16)
    local_width = w_in.shape[2]
    parts = jax.nn.silu(
        jnp.dot(
            normed, w_in.reshape(w_in.shape[0], 4 * local_width), preferred_element_type=jnp.float32
        )
    ).astype(jnp.bfloat16)
    parts = parts.reshape(cand_count, 4, local_width)
    gate_u, value_v, query_q, key_k = (parts[:, 0], parts[:, 1], parts[:, 2], parts[:, 3])
    rounds_here = MAXBLK // shards
    offsets = (own_index - hist_home) % shards
    wanted = offsets[:, None] + jnp.arange(rounds_here, dtype=jnp.int32)[None, :] * shards
    slots = jnp.take_along_axis(hist_slot, wanted, axis=1)
    send_keys = jnp.take(cache_k, slots, axis=0)
    send_values = jnp.take(cache_v, slots, axis=0)
    key_count = MAXBLK * BLK
    own_len = hist_len[0]
    got_keys, got_values = (
        lax.all_to_all(send_keys, "req", split_axis=0, concat_axis=0, tiled=True),
        lax.all_to_all(send_values, "req", split_axis=0, concat_axis=0, tiled=True),
    )
    live_keys = (jnp.arange(key_count, dtype=jnp.int32) < own_len).astype(jnp.float32)
    home_block = hist_home[own_index]
    block_order = jnp.arange(MAXBLK, dtype=jnp.int32)
    source = (home_block + block_order % shards) % shards
    round_at = block_order // shards
    hist_keys = got_keys[source, round_at].reshape(key_count, local_width)
    hist_values = got_values[source, round_at].reshape(key_count, local_width)
    block_mask = jnp.repeat(hist_mask[0].astype(jnp.float32), BLK, axis=1) * live_keys[None, :]
    score_scale = DH ** (-0.5)
    outputs = []
    for head_index in range(local_width // DH):
        lo_col = head_index * DH
        q_head = query_q[:, lo_col : lo_col + DH]
        scores = (
            lax.dot_general(
                q_head,
                hist_keys[:, lo_col : lo_col + DH],
                (((1,), (1,)), ((), ())),
                preferred_element_type=jnp.float32,
            )
            * score_scale
        )
        weights = (
            jax.nn.silu(scores).reshape(cand_count // GROUP, GROUP, key_count)
            * block_mask[:, None, :]
        )
        weights = weights.reshape(cand_count, key_count).astype(jnp.bfloat16)
        own_score = (
            jnp.sum(
                q_head.astype(jnp.float32) * key_k[:, lo_col : lo_col + DH].astype(jnp.float32),
                axis=1,
                keepdims=True,
            )
            * score_scale
        )
        own_term = jax.nn.silu(own_score) * value_v[:, lo_col : lo_col + DH].astype(jnp.float32)
        outputs.append(
            jnp.dot(
                weights, hist_values[:, lo_col : lo_col + DH], preferred_element_type=jnp.float32
            )
            + own_term
        )
    attn = jnp.concatenate(outputs, axis=1)
    width_all = HEADS * DH
    row_total = lax.psum(jnp.sum(attn, axis=1, keepdims=True), "mp")
    attn_mean = row_total / width_all
    attn_centred = attn - attn_mean
    square_total = lax.psum(jnp.sum(attn_centred * attn_centred, axis=1, keepdims=True), "mp")
    attn_spread = square_total / width_all
    hidden = (attn_centred * lax.rsqrt(attn_spread + EPS) * gate_u.astype(jnp.float32)).astype(
        jnp.bfloat16
    )
    mixed = lax.psum_scatter(
        lax.dot_general(
            w_out, hidden, (((0,), (1,)), ((), ())), preferred_element_type=jnp.float32
        ),
        "mp",
        scatter_dimension=0,
        tiled=True,
    ).T
    return (own_rows.astype(jnp.float32) + mixed).astype(jnp.bfloat16)


def remote(src, dst, send_sem, recv_sem, device):
    return pltpu.make_async_remote_copy(
        src_ref=src,
        dst_ref=dst,
        send_sem=send_sem,
        recv_sem=recv_sem,
        device_id=device,
        device_id_type=pl.DeviceIdType.MESH,
    )


def half_silu(half):
    return half + half * jnp.tanh(half)


SPAN = 256
TILE = 256


def kernel(
    shards,
    feats,
    perm,
    w_in_far,
    w_out,
    cache_k_far,
    cache_v_far,
    block_mask,
    length,
    home,
    slot,
    out,
    w_in,
    cache_k,
    cache_v,
    w_parts,
    counts,
    picked,
    rows_all,
    normed,
    own_rows,
    q_all,
    u_all,
    v_own,
    k_own,
    wo_all,
    other_k,
    other_v,
    counts_all,
    hist_k,
    hist_v,
    mask,
    part_out,
    part_in,
    part_own,
    total,
    attn_all,
    row_s,
    row_r,
    core_s,
    core_r,
    x_s,
    x_r,
    fwd_s,
    fwd_r,
    kv_s,
    kv_r,
    cnt_s,
    cnt_r,
    wo_s,
    wo_r,
    q_s,
    q_r,
    p_s,
    p_r,
    u_s,
    u_r,
    a_s,
    a_r,
    in_s,
):
    me = lax.axis_index("req")
    mp = lax.axis_index("mp")
    lines = shards // 2
    line, side = me // 2, me % 2
    lines_by_distance = (line, line + 1 - 2 * (line % 2), (line + 2) % 4, 3 - line)
    others = [(side + turn) % 2 + 2 * at for at in lines_by_distance for turn in range(2)][1:]
    mate = line * 2 + (1 - side)
    core_mp = (mp // 2) * 2 + (1 - mp % 2)
    x_mp = (1 - mp // 2) * 2 + mp % 2
    far_mp = (1 - mp // 2) * 2 + (1 - mp % 2)
    slots = feats.shape[1]
    width = feats.shape[2]
    cands = shards * slots
    groups, pieces = cands // GROUP, cands // SPAN
    rounds = MAXBLK // shards
    keys_here = rounds * BLK
    core, across, side_mate = (me, core_mp), (me, x_mp), (mate, mp)

    loads = [
        pltpu.make_async_copy(far, near, in_s.at[index])
        for index, (far, near) in enumerate(
            (
                (feats.at[me], rows_all.at[mp, pl.ds(me * slots, slots)]),
                (w_in_far, w_in),
                (cache_k_far, cache_k),
                (cache_v_far, cache_v),
                (w_out.at[:, pl.ds(pl.multiple_of(mp * width, width), width)], wo_all.at[mp]),
            )
        )
    ]
    for load in loads:
        load.start()

    barrier = pltpu.get_barrier_semaphore()
    for step in range(1, shards):
        pl.semaphore_signal(
            barrier, inc=1, device_id=((me + step) % shards, mp), device_id_type=pl.DeviceIdType.MESH
        )
    for step in range(1, 4):
        pl.semaphore_signal(
            barrier, inc=1, device_id=(me, (mp + step) % 4), device_id_type=pl.DeviceIdType.MESH
        )
    pl.semaphore_wait(barrier, shards + 2)

    def row_copy(source, target):
        return remote(
            feats.at[target],
            rows_all.at[mp, pl.ds(source * slots, slots)],
            row_s.at[target],
            row_r.at[source],
            (target, mp),
        )

    def count_copy(source, target):
        return remote(
            counts, counts_all.at[source], cnt_s.at[target], cnt_r.at[source], (target * 2 + side, mp)
        )

    def out_weight_copy(source, target):
        return remote(
            w_out.at[:, pl.ds(pl.multiple_of(target * width, width), width)],
            wo_all.at[source],
            wo_s.at[target],
            wo_r.at[source],
            (me, target),
        )

    def chunk(part, source):
        return rows_all.at[part, pl.ds(source * slots, slots)]

    def core_copy(source):
        return remote(chunk(mp, source), chunk(mp, source), core_s.at[source], core_r.at[source], core)

    def x_copy(source):
        return remote(chunk(mp, source), chunk(mp, source), x_s.at[source], x_r.at[source], across)

    def fwd_copy(source):
        return remote(chunk(x_mp, source), chunk(x_mp, source), fwd_s.at[source], fwd_r.at[source], core)

    def core_got(source):
        return remote(
            chunk(core_mp, source), chunk(core_mp, source), core_s.at[source], core_r.at[source], core
        )

    def x_got(source):
        return remote(chunk(x_mp, source), chunk(x_mp, source), x_s.at[source], x_r.at[source], across)

    def fwd_got(source):
        return remote(
            chunk(far_mp, source), chunk(far_mp, source), fwd_s.at[source], fwd_r.at[source], core
        )

    keys_copy = remote(cache_k_far, other_k, kv_s.at[0], kv_r.at[0], side_mate)
    values_copy = remote(cache_v_far, other_v, kv_s.at[1], kv_r.at[1], side_mate)

    for target in others[::-1]:
        row_copy(me, target).start()

    places = lax.broadcasted_iota(jnp.int32, (groups, MAXBLK), 1) * BLK
    counts[...] = jnp.zeros_like(counts)
    counts[0:groups, :] = (block_mask[0] * jnp.clip(length[0] - places, 0, BLK)).astype(jnp.float32)
    for step in range(1, lines):
        count_copy(line, (line + step) % lines).start()
    keys_copy.start()
    values_copy.start()
    loads[0].wait()
    counts_all[line] = counts[...]
    core_copy(me).start()
    x_copy(me).start()

    loads[1].wait()

    @pl.loop(0, w_in.shape[0], step=GROUP)
    def _(first):
        rows = pl.ds(pl.multiple_of(first, GROUP), GROUP)
        for part in range(4):
            w_parts[part, rows, :] = w_in[rows, part, :]

    for source in others:
        row_copy(source, me).wait_recv()
        core_copy(source).start()
        x_copy(source).start()

    for step in range(1, 4):
        out_weight_copy(mp, (mp + step) % 4).start()

    def gather(at, keys_ref, values_ref, shard, half):
        request = at * 2 + side
        first = lax.rem(shard - home[request] + shards, shards)
        for turn in range(rounds):
            place = slot[request, first + turn * shards]
            picked[turn * BLK : (turn + 1) * BLK, :] = keys_ref[place]
            begin = half * keys_here + turn * BLK
            hist_v[at, begin : begin + BLK, :] = values_ref[place]
        hist_k[at, :, half * keys_here : (half + 1) * keys_here] = jnp.transpose(picked[...])

    loads[2].wait()
    loads[3].wait()
    loads[4].wait()

    @pl.loop(0, lines)
    def _(at):
        gather(at, cache_k, cache_v, me, 0)

    for source in [me] + others:
        x_got(source).wait_recv()
        fwd_copy(source).start()

    for step in range(1, lines):
        count_copy((line + step) % lines, line).wait_recv()

    @pl.loop(0, lines)
    def _(at):
        request = at * 2 + side
        number = counts_all[at].astype(jnp.bfloat16)
        for half, shard in enumerate((me, mate)):
            first = lax.rem(shard - home[request] + shards, shards)
            key_at = lax.broadcasted_iota(jnp.int32, (MAXBLK, keys_here), 1)
            block_at = lax.broadcasted_iota(jnp.int32, (MAXBLK, keys_here), 0)
            spread = (block_at == first + (key_at // BLK) * shards).astype(jnp.float32)
            live = jnp.dot(number, spread.astype(jnp.bfloat16), preferred_element_type=jnp.float32)
            place = lax.broadcasted_iota(jnp.int32, live.shape, 1) % BLK
            mask[at, :, half * keys_here : (half + 1) * keys_here] = jnp.where(
                place.astype(jnp.float32) < live, 0.5 * DH ** (-0.5), 0.0
            )

    for source in [me] + others:
        core_got(source).wait_recv()
        fwd_got(source).wait_recv()


    def q_copy(source, device_line, piece, index):
        rows = pl.ds(piece * SPAN, SPAN)
        return remote(
            q_all.at[source, rows],
            q_all.at[source, rows],
            q_s.at[index * pieces + piece],
            q_r.at[source * pieces + piece],
            (device_line * 2 + side, mp),
        )

    below, above = line > 0, line < lines - 1

    def project(part, piece):
        rows = pl.ds(piece * SPAN, SPAN)
        scores = jnp.dot(normed[rows, :], w_parts[part], preferred_element_type=jnp.float32)
        return half_silu(0.5 * scores).astype(jnp.bfloat16)

    @pl.loop(0, pieces)
    def _(piece):
        rows = pl.ds(piece * SPAN, SPAN)
        wanted = perm[:, pl.ds(pl.multiple_of(piece * SPAN, SPAN), SPAN)]
        chosen = lax.broadcasted_iota(jnp.int32, (cands, SPAN), 0) == wanted
        pick = jnp.transpose(chosen.astype(jnp.float32)).astype(jnp.bfloat16)
        features = jnp.concatenate(
            [jnp.dot(pick, rows_all[part], preferred_element_type=jnp.float32) for part in range(4)],
            axis=1,
        )
        own_rows[rows, :] = jnp.dot(pick, rows_all[mp], preferred_element_type=jnp.float32)
        centred = features - jnp.mean(features, axis=1, keepdims=True)
        variance = jnp.mean(centred * centred, axis=1, keepdims=True)
        normed[rows, :] = (centred * lax.rsqrt(variance + EPS)).astype(jnp.bfloat16)
        q_all[line, rows, :] = project(2, piece)

        @pl.when(above)
        def _():
            q_copy(line, line + 1, piece, line).start()

        @pl.when(below)
        def _():
            q_copy(line, line - 1, piece, lines).start()

    @pl.loop(0, pieces)
    def _(piece):
        u_all[mp, pl.ds(piece * SPAN, SPAN), :] = project(0, piece)

    def part_copy(buffer, part, sems, index, device):
        send, receive = sems
        return remote(buffer.at[part], buffer.at[part], send.at[index], receive.at[index], device)

    u_sems = (u_s, u_r)
    part_copy(u_all, mp, u_sems, 0, core).start()
    part_copy(u_all, mp, u_sems, 1, across).start()

    @pl.loop(0, pieces)
    def _(piece):
        rows = pl.ds(piece * SPAN, SPAN)
        v_own[rows, :] = project(1, piece)
        k_own[rows, :] = project(3, piece)

    def attend(at, piece, half):
        rows = pl.ds(piece * SPAN, SPAN)
        heads = []
        for lo in range(0, width, DH):
            query = q_all[at, rows, lo : lo + DH]
            summed = None
            for first in range(half * keys_here, (half + 1) * keys_here, TILE):
                tile = slice(first, first + TILE)
                scores = jnp.dot(query, hist_k[at, lo : lo + DH, tile], preferred_element_type=jnp.float32)
                halves = [
                    scores[at_row : at_row + GROUP]
                    * mask[at, pl.ds(piece * (SPAN // GROUP) + at_row // GROUP, 1), tile]
                    for at_row in range(0, SPAN, GROUP)
                ]
                weights = half_silu(jnp.concatenate(halves, axis=0).astype(jnp.bfloat16))
                term = jnp.dot(
                    weights, hist_v[at, tile, lo : lo + DH], preferred_element_type=jnp.float32
                )
                summed = term if summed is None else summed + term
            heads.append(summed)
        return jnp.concatenate(heads, axis=1)

    def p_copy(target, nearer, place, piece):
        rows = pl.ds(piece * SPAN, SPAN)
        return remote(
            part_out.at[target, rows],
            part_in.at[place, rows],
            p_s.at[target * pieces + piece],
            p_r.at[place * pieces + piece],
            (nearer * 2 + side, mp),
        )

    def send_part(target, piece):
        rows = pl.ds(piece * SPAN, SPAN)

        @pl.when(target > line)
        def _():
            p_copy(target, line + 1, target, piece).start()

        @pl.when(target < line - 1)
        def _():
            p_copy(target, line - 1, target, piece).start()

        @pl.when(target == line - 1)
        def _():
            p_copy(target, line - 1, lines, piece).start()

    def visit(at, onward, piece):
        rows = pl.ds(piece * SPAN, SPAN)
        q_copy(at, line, piece, at).wait_recv()

        @pl.when((onward >= 0) & (onward < lines))
        def _():
            q_copy(at, onward, piece, at).start()

        part_own[at, rows, :] = attend(at, piece, 0)

    @pl.loop(0, pieces)
    def _(piece):
        rows = pl.ds(piece * SPAN, SPAN)
        own = []
        for lo in range(0, width, DH):
            query = q_all[line, rows, lo : lo + DH].astype(jnp.float32)
            key = k_own[rows, lo : lo + DH].astype(jnp.float32)
            half = jnp.sum(query * key, axis=1, keepdims=True) * (0.5 * DH ** (-0.5))
            own.append(half_silu(half) * v_own[rows, lo : lo + DH].astype(jnp.float32))
        total[rows, :] = attend(line, piece, 0) + jnp.concatenate(own, axis=1)

    mid = above & below

    def meet(distance):
        @pl.loop(0, pieces)
        def _(piece):
            @pl.when(line + distance < lines)
            def _():
                visit(line + distance, line - 1, piece)

            @pl.when(line - distance >= 0)
            def _():
                visit(line - distance, line + 1, piece)

    def complete(at):
        gather(at, other_k, other_v, mate, 1)

        @pl.loop(0, pieces)
        def _(piece):
            rows = pl.ds(piece * SPAN, SPAN)
            part_own[at, rows, :] += attend(at, piece, 1)

            @pl.when(mid)
            def _():
                p_copy(at, line, at, piece).wait_recv()
                part_own[at, rows, :] += part_in[at, rows, :].astype(jnp.float32)

            part_out[at, rows, :] = part_own[at, rows, :].astype(jnp.bfloat16)
            send_part(at, piece)

    def complete_own():
        gather(line, other_k, other_v, mate, 1)

        @pl.loop(0, pieces)
        def _(piece):
            total[pl.ds(piece * SPAN, SPAN), :] += attend(line, piece, 1)

    meet(1)
    meet(2)
    part_copy(u_all, x_mp, u_sems, 1, across).wait_recv()
    part_copy(u_all, x_mp, u_sems, 2, core).start()
    keys_copy.wait_recv()
    values_copy.wait_recv()
    low = line < 2

    @pl.when(mid)
    def _():
        complete_own()

    complete(jnp.where(low, line + 1, line - 1))
    complete(jnp.where(low, line + 2, line - 2))
    meet(3)
    complete(jnp.where(mid, 3 * (line - 1), 3 - line))

    @pl.when(jnp.logical_not(mid))
    def _():
        complete_own()

    part_copy(u_all, core_mp, u_sems, 0, core).wait_recv()
    part_copy(u_all, far_mp, u_sems, 2, core).wait_recv()
    for step in range(1, 4):
        out_weight_copy((mp + step) % 4, mp).wait_recv()

    def attn_copy(part, kind, piece, device):
        block = attn_all.at[part, pl.ds(piece * SPAN, SPAN)]
        index = kind * pieces + piece
        return remote(block, block, a_s.at[index], a_r.at[index], device)

    def collect(piece):
        rows = pl.ds(piece * SPAN, SPAN)

        @pl.when(below)
        def _():
            p_copy(line, line, line, piece).wait_recv()
            total[rows, :] += part_in[line, rows, :].astype(jnp.float32)

        @pl.when(above)
        def _():
            p_copy(line, line, lines, piece).wait_recv()
            total[rows, :] += part_in[lines, rows, :].astype(jnp.float32)

        attn_all[mp, rows, :] = total[rows, :].astype(jnp.bfloat16)
        attn_copy(mp, 0, piece, core).start()
        attn_copy(mp, 1, piece, across).start()

    def pass_on(piece):
        attn_copy(x_mp, 1, piece, across).wait_recv()
        attn_copy(x_mp, 2, piece, core).start()

    def finish(piece):
        rows = pl.ds(piece * SPAN, SPAN)
        attn_copy(core_mp, 0, piece, core).wait_recv()
        attn_copy(far_mp, 2, piece, core).wait_recv()
        attn = jnp.concatenate([attn_all[part, rows, :].astype(jnp.float32) for part in range(4)], axis=1)
        gate = jnp.concatenate([u_all[part, rows, :].astype(jnp.float32) for part in range(4)], axis=1)
        centred = attn - jnp.mean(attn, axis=1, keepdims=True)
        variance = jnp.mean(centred * centred, axis=1, keepdims=True)
        hidden = (centred * lax.rsqrt(variance + EPS) * gate).astype(jnp.bfloat16)
        mixed = own_rows[rows, :]
        for part in range(4):
            mixed = mixed + jnp.dot(
                hidden[:, part * width : (part + 1) * width],
                wo_all[part],
                preferred_element_type=jnp.float32,
            )
        out[rows, :] = mixed.astype(jnp.bfloat16)

    @pl.loop(0, pieces + 2)
    def _(turn):
        @pl.when(turn < pieces)
        def _():
            collect(turn)

        @pl.when((turn >= 1) & (turn < pieces + 1))
        def _():
            pass_on(turn - 1)

        @pl.when(turn >= 2)
        def _():
            finish(turn - 2)

    for target in others:
        row_copy(me, target).wait_send()

    @pl.loop(0, shards)
    def _(source):
        core_copy(source).wait_send()
        x_copy(source).wait_send()
        fwd_copy(source).wait_send()

    keys_copy.wait_send()
    values_copy.wait_send()
    for step in range(1, lines):
        count_copy(line, (line + step) % lines).wait_send()
    for step in range(1, 4):
        out_weight_copy(mp, (mp + step) % 4).wait_send()
    part_copy(u_all, mp, u_sems, 0, core).wait_send()
    part_copy(u_all, mp, u_sems, 1, across).wait_send()
    part_copy(u_all, x_mp, u_sems, 2, core).wait_send()

    @pl.loop(0, pieces)
    def _(piece):
        for step in range(1, lines):
            at = (line + step) % lines
            p_copy(at, line, at, piece).wait_send()

            @pl.when(jnp.where(at > line, below, above))
            def _():
                q_copy(at, line, piece, at).wait_send()

        @pl.when(above)
        def _():
            q_copy(line, line, piece, line).wait_send()

        @pl.when(below)
        def _():
            q_copy(line, line, piece, lines).wait_send()

        attn_copy(mp, 0, piece, core).wait_send()
        attn_copy(mp, 1, piece, across).wait_send()
        attn_copy(x_mp, 2, piece, core).wait_send()


def move_queries(
    cand_feats, cand_perm, w_in, w_out, cache_k, cache_v, hist_len, hist_home, hist_slot, hist_mask
):
    shards = lax.axis_size("req")
    cands, width = cand_feats.shape
    full = w_in.shape[0]
    lines = shards // 2
    pieces = cands // SPAN
    keys = 2 * (MAXBLK // shards) * BLK
    bf16, f32 = jnp.bfloat16, jnp.float32
    vmem = pl.BlockSpec(memory_space=pltpu.VMEM)
    smem = pl.BlockSpec(memory_space=pltpu.SMEM)
    far = pl.BlockSpec(memory_space=pltpu.HBM)
    lots = (lines + 1) * pieces
    pairs = [shards, shards, shards, shards, 2, lines, 4, lots, lots, 3, 3 * pieces]
    return pl.pallas_call(
        functools.partial(kernel, shards),
        out_shape=jax.ShapeDtypeStruct((cands, width), bf16),
        in_specs=[far, vmem] + [far] * 4 + [vmem] + [smem] * 3,
        out_specs=vmem,
        scratch_shapes=[
            pltpu.VMEM(w_in.shape, bf16),
            pltpu.VMEM(cache_k.shape, bf16),
            pltpu.VMEM(cache_v.shape, bf16),
            pltpu.VMEM((4, full, width), bf16),
            pltpu.VMEM((8, MAXBLK), f32),
            pltpu.VMEM((keys // 2, width), bf16),
            pltpu.VMEM((4, cands, width), bf16),
            pltpu.VMEM((cands, full), bf16),
            pltpu.VMEM((cands, width), f32),
            pltpu.VMEM((lines, cands, width), bf16),
            pltpu.VMEM((4, cands, width), bf16),
            pltpu.VMEM((cands, width), bf16),
            pltpu.VMEM((cands, width), bf16),
            pltpu.VMEM((4, width, width), bf16),
            pltpu.VMEM(cache_k.shape, bf16),
            pltpu.VMEM(cache_v.shape, bf16),
            pltpu.VMEM((lines, 8, MAXBLK), f32),
            pltpu.VMEM((lines, width, keys), bf16),
            pltpu.VMEM((lines, keys, width), bf16),
            pltpu.VMEM((lines, 8, keys), f32),
            pltpu.VMEM((lines, cands, width), bf16),
            pltpu.VMEM((lines + 1, cands, width), bf16),
            pltpu.VMEM((lines, cands, width), f32),
            pltpu.VMEM((cands, width), f32),
            pltpu.VMEM((4, cands, width), bf16),
        ]
        + [pltpu.SemaphoreType.DMA((count,)) for count in pairs for _ in range(2)]
        + [pltpu.SemaphoreType.DMA((5,))],
        compiler_params=pltpu.CompilerParams(
            collective_id=0, has_side_effects=True, vmem_limit_bytes=40 * 1024 * 1024
        ),
        cost_estimate=pl.CostEstimate(flops=8 * 10**9, bytes_accessed=2**23, transcendentals=2**22),
    )(
        cand_feats.reshape(shards, cands // shards, width),
        cand_perm,
        w_in,
        w_out,
        cache_k,
        cache_v,
        hist_mask,
        hist_len,
        hist_home,
        hist_slot,
    )


def local(cand_feats, cand_perm, w_in, *rest):
    shards = lax.axis_size("req")
    shard_keys = MAXBLK // shards * BLK
    queries_fit = cand_perm.shape[1] <= shard_keys and shards == 8
    plan = move_queries if queries_fit and lax.axis_size("mp") == 4 else move_blocks
    return plan(cand_feats, cand_perm, w_in, *rest)


def solution(mesh):
    in_specs = (
        P("req", "mp"),
        P("req", None),
        P(None, None, "mp"),
        P("mp", None),
        P("req", None, "mp"),
        P("req", None, "mp"),
        P("req"),
        P(),
        P(),
        P("req", None, None),
    )
    out_specs = P("req", "mp")
    return jax.shard_map(local, mesh=mesh, in_specs=in_specs, out_specs=out_specs, check_vma=False)
```
